32 devices in a mesh: mom: 4 (over x, core), en: 8 (over z, y).
Axes of the slice: x: 2, y: 2, z: 4, core: 2. Of those that a mesh axis runs over, the one named last changes fastest.
Arguments:
- green_less: bfloat16 [8, 192, 8, 288], P('mom', 'en'), may hold values from -6 to 6
- green_greater: bfloat16 [8, 192, 8, 288], P('mom', 'en'), may hold values from -6 to 6
- derivative: float32 [2, 3, 144], replicated, may hold values from -1.75 to 1.75
- neighbours: int32 [2, 4], replicated, may hold values from 0 to 1
- phonon: bfloat16 [2, 8, 24, 3, 8], replicated, may hold values from 0.0099487305 to 0.099609375
Outputs:
- self_energy: bfloat16 [8, 192, 8, 288], P('mom', 'en')
- polarisation: float32 [8, 24, 3, 8], P('mom')
The draws below stay inside these ranges and needn't reach their ends.
All inputs are finite; a program needn't handle non-finite values.
Results may differ from the reference program's by a relative error of at most 0.0034.
Values may be sent and summed in bfloat16 or wider, within the bound.
No kernel may reach another device: no remote copies, remote signals or barrier semaphores. Data moves between devices by JAX's collectives and lax.ppermute only.
A program may use at most 64 MiB of HBM per device.

```python
import math
import jax
import jax.numpy as jnp
from jax import lax

NO = 12
NB = 4
A = 2
W = 24
ED = 24
K = 8
NE = 192
P_SIZE = 8


def draw_green_less(key, part):
    energy = jnp.arange(NE, dtype=jnp.float32) / NE
    shape = (K, NE, A * NB, 2 * NO * NO)
    scale = 0.5 + energy
    values = jax.random.normal(key, shape, jnp.float32) * scale[None, :, None, None]
    return jnp.clip(values, -6.0, 6.0).astype(jnp.bfloat16)


def touch_ends(drawn, stream_key, smallest, largest):
    extent = drawn.shape
    place = [jax.random.randint(jax.random.fold_in(stream_key, axis), (), 0, extent[axis]) for axis in range(len(extent))]
    drawn = drawn.at[tuple(place)].set(smallest)
    longest = extent.index(max(extent))
    place[longest] = (place[longest] + 1) % extent[longest]
    return drawn.at[tuple(place)].set(largest)


def levels(rng, shape, pieces, smallest, largest):
    loudness, own = 1.0, jax.random.fold_in(rng, 6)
    for axis_at, parts in pieces:
        draws = jnp.exp(jax.random.uniform(jax.random.fold_in(own, axis_at), (parts,), jnp.float32, smallest / len(pieces), largest / len(pieces)))
        loudness = loudness * jnp.repeat(draws, shape[axis_at] // parts).reshape([-1 if axis == axis_at else 1 for axis in range(len(shape))])
    return loudness


def bell_draw(rng, dims, spread, reach, cuts=(), kind=jnp.bfloat16):
    factor_of = levels(rng, dims, cuts, -0.22, 0.18) if cuts else 1.0
    values = jax.random.normal(rng, dims, jnp.float32) * spread * factor_of
    return jnp.minimum(jnp.maximum(values, -reach), reach).astype(kind)


def setup_inputs(seed: int = 0) -> dict:
    seeds = jax.random.split(jax.random.key(seed), 6)
    return {
        "green_less": draw_green_less(jax.random.fold_in(seeds[5], 71), 0),
        "green_greater": bell_draw(seeds[1], (K, NE, P_SIZE, 2 * NO * NO), 1.0, 6.0, ((0, 4), (1, 8))),
        "derivative": bell_draw(seeds[2], (A, 3, NO * NO), NO ** -0.5, 1.75, (), jnp.float32),
        "neighbours": touch_ends(jax.random.randint(seeds[3], (A, NB), 0, A), jax.random.fold_in(seeds[3], 1), 0, A - 1).astype(jnp.int32),
        "phonon": jnp.clip(jnp.exp(jax.random.uniform(seeds[4], (2, K, W, 3, P_SIZE), jnp.float32, math.log(0.0099487305), math.log(0.099609375))), 0.0099487305, 0.099609375).astype(jnp.bfloat16),
    }


HIGHEST = lax.Precision.HIGHEST

def band_table(length_out, length_in, depth_count):
    row_index = jnp.arange(length_out, dtype=jnp.int32)[:, None, None]
    col_index = jnp.arange(length_in, dtype=jnp.int32)[None, :, None]
    offsets = jnp.arange(depth_count, dtype=jnp.int32)[None, None, :]
    return (col_index - row_index == offsets).astype(jnp.float32)

def reference(green_less, green_greater, derivative, neighbours, phonon):
    pair_count = A * NB
    matrices = derivative.reshape(A, 3, NO, NO)
    left_blocks = jnp.repeat(matrices, NB, axis=0)
    right_blocks = matrices[neighbours.reshape(-1).astype(jnp.int32)]
    kernel = jnp.concatenate([jnp.flip(phonon[0], 1), jnp.zeros((K, 1, 3, pair_count), phonon.dtype), phonon[1]], axis=1).astype(jnp.float32)
    toeplitz = jnp.einsum('kimp,eji->kpmej', kernel, band_table(ED, ED + 2 * W, 2 * W + 1))
    selector = band_table(ED, ED + W - 1, W)
    padded = jnp.pad(green_less, ((0, 0), (W, W), (0, 0), (0, 0)))
    sign_pair = jnp.array([1.0, -1.0], jnp.float32)

    def one_block(block_index):
        first_row = (block_index * ED).astype(jnp.int32)
        window = lax.dynamic_slice_in_dim(padded, first_row, ED + 2 * W, 1).astype(jnp.float32)
        greater = lax.dynamic_slice_in_dim(green_greater, first_row, ED, 1).astype(jnp.float32)
        greater = greater.reshape(K, ED, pair_count, 2, NO, NO)
        half_product = jnp.einsum('kepcui,pmis->kepmcus', greater, left_blocks, precision=HIGHEST)
        weighted = jnp.einsum('kepmcus,pmut->kepmcst', half_product, right_blocks, precision=HIGHEST)
        weighted = weighted * sign_pair[:, None, None]
        weighted = lax.optimization_barrier(weighted.astype(jnp.bfloat16)).astype(jnp.float32)
        weighted = weighted.reshape(K, ED, pair_count, 3, 2 * NO * NO)
        upper_rows = window[:, W + 1:]
        window_sum = jnp.zeros((K, ED, pair_count, 3, 2 * NO * NO), jnp.float32)
        polar_rows = []
        for momentum in range(K):
            window_sum = window_sum + jnp.einsum('pmej,kjpx->kepmx', toeplitz[momentum], jnp.roll(window, momentum, axis=0))
            pair_sums = jnp.einsum('kjpx,kepmx->pmje', jnp.roll(upper_rows, -momentum, axis=0), weighted)
            polar_rows.append(jnp.einsum('pmje,ejw->wmp', pair_sums, selector, precision=HIGHEST))
        product_left = jnp.einsum('pmis,kepmcst->kepmcit', left_blocks, window_sum.reshape(K, ED, pair_count, 3, 2, NO, NO), precision=HIGHEST)
        energy = jnp.einsum('kepmcit,pmut->kepciu', product_left, right_blocks, precision=HIGHEST)
        energy = energy.reshape(K, ED, pair_count, 2 * NO * NO).astype(jnp.bfloat16)
        return (energy, jnp.stack(polar_rows))
    block_energy, block_polar = lax.map(one_block, jnp.arange(NE // ED, dtype=jnp.int32))
    self_energy = jnp.moveaxis(block_energy, 0, 1).reshape(K, NE, pair_count, 2 * NO * NO)
    polarisation = lax.optimization_barrier(jnp.sum(block_polar, axis=0)) / (NO * jnp.sqrt(jnp.float32(K * NE)))
    return (self_energy, polarisation)
```

```python
import functools

import jax
import jax.numpy as jnp
import numpy as np
from jax import lax
from jax.experimental import pallas as pl
from jax.experimental.pallas import tpu as pltpu
from jax.sharding import PartitionSpec as P

NO = 12
NB = 4
LANES = 128
BF = jnp.bfloat16
F32 = jnp.float32
HIGHEST = lax.Precision.HIGHEST
VMEM = pl.BlockSpec(memory_space=pltpu.VMEM)
SMEM = pl.BlockSpec(memory_space=pltpu.SMEM)
PARAMS = pltpu.CompilerParams(vmem_limit_bytes=48 * 1024 * 1024)


def dot(a, b):
    return jnp.dot(a, b, preferred_element_type=F32)


def dot_t(a, b):
    return lax.dot_general(a, b, (((1,), (1,)), ((), ())), preferred_element_type=F32)


def call(kernel, outs, ins, scratch=(), smem=1):
    return pl.pallas_call(
        kernel,
        out_shape=outs,
        in_specs=[SMEM] * smem + [VMEM] * (len(ins) - smem),
        out_specs=[VMEM] * len(outs),
        scratch_shapes=list(scratch),
        compiler_params=PARAMS,
    )(*ins)


def shape(dims, dtype):
    return jax.ShapeDtypeStruct(dims, dtype)


def pack_kernel(c_ref, g_ref, b_ref, perm_ref, g_own, b_own, g_far, b_far, halves):
    core = c_ref[0]
    rows = g_own.shape[0]
    pairs = g_ref.shape[2]
    entries = g_ref.shape[3]
    half = pairs // 2
    for src, own, far in ((g_ref, g_own, g_far), (b_ref, b_own, b_far)):
        sorted_rows = dot(perm_ref[...], src[...].reshape(rows * pairs, entries))
        for h in range(2):
            parts = [sorted_rows[(h * half + j) * rows : (h * half + j + 1) * rows] for j in range(half)]
            halves[h] = jnp.concatenate(parts, axis=1)
        own[...] = halves[core].astype(BF)
        far[...] = halves[1 - core].astype(BF)


def table_kernel(base_ref, left_ref, right_ref, rows_l_ref, rows_r_ref, hi_ref, lo_ref, t_ref, *, half, momenta, local_k, local_e):
    width = hi_ref.shape[2]
    for p in range(half):
        for m in range(3):
            u = left_ref[p * 3 + m]
            v = right_ref[p * 3 + m]
            for c in range(2):
                j = 2 * p + c
                if j:
                    uj = pltpu.roll(u, 16 * j, 1)
                    vj = pltpu.roll(v, 16 * j, 1)
                else:
                    uj, vj = u, v
                u_hi = uj.astype(BF)
                v_hi = vj.astype(BF)
                u_lo = (uj - u_hi.astype(F32)).astype(BF)
                v_lo = (vj - v_hi.astype(F32)).astype(BF)
                a = dot(rows_l_ref[...], jnp.concatenate([u_hi, u_lo], axis=0))
                b = dot(rows_r_ref[...], jnp.concatenate([v_hi, v_lo], axis=0))
                kron = a * b
                k_hi = kron.astype(BF)
                hi_ref[j * 3 + m] = k_hi
                lo_ref[j * 3 + m] = (kron - k_hi.astype(F32)).astype(BF)
    chip_k = 2 * local_k
    tiles = 3 * local_e // 8
    step = 8 * momenta
    first = momenta * (3 * local_e - 8)
    length = base_ref.shape[1]
    for p in range(half):
        for m in range(3):
            grid = {}
            for a in range(chip_k):
                index = (p * 3 + m) * chip_k + a
                row = base_ref[index : index + 1, :]
                block = pltpu.roll(jnp.broadcast_to(row, (8, length)), 0, 1, stride=momenta, stride_axis=0)
                moved = {0: block}
                for t in range(tiles):
                    offset = first - step * t
                    part = offset % LANES
                    if part not in moved:
                        moved[part] = pltpu.roll(block, length - part, 1)
                    start = offset - part
                    grid[(t, a)] = moved[part][:, start : start + 2 * LANES]
            order = []
            per = local_e // 8
            for blk in range(3):
                for a in range(chip_k):
                    order += [grid[(blk * per + i, a)] for i in range(per)]
            t_ref[p * 3 + m] = jnp.concatenate(order, axis=0).astype(BF)


def product_kernel(c_ref, *refs, half, entries, chips):
    core = c_ref[0]
    blocks = refs[: 2 * chips]
    perm_ref, hi_ref, lo_ref, t_ref = refs[2 * chips : 2 * chips + 4]
    g1_ref, own_ref, far_ref, lo_own, lo_far, up_own, up_far = refs[2 * chips + 4 : 2 * chips + 11]
    gathered, result = refs[2 * chips + 11 :]
    for s in range(chips):
        gathered[2 * s + core] = blocks[2 * s][...]
        gathered[2 * s + 1 - core] = blocks[2 * s + 1][...]
    count, rows, width = gathered.shape
    depth = count * rows
    tiles = width // LANES
    g = dot(perm_ref[...], gathered[...].reshape(depth, width)).astype(BF)
    block_rows = hi_ref.shape[1]
    sums = [[None] * tiles for _ in range(3)]
    for j in range(2 * half):
        start = (entries // 2) * j // LANES * LANES
        shift = (entries // 2) * j - start
        lhs = g[:, start : start + 2 * LANES]

        def padded(ref, index):
            parts = [ref[index]]
            if shift:
                parts = [jnp.zeros((shift, 2 * LANES), BF)] + parts
            rest = 2 * LANES - shift - block_rows
            if rest:
                parts = parts + [jnp.zeros((rest, 2 * LANES), BF)]
            return jnp.concatenate(parts, axis=0)

        for m in range(3):
            r = dot(lhs, padded(hi_ref, j * 3 + m)) + dot(lhs, padded(lo_ref, j * 3 + m))
            for i in range(2):
                tile = start // LANES + i
                piece = r[:, i * LANES : (i + 1) * LANES]
                sums[m][tile] = piece if sums[m][tile] is None else sums[m][tile] + piece
    high = [[None] * tiles for _ in range(3)]
    low = [[None] * tiles for _ in range(3)]
    for m in range(3):
        for i in range(tiles):
            high[m][i] = sums[m][i].astype(BF)
            low[m][i] = (sums[m][i] - high[m][i].astype(F32)).astype(BF)
            g1_ref[m, :, i * LANES : (i + 1) * LANES] = high[m][i]
    lane = lax.broadcasted_iota(jnp.int32, (1, LANES), 1)
    carried = None
    for p in range(half):
        begin = entries * p
        first = begin // LANES
        last = (begin + entries - 1) // LANES
        total = None
        for m in range(3):
            t = t_ref[p * 3 + m][:, :depth]
            for part in (high, low):
                term = dot(t, jnp.concatenate(part[m][first : last + 1], axis=1))
                total = term if total is None else total + term
        for i in range(first, last + 1):
            tile = total[:, (i - first) * LANES : (i - first + 1) * LANES]
            if i == first and begin % LANES:
                tile = jnp.where(lane < begin % LANES, carried, tile)
            if i == last and (begin + entries) % LANES:
                carried = tile
            else:
                for r in range(6):
                    result[r, :, i * LANES : (i + 1) * LANES] = tile[r * rows : (r + 1) * rows]
    lo_own[...] = result[core].astype(BF)
    lo_far[...] = result[1 - core].astype(BF)
    own_ref[...] = result[2 + core]
    far_ref[...] = result[3 - core].astype(BF)
    up_own[...] = result[4 + core].astype(BF)
    up_far[...] = result[5 - core].astype(BF)


def polar_kernel(c_ref, b_own, b_far, prev_own, prev_far, turn_ref, g1_ref, out_ref, gathered, *, half, entries, local_k, local_e, momenta, window, scale):
    core = c_ref[0]
    gathered[core] = prev_own[...]
    gathered[1 - core] = prev_far[...]
    gathered[2 + core] = b_own[...]
    gathered[3 - core] = b_far[...]
    count, rows, width = gathered.shape
    tiles = width // LANES
    b = gathered[...].reshape(count * rows, width)
    sums = [None] * tiles
    for j in range(2 * half):
        start = (entries // 2) * j // LANES * LANES
        r = dot(b[:, start : start + 2 * LANES], turn_ref[j])
        for i in range(2):
            tile = start // LANES + i
            piece = r[:, i * LANES : (i + 1) * LANES]
            sums[tile] = piece if sums[tile] is None else sums[tile] + piece
    chip_k = 2 * local_k
    group = 2 * local_e
    used = chip_k * group
    columns = -(-used // LANES) * LANES
    ordered = []
    for i in range(tiles):
        pieces = []
        for k in range(chip_k):
            for side in range(2):
                at = (side * chip_k + k) * local_e
                pieces.append(sums[i][at : at + local_e])
        if columns > used:
            pieces.append(jnp.zeros((columns - used, LANES), F32))
        ordered.append(jnp.concatenate(pieces, axis=0))
    lane = lax.broadcasted_iota(jnp.int32, (1, LANES), 1)
    per = LANES // window
    held = [jnp.zeros((momenta, LANES), F32) for _ in range(out_ref.shape[1] // LANES)]
    for p in range(half):
        begin = entries * p
        first = begin // LANES
        last = (begin + entries - 1) // LANES
        parts = []
        for i in range(first, last + 1):
            tile = ordered[i]
            if i == first and begin % LANES:
                tile = jnp.where(lane < begin % LANES, 0.0, tile)
            if i == last and (begin + entries) % LANES:
                tile = jnp.where(lane < (begin + entries) % LANES, tile, 0.0)
            parts.append(tile.astype(BF))
        rhs = jnp.concatenate(parts, axis=1)
        for m in range(3):
            s = dot_t(g1_ref[m][:, first * LANES : (last + 1) * LANES], rhs)
            acc = None
            for e in range(local_e):
                row = s[e * momenta : (e + 1) * momenta]
                if e:
                    row = pltpu.roll(row, columns - e, 1)
                acc = row if acc is None else acc + row
            total = None
            for a in range(chip_k):
                piece = acc if a == 0 else pltpu.roll(acc, columns - group * a, 1)
                piece = piece[:, :LANES]
                if a:
                    piece = pltpu.roll(piece, momenta - a, 0)
                total = piece if total is None else total + piece
            slot = p * 3 + m
            at = slot % per * window
            total = jnp.where(lane < window, total * scale, 0.0)
            if at:
                total = pltpu.roll(total, at, 1)
            held[slot // per] = held[slot // per] + total
    for i, tile in enumerate(held):
        out_ref[:, i * LANES : (i + 1) * LANES] = tile


def join_kernel(c_ref, own, own_far, low_own, low_far, up_own, up_far, perm_ref, out_ref, halves):
    core = c_ref[0]
    pairs = out_ref.shape[2]
    entries = out_ref.shape[3]
    half = pairs // 2
    halves[core] = own[...] + low_own[...].astype(F32) + up_own[...].astype(F32)
    halves[1 - core] = own_far[...].astype(F32) + low_far[...].astype(F32) + up_far[...].astype(F32)
    parts = []
    for p in range(pairs):
        begin = entries * (p % half)
        parts.append(halves[p // half][:, begin : begin + entries])
    stacked = jnp.concatenate(parts, axis=0).astype(BF)
    out_ref[...] = dot(perm_ref[...], stacked).astype(BF).reshape(out_ref.shape)


def row_perm(outer, inner):
    rows = outer * inner
    matrix = np.zeros((rows, rows), np.float32)
    for j in range(inner):
        for i in range(outer):
            matrix[j * outer + i, i * inner + j] = 1
    return matrix


def body(green_less, green_greater, derivative, neighbours, phonon, *, mom, en):
    local_k, local_e, pairs, entries = green_less.shape
    momenta, window = phonon.shape[1], phonon.shape[2]
    atoms = derivative.shape[0]
    half = pairs // 2
    rows = local_k * local_e
    width = half * entries
    chips = mom // 2
    chip_k = 2 * local_k
    total_e = local_e * en
    size = NO * NO
    me = lax.axis_index("mom")
    core = jnp.mod(me, 2).astype(jnp.int32)
    cores = core[None]

    sort_pairs = row_perm(rows, pairs)
    g_own, b_own, g_far, b_far = call(
        pack_kernel,
        [shape((rows, width), BF)] * 4,
        [cores, green_less, green_greater, jnp.asarray(sort_pairs, BF)],
        [pltpu.VMEM((2, rows, width), F32)],
    )

    def move(value, dchip, dcore, de):
        links = []
        for m in range(mom):
            target = ((m // 2 + dchip) % chips) * 2 + (m % 2 if dcore == 0 else 1 - m % 2)
            for e in range(en):
                if 0 <= e + de < en:
                    links.append((m * en + e, target * en + e + de))
        return lax.ppermute(value, ("mom", "en"), links)

    blocks = [g_own, move(g_far, 0, 1, 0)]
    for s in range(1, chips):
        blocks += [move(g_own, -s, 0, 0), move(g_far, -s, 1, 0)]
    b_core = move(b_far, 0, 1, 0)
    prev_own = move(b_own, 0, 0, 1)
    prev_far = move(b_far, 0, 1, 1)

    matrices = derivative.reshape(atoms, 3, NO, NO)
    lookup = (
        neighbours.reshape(-1)[:, None] == jnp.arange(atoms, dtype=jnp.int32)[None, :]
    ).astype(F32)
    left = jnp.repeat(matrices, NB, axis=0)
    right = jnp.dot(lookup, derivative.reshape(atoms, 3 * size), precision=HIGHEST)
    right = right.reshape(pairs, 3, NO, NO)
    left = lax.dynamic_slice_in_dim(left, core * half, half, 0).reshape(3 * half, NO, NO)
    right = lax.dynamic_slice_in_dim(right, core * half, half, 0).reshape(3 * half, NO, NO)
    left_t = jnp.repeat(jnp.swapaxes(left, 1, 2), NO, axis=2)
    right_t = jnp.tile(jnp.swapaxes(right, 1, 2), (1, 1, NO))
    spare = ((0, 0), (0, 16 - NO), (0, 2 * LANES - size))
    left_t = jnp.pad(left_t, spare)
    right_t = jnp.pad(right_t, spare)
    rows_l = np.zeros((size, 32), np.float32)
    rows_r = np.zeros((size, 32), np.float32)
    for s in range(NO):
        for t in range(NO):
            rows_l[s * NO + t, [s, 16 + s]] = 1
            rows_r[s * NO + t, [t, 16 + t]] = 1
    weights = lax.dynamic_slice_in_dim(phonon, core * half, half, 4)
    lead = 2 * local_e - 8 - window
    blank = jnp.zeros((momenta, 1, 3, half), BF)
    line = jnp.concatenate([jnp.flip(weights[0], 1), blank, weights[1]], axis=1)
    line = jnp.pad(line, ((0, 0), (lead, 4 * local_e - lead - line.shape[1]), (0, 0), (0, 0)))
    pick = np.zeros((chip_k, momenta, momenta), np.float32)
    for a in range(chip_k):
        for k in range(momenta):
            pick[a, k, (a - k) % momenta] = 1
    base = jnp.einsum("akq,qymp->pmayk", jnp.asarray(pick, BF), line, preferred_element_type=F32)
    base = base.reshape(half * 3 * chip_k, 4 * local_e * momenta)
    k_hi, k_lo, toeplitz = call(
        functools.partial(table_kernel, half=half, momenta=momenta, local_k=local_k, local_e=local_e),
        [
            shape((6 * half, size, 2 * LANES), BF),
            shape((6 * half, size, 2 * LANES), BF),
            shape((3 * half, 3 * chip_k * local_e, 2 * LANES), BF),
        ],
        [base, left_t, right_t, jnp.asarray(rows_l, BF), jnp.asarray(rows_r, BF)],
        smem=0,
    )

    to_energy = np.zeros((momenta * local_e,) * 2, np.float32)
    for k in range(momenta):
        for e in range(local_e):
            to_energy[e * momenta + k, k * local_e + e] = 1
    g1, own, far, lo_own, lo_far, up_own, up_far = call(
        functools.partial(product_kernel, half=half, entries=entries, chips=chips),
        [shape((3, momenta * local_e, width), BF), shape((rows, width), F32)]
        + [shape((rows, width), BF)] * 5,
        [cores] + blocks + [jnp.asarray(to_energy, BF), k_hi, k_lo, toeplitz],
        [pltpu.VMEM((2 * chips, rows, width), BF), pltpu.VMEM((6, rows, width), F32)],
    )
    from_above = move(lo_own, 0, 0, -1)
    from_above_far = move(lo_far, 0, 1, -1)
    from_below = move(up_own, 0, 0, 1)
    from_below_far = move(up_far, 0, 1, 1)
    own_other = move(far, 0, 1, 0)

    turn = np.zeros((2 * half, 2 * LANES, 2 * LANES), np.float32)
    for j in range(2 * half):
        shift = size * j % LANES
        for u in range(NO):
            for i in range(NO):
                turn[j, shift + u * NO + i, shift + i * NO + u] = 1 - 2 * (j % 2)
    slots = half * 3
    per = LANES // window
    (partial,) = call(
        functools.partial(
            polar_kernel, half=half, entries=entries, local_k=local_k, local_e=local_e,
            momenta=momenta, window=window, scale=1.0 / (NO * float(np.sqrt(momenta * total_e))),
        ),
        [shape((momenta, -(-slots // per) * LANES), F32)],
        [cores, b_own, b_core, prev_own, prev_far, jnp.asarray(turn, BF), g1],
        [pltpu.VMEM((4, rows, width), BF)],
    )
    terms = lax.all_gather(partial, ("mom", "en"), axis=0, tiled=False)
    terms = lax.dynamic_slice_in_dim(terms, me * local_k, local_k, 1)
    summed = jnp.sum(terms.reshape(chips, 2, en, local_k, -1), axis=(0, 2))
    summed = summed.reshape(2, local_k, -1, LANES)[..., : per * window]
    summed = summed.reshape(2, local_k, -1, window)[:, :, :slots]
    summed = summed.reshape(2, local_k, half, 3, window)
    polar = jnp.flip(summed.transpose(1, 4, 3, 0, 2), 1).reshape(local_k, window, 3, pairs)

    (self_energy,) = call(
        join_kernel,
        [shape(green_less.shape, BF)],
        [cores, own, own_other, from_below, from_below_far, from_above, from_above_far, jnp.asarray(sort_pairs.T, BF)],
        [pltpu.VMEM((2, rows, width), F32)],
    )
    return (self_energy, polar)


def solution(mesh):
    return jax.shard_map(
        functools.partial(body, mom=mesh.shape["mom"], en=mesh.shape["en"]),
        mesh=mesh,
        in_specs=(P("mom", "en", None, None), P("mom", "en", None, None), P(), P(), P()),
        out_specs=(P("mom", "en", None, None), P("mom", None, None, None)),
        check_vma=False,
    )
```

```python
import functools

import jax
import jax.numpy as jnp
import numpy as np
from jax import lax
from jax.experimental import pallas as pl
from jax.experimental.pallas import tpu as pltpu
from jax.sharding import PartitionSpec as P

NO = 12
NB = 4
LANES = 128
BF = jnp.bfloat16
F32 = jnp.float32
HIGHEST = lax.Precision.HIGHEST
VMEM = pl.BlockSpec(memory_space=pltpu.VMEM)
SMEM = pl.BlockSpec(memory_space=pltpu.SMEM)
PARAMS = pltpu.CompilerParams(vmem_limit_bytes=24 * 1024 * 1024)


def dot(a, b):
    return jnp.dot(a, b, preferred_element_type=F32)


def dot_t(a, b):
    return lax.dot_general(a, b, (((1,), (1,)), ((), ())), preferred_element_type=F32)


def call(kernel, outs, ins, scratch=(), smem=1):
    return pl.pallas_call(
        kernel,
        out_shape=outs,
        in_specs=[SMEM] * smem + [VMEM] * (len(ins) - smem),
        out_specs=[VMEM] * len(outs),
        scratch_shapes=list(scratch),
        compiler_params=PARAMS,
    )(*ins)


def shape(dims, dtype):
    return jax.ShapeDtypeStruct(dims, dtype)


def pack_kernel(s_ref, g_hbm, b_hbm, g_own, b_own, g_far, b_far, g_ref, b_ref, halves, sems):
    core = s_ref[0]
    copies = []
    for i, (src, dst) in enumerate(((g_hbm, g_ref), (b_hbm, b_ref))):
        copies.append(pltpu.make_async_copy(src, dst, sems.at[i]))
        copies[-1].start()
    rows = g_own.shape[0]
    pairs = g_ref.shape[2]
    entries = g_ref.shape[3]
    half = pairs // 2
    dims = (rows, rows * pairs)
    gap = lax.broadcasted_iota(jnp.int32, dims, 1) - pairs * lax.broadcasted_iota(jnp.int32, dims, 0)
    perm = jnp.concatenate([(gap == p).astype(F32).astype(BF) for p in range(pairs)], axis=0)
    for copy, src, own, far in ((copies[0], g_ref, g_own, g_far), (copies[1], b_ref, b_own, b_far)):
        copy.wait()
        sorted_rows = dot(perm, src[...].reshape(rows * pairs, entries))
        for h in range(2):
            parts = [sorted_rows[(h * half + j) * rows : (h * half + j + 1) * rows] for j in range(half)]
            halves[h] = jnp.concatenate(parts, axis=1)
        own[...] = halves[core].astype(BF)
        far[...] = halves[1 - core].astype(BF)


def table_kernel(s_ref, near_ref, deriv_ref, phonon_ref, const_ref, mask_ref, hi_ref, lo_ref, t_ref, factors, bases, *, half, local_k, local_e):
    core = s_ref[0]
    _, momenta, _, pairs, window = phonon_ref.shape
    size = NO * NO
    atoms = deriv_ref.shape[1]
    spread = []
    for m in range(3):
        for atom in range(atoms):
            spread.append(deriv_ref[m, atom : atom + 1, :] * mask_ref[...])
    spread = jnp.concatenate(spread, axis=0)
    spread_hi = spread.astype(BF)
    spread_lo = (spread - spread_hi.astype(F32)).astype(BF)
    for i, part in enumerate((spread_hi, spread_lo)):
        rows = dot(part, const_ref[:, : 4 * LANES])
        for n in range(3 * atoms):
            factors[n, 16 * i : 16 * i + 16] = rows[16 * n : 16 * n + 16]
    rows_l = const_ref[:, 4 * LANES : 4 * LANES + 32]
    rows_r = const_ref[:, 5 * LANES : 5 * LANES + 32]
    for p in range(half):
        pair = core * half + p
        atom = pair // NB
        other = near_ref[atom, pair % NB]
        for m in range(3):
            u = factors[m * atoms + atom][:, : 2 * LANES]
            v = factors[m * atoms + other][:, 2 * LANES :]
            for c in range(2):
                j = 2 * p + c
                shift = size * j % LANES
                uj = pltpu.roll(u, shift, 1) if shift else u
                vj = pltpu.roll(v, shift, 1) if shift else v
                kron = dot(rows_l, uj.astype(BF)) * dot(rows_r, vj.astype(BF))
                k_hi = kron.astype(BF)
                hi_ref[j * 3 + m] = k_hi
                lo_ref[j * 3 + m] = (kron - k_hi.astype(F32)).astype(BF)
    chip_k = 2 * local_k
    tiles = 3 * local_e // 8
    step = 8 * momenta
    first = momenta * (3 * local_e - 8)
    length = bases.shape[3]
    middle = 2 * local_e - 8
    dims = (window, length)
    lane = lax.broadcasted_iota(jnp.int32, dims, 1)
    depth = lax.broadcasted_iota(jnp.int32, dims, 0) + 1
    line = None
    for side in range(2):
        gap = lane - momenta * (middle + depth if side else middle - depth)
        for q in range(momenta):
            place = (gap == (-q) % momenta).astype(F32).astype(BF)
            weights = phonon_ref[side, q].astype(F32).reshape(3 * pairs, window).astype(BF)
            term = dot(weights, place)
            line = term if line is None else line + term
    lane = lax.broadcasted_iota(jnp.int32, (1, length), 1)
    k = lane - momenta * jnp.floor((lane.astype(F32) + 0.5) / momenta).astype(jnp.int32)
    for a in range(chip_k):
        moved = line
        if a:
            moved = jnp.where(k >= a, pltpu.roll(line, a, 1), pltpu.roll(line, length - momenta + a, 1))
        bases[a] = moved.reshape(3, pairs, length)
    for p in range(half):
        for m in range(3):
            grid = {}
            for a in range(chip_k):
                row = bases[a, m, pl.ds(core * half + p, 1), :]
                block = pltpu.roll(jnp.broadcast_to(row, (8, length)), 0, 1, stride=momenta, stride_axis=0)
                moved = {0: block}
                for t in range(tiles):
                    offset = first - step * t
                    part = offset % LANES
                    if part not in moved:
                        moved[part] = pltpu.roll(block, length - part, 1)
                    start = offset - part
                    grid[(t, a)] = moved[part][:, start : start + 2 * LANES]
            order = []
            per = local_e // 8
            for blk in range(3):
                for a in range(chip_k):
                    order += [grid[(blk * per + i, a)] for i in range(per)]
            t_ref[p * 3 + m] = jnp.concatenate(order, axis=0).astype(BF)


def product_kernel(c_ref, *refs, half, entries, chips):
    core = c_ref[0]
    blocks = refs[: 2 * chips]
    perm_ref, hi_ref, lo_ref, t_ref = refs[2 * chips : 2 * chips + 4]
    g1_ref, own_ref, far_ref, lo_own, lo_far, up_own, up_far = refs[2 * chips + 4 : 2 * chips + 11]
    gathered, result = refs[2 * chips + 11 :]
    for s in range(chips):
        gathered[2 * s + core] = blocks[2 * s][...]
        gathered[2 * s + 1 - core] = blocks[2 * s + 1][...]
    count, rows, width = gathered.shape
    depth = count * rows
    tiles = width // LANES
    g = dot(perm_ref[...], gathered[...].reshape(depth, width)).astype(BF)
    block_rows = hi_ref.shape[1]
    sums = [[None] * tiles for _ in range(3)]
    for j in range(2 * half):
        start = (entries // 2) * j // LANES * LANES
        shift = (entries // 2) * j - start
        lhs = g[:, start : start + 2 * LANES]

        def padded(ref, index):
            parts = [ref[index]]
            if shift:
                parts = [jnp.zeros((shift, 2 * LANES), BF)] + parts
            rest = 2 * LANES - shift - block_rows
            if rest:
                parts = parts + [jnp.zeros((rest, 2 * LANES), BF)]
            return jnp.concatenate(parts, axis=0)

        for m in range(3):
            r = dot(lhs, padded(hi_ref, j * 3 + m)) + dot(lhs, padded(lo_ref, j * 3 + m))
            for i in range(2):
                tile = start // LANES + i
                piece = r[:, i * LANES : (i + 1) * LANES]
                sums[m][tile] = piece if sums[m][tile] is None else sums[m][tile] + piece
    high = [[None] * tiles for _ in range(3)]
    low = [[None] * tiles for _ in range(3)]
    for m in range(3):
        for i in range(tiles):
            high[m][i] = sums[m][i].astype(BF)
            low[m][i] = (sums[m][i] - high[m][i].astype(F32)).astype(BF)
            g1_ref[m, :, i * LANES : (i + 1) * LANES] = high[m][i]
    lane = lax.broadcasted_iota(jnp.int32, (1, LANES), 1)
    carried = None
    for p in range(half):
        begin = entries * p
        first = begin // LANES
        last = (begin + entries - 1) // LANES
        total = None
        for m in range(3):
            t = t_ref[p * 3 + m][:, :depth]
            for part in (high, low):
                term = dot(t, jnp.concatenate(part[m][first : last + 1], axis=1))
                total = term if total is None else total + term
        for i in range(first, last + 1):
            tile = total[:, (i - first) * LANES : (i - first + 1) * LANES]
            if i == first and begin % LANES:
                tile = jnp.where(lane < begin % LANES, carried, tile)
            if i == last and (begin + entries) % LANES:
                carried = tile
            else:
                for r in range(6):
                    result[r, :, i * LANES : (i + 1) * LANES] = tile[r * rows : (r + 1) * rows]
    below = 1.0 - c_ref[1].astype(F32)
    above = 1.0 - c_ref[2].astype(F32)
    lo_own[...] = (result[core] * below).astype(BF)
    lo_far[...] = (result[1 - core] * below).astype(BF)
    own_ref[...] = result[2 + core]
    far_ref[...] = result[3 - core].astype(BF)
    up_own[...] = (result[4 + core] * above).astype(BF)
    up_far[...] = (result[5 - core] * above).astype(BF)


def polar_kernel(c_ref, b_own, b_far, prev_own, prev_far, turn_ref, sort_ref, g1_ref, out_ref, gathered, *, half, entries, local_k, local_e, scale):
    core = c_ref[0]
    present = 1.0 - c_ref[1].astype(F32)
    gathered[core] = (prev_own[...].astype(F32) * present).astype(BF)
    gathered[1 - core] = (prev_far[...].astype(F32) * present).astype(BF)
    gathered[2 + core] = b_own[...]
    gathered[3 - core] = b_far[...]
    count, rows, width = gathered.shape
    tiles = width // LANES
    b = dot(sort_ref[...], gathered[...].reshape(count * rows, width)).astype(BF)
    sums = [None] * tiles
    for j in range(2 * half):
        start = (entries // 2) * j // LANES * LANES
        r = dot(b[:, start : start + 2 * LANES], turn_ref[j])
        for i in range(2):
            tile = start // LANES + i
            piece = r[:, i * LANES : (i + 1) * LANES]
            sums[tile] = piece if sums[tile] is None else sums[tile] + piece
    chip_k = 2 * local_k
    group = 2 * local_e
    columns = sort_ref.shape[0]
    window = local_e
    momenta = g1_ref.shape[1] // local_e
    lane = lax.broadcasted_iota(jnp.int32, (1, LANES), 1)
    pieces = []
    for p in range(half):
        begin = entries * p
        first = begin // LANES
        last = (begin + entries - 1) // LANES
        parts = []
        for i in range(first, last + 1):
            tile = sums[i]
            if i == first and begin % LANES:
                tile = jnp.where(lane < begin % LANES, 0.0, tile)
            if i == last and (begin + entries) % LANES:
                tile = jnp.where(lane < (begin + entries) % LANES, tile, 0.0)
            parts.append(tile.astype(BF))
        rhs = jnp.concatenate(parts, axis=1)
        held = None
        for m in range(3):
            s = dot_t(g1_ref[m][:, first * LANES : (last + 1) * LANES], rhs)
            acc = None
            for e in range(local_e):
                row = pltpu.roll(s[e * momenta : (e + 1) * momenta], columns - (local_e - e), 1)
                acc = row if acc is None else acc + row
            total = None
            for a in range(chip_k):
                piece = acc if a == 0 else pltpu.roll(acc, columns - group * a, 1)
                piece = piece[:, :LANES]
                if a:
                    piece = pltpu.roll(piece, momenta - a, 0)
                total = piece if total is None else total + piece
            total = jnp.where(lane < window, total * scale, 0.0)
            if m:
                total = pltpu.roll(total, m * (LANES // 4), 1)
            held = total if held is None else held + total
        pieces.append(held)
    targets, en = out_ref.shape[:2]
    for t in range(targets):
        tile = jnp.concatenate(
            [pieces[p][t * local_k + i : t * local_k + i + 1] for i in range(local_k) for p in range(half)], axis=0
        )
        for e in range(en):
            out_ref[t, e] = tile


def total_kernel(in_ref, out_ref, *, half):
    targets, en = in_ref.shape[:2]
    local_k, _, _, window = out_ref.shape
    sums = []
    for c in range(2):
        total = None
        for t in range(c, targets, 2):
            for e in range(en):
                total = in_ref[t, e] if total is None else total + in_ref[t, e]
        sums.append(total)
    for i in range(local_k):
        tile = jnp.concatenate([sums[c][i * half : (i + 1) * half] for c in range(2)], axis=0)
        for m in range(3):
            moved = pltpu.roll(tile, LANES - m * (LANES // 4), 1) if m else tile
            out_ref[i, m] = moved[:, :window]


def join_kernel(c_ref, own, own_far, low_own, low_far, up_own, up_far, perm_ref, out_ref, halves):
    core = c_ref[0]
    pairs = out_ref.shape[2]
    entries = out_ref.shape[3]
    half = pairs // 2
    halves[core] = own[...] + low_own[...].astype(F32) + up_own[...].astype(F32)
    halves[1 - core] = own_far[...].astype(F32) + low_far[...].astype(F32) + up_far[...].astype(F32)
    parts = []
    for p in range(pairs):
        begin = entries * (p % half)
        parts.append(halves[p // half][:, begin : begin + entries])
    stacked = jnp.concatenate(parts, axis=0).astype(BF)
    out_ref[...] = dot(perm_ref[...], stacked).astype(BF).reshape(out_ref.shape)


def row_perm(outer, inner):
    rows = outer * inner
    matrix = np.zeros((rows, rows), np.float32)
    for j in range(inner):
        for i in range(outer):
            matrix[j * outer + i, i * inner + j] = 1
    return matrix


def body(green_less, green_greater, derivative, neighbours, phonon, *, mom, en):
    local_k, local_e, pairs, entries = green_less.shape
    momenta, window = phonon.shape[1], phonon.shape[2]
    atoms = derivative.shape[0]
    half = pairs // 2
    rows = local_k * local_e
    width = half * entries
    chips = mom // 2
    chip_k = 2 * local_k
    total_e = local_e * en
    size = NO * NO
    core = jnp.mod(lax.axis_index("mom"), 2).astype(jnp.int32)
    place = lax.axis_index("en").astype(jnp.int32)
    scalars = jnp.stack([core, (place == 0).astype(jnp.int32), (place == en - 1).astype(jnp.int32)])

    sort_pairs = row_perm(rows, pairs)
    anywhere = pl.BlockSpec(memory_space=pl.ANY)
    g_own, b_own, g_far, b_far = pl.pallas_call(
        pack_kernel,
        out_shape=[shape((rows, width), BF)] * 4,
        in_specs=[SMEM, anywhere, anywhere],
        out_specs=[VMEM] * 4,
        scratch_shapes=[
            pltpu.VMEM(green_less.shape, BF),
            pltpu.VMEM(green_less.shape, BF),
            pltpu.VMEM((2, rows, width), F32),
            pltpu.SemaphoreType.DMA((2,)),
        ],
        compiler_params=PARAMS,
    )(scalars, green_less, green_greater)

    def move(value, dchip, dcore, de):
        links = []
        for m in range(mom):
            target = ((m // 2 + dchip) % chips) * 2 + (m % 2 if dcore == 0 else 1 - m % 2)
            for e in range(en):
                links.append((m * en + e, target * en + (e + de) % en))
        return lax.ppermute(value, ("mom", "en"), links)

    blocks = [g_own, move(g_far, 0, 1, 0)]
    for s in range(1, chips):
        blocks += [move(g_own, -s, 0, 0), move(g_far, -s, 1, 0)]
    b_core = move(b_far, 0, 1, 0)
    prev_own = move(b_own, 0, 0, 1)
    prev_far = move(b_far, 0, 1, 1)

    const = np.zeros((size, 6 * LANES), np.float32)
    mask = np.zeros((16, size), np.float32)
    for s in range(NO):
        for t in range(NO):
            const[s * NO : (s + 1) * NO, s * NO + t] = 1
            const[t * NO : (t + 1) * NO, 2 * LANES + s * NO + t] = 1
            const[s * NO + t, [4 * LANES + s, 4 * LANES + 16 + s]] = 1
            const[s * NO + t, [5 * LANES + t, 5 * LANES + 16 + t]] = 1
            mask[t, s * NO + t] = 1
    k_hi, k_lo, toeplitz = pl.pallas_call(
        functools.partial(table_kernel, half=half, local_k=local_k, local_e=local_e),
        out_shape=[
            shape((6 * half, size, 2 * LANES), BF),
            shape((6 * half, size, 2 * LANES), BF),
            shape((3 * half, 3 * chip_k * local_e, 2 * LANES), BF),
        ],
        in_specs=[SMEM, SMEM, VMEM, VMEM, VMEM, VMEM],
        out_specs=[VMEM] * 3,
        scratch_shapes=[
            pltpu.VMEM((3 * atoms, 32, 4 * LANES), F32),
            pltpu.VMEM((chip_k, 3, pairs, 4 * local_e * momenta), F32),
        ],
        compiler_params=PARAMS,
    )(
        scalars, neighbours, derivative.transpose(1, 0, 2), phonon.transpose(0, 1, 3, 4, 2),
        jnp.asarray(const, BF), jnp.asarray(mask),
    )

    to_energy = np.zeros((momenta * local_e,) * 2, np.float32)
    for k in range(momenta):
        for e in range(local_e):
            to_energy[e * momenta + k, k * local_e + e] = 1
    g1, own, far, lo_own, lo_far, up_own, up_far = call(
        functools.partial(product_kernel, half=half, entries=entries, chips=chips),
        [shape((3, momenta * local_e, width), BF), shape((rows, width), F32)]
        + [shape((rows, width), BF)] * 5,
        [scalars] + blocks + [jnp.asarray(to_energy, BF), k_hi, k_lo, toeplitz],
        [pltpu.VMEM((2 * chips, rows, width), BF), pltpu.VMEM((6, rows, width), F32)],
    )
    from_above = move(lo_own, 0, 0, -1)
    from_above_far = move(lo_far, 0, 1, -1)
    from_below = move(up_own, 0, 0, 1)
    from_below_far = move(up_far, 0, 1, 1)
    own_other = move(far, 0, 1, 0)

    turn = np.zeros((2 * half, 2 * LANES, 2 * LANES), np.float32)
    for j in range(2 * half):
        shift = size * j % LANES
        for u in range(NO):
            for i in range(NO):
                turn[j, shift + u * NO + i, shift + i * NO + u] = 1 - 2 * (j % 2)
    sort_e = np.zeros((-(-chip_k * 2 * local_e // LANES) * LANES, 2 * chip_k * local_e), np.float32)
    for k in range(chip_k):
        for i in range(local_e):
            at = k * 2 * local_e + i
            sort_e[at, (chip_k + k) * local_e + local_e - 1 - i] = 1
            sort_e[at + local_e, k * local_e + local_e - 1 - i] = 1
    (partial,) = call(
        functools.partial(
            polar_kernel, half=half, entries=entries, local_k=local_k, local_e=local_e,
            scale=1.0 / (NO * float(np.sqrt(momenta * total_e))),
        ),
        [shape((mom, en, local_k * half, LANES), F32)],
        [scalars, b_own, b_core, prev_own, prev_far, jnp.asarray(turn, BF), jnp.asarray(sort_e, BF), g1],
        [pltpu.VMEM((4, rows, width), BF)],
    )
    terms = lax.all_to_all(
        partial.reshape(mom * en, local_k * half, LANES), ("mom", "en"), split_axis=0, concat_axis=0, tiled=True
    )
    (polar,) = call(
        functools.partial(total_kernel, half=half),
        [shape((local_k, 3, pairs, window), F32)],
        [terms.reshape(mom, en, local_k * half, LANES)],
        smem=0,
    )
    polar = polar.transpose(0, 3, 1, 2)

    (self_energy,) = call(
        join_kernel,
        [shape(green_less.shape, BF)],
        [scalars, own, own_other, from_below, from_below_far, from_above, from_above_far, jnp.asarray(sort_pairs.T, BF)],
        [pltpu.VMEM((2, rows, width), F32)],
    )
    return (self_energy, polar)


def solution(mesh):
    return jax.shard_map(
        functools.partial(body, mom=mesh.shape["mom"], en=mesh.shape["en"]),
        mesh=mesh,
        in_specs=(P("mom", "en", None, None), P("mom", "en", None, None), P(), P(), P()),
        out_specs=(P("mom", "en", None, None), P("mom", None, None, None)),
        check_vma=False,
    )
```

```python
import functools

import jax
import jax.numpy as jnp
import numpy as np
from jax import lax
from jax.experimental import pallas as pl
from jax.experimental.pallas import tpu as pltpu
from jax.sharding import PartitionSpec as P

NO = 12
NB = 4
LANES = 128
BF = jnp.bfloat16
F32 = jnp.float32
HIGHEST = lax.Precision.HIGHEST
VMEM = pl.BlockSpec(memory_space=pltpu.VMEM)
HBM = pl.BlockSpec(memory_space=pltpu.HBM)
PARAMS = pltpu.CompilerParams(vmem_limit_bytes=24 * 1024 * 1024)


def dot(a, b):
    return jnp.dot(a, b, preferred_element_type=F32)


def dot_t(a, b):
    return lax.dot_general(a, b, (((1,), (1,)), ((), ())), preferred_element_type=F32)


def call(kernel, outs, ins, scratch=(), specs=None):
    return pl.pallas_call(
        kernel,
        out_shape=outs,
        in_specs=specs or [VMEM] * len(ins),
        out_specs=[VMEM] * len(outs),
        scratch_shapes=list(scratch),
        compiler_params=PARAMS,
    )(*ins)


def my_core():
    return lax.rem(lax.axis_index("mom"), 2).astype(jnp.int32)


def index(dims, axis):
    return lax.broadcasted_iota(jnp.int32, dims, axis)


def split(value, count):
    whole = jnp.floor((value.astype(F32) + 0.5) * (1.0 / count)).astype(jnp.int32)
    return whole, value - count * whole


def ones_at(condition):
    return condition.astype(F32).astype(BF)


def shape(dims, dtype):
    return jax.ShapeDtypeStruct(dims, dtype)


def pack_kernel(g_hbm, b_hbm, g_own, b_own, g_far, b_far, g_ref, b_ref, halves, sems):
    core = my_core()
    copies = []
    for i, (src, dst) in enumerate(((g_hbm, g_ref), (b_hbm, b_ref))):
        copies.append(pltpu.make_async_copy(src, dst, sems.at[i]))
        copies[-1].start()
    rows = g_own.shape[0]
    pairs = g_ref.shape[2]
    entries = g_ref.shape[3]
    half = pairs // 2
    dims = (rows, rows * pairs)
    gap = index(dims, 1) - pairs * index(dims, 0)
    perm = jnp.concatenate([ones_at(gap == p) for p in range(pairs)], axis=0)
    for copy, src, own, far in ((copies[0], g_ref, g_own, g_far), (copies[1], b_ref, b_own, b_far)):
        copy.wait()
        sorted_rows = dot(perm, src[...].reshape(rows * pairs, entries))
        for h in range(2):
            parts = [sorted_rows[(h * half + j) * rows : (h * half + j + 1) * rows] for j in range(half)]
            halves[h] = jnp.concatenate(parts, axis=1)
        own[...] = halves[core].astype(BF)
        far[...] = halves[1 - core].astype(BF)


def table_kernel(
    near_hbm, deriv_hbm, phonon_hbm, hi_ref, lo_ref, t_ref, perm_ref, join_ref, turn_ref, sort_ref,
    near_ref, deriv_ref, phonon_ref, factors, bases, sems, *, half, local_k, local_e,
):
    copies = []
    for i, (src, dst) in enumerate(((near_hbm, near_ref), (deriv_hbm, deriv_ref), (phonon_hbm, phonon_ref))):
        copies.append(pltpu.make_async_copy(src, dst, sems.at[i]))
        copies[-1].start()
    core = my_core()
    _, momenta, _, pairs, window = phonon_ref.shape
    size = NO * NO
    chip_k = 2 * local_k
    dims = perm_ref.shape
    e, k = split(index(dims, 0), momenta)
    perm_ref[...] = ones_at(index(dims, 1) == k * local_e + e)
    dims = join_ref.shape
    row, p = split(index(dims, 0), pairs)
    join_ref[...] = ones_at(index(dims, 1) == p * (local_k * local_e) + row)
    dims = sort_ref.shape
    k, i = split(index(dims, 0), 2 * local_e)
    at = jnp.where(i < local_e, (chip_k + k) * local_e + local_e - 1 - i, k * local_e + 2 * local_e - 1 - i)
    sort_ref[...] = ones_at((index(dims, 1) == at) & (k < chip_k))
    dims = turn_ref.shape[1:]
    u, i = split(index(dims, 0), NO)
    turn = ((index(dims, 1) == i * NO + u) & (u < NO)).astype(F32)
    for j in range(2 * half):
        shift = size * j % LANES
        moved = pltpu.roll(pltpu.roll(turn, shift, 0), shift, 1) if shift else turn
        turn_ref[j] = (moved * (1.0 - 2.0 * (j % 2))).astype(BF)
    x = (size, 2 * LANES)
    outer, inner = split(index(x, 0), NO)
    lane_outer, lane_inner = split(index(x, 1), NO)
    pick_l = ones_at(outer == lane_outer)
    pick_r = ones_at((outer == lane_inner) & (lane_outer < NO))
    picks = jnp.concatenate([pick_l, pick_r], axis=1)
    x = (size, 32)
    outer, inner = split(index(x, 0), NO)
    slot = split(index(x, 1), 16)[1]
    rows_l = ones_at(outer == slot)
    rows_r = ones_at(inner == slot)
    x = (16, size)
    mask = (split(index(x, 1), NO)[1] == index(x, 0)).astype(F32)
    for copy in copies:
        copy.wait()
    atoms = deriv_ref.shape[1]
    spread = []
    for m in range(3):
        for atom in range(atoms):
            spread.append(deriv_ref[m, atom : atom + 1, :] * mask)
    spread = jnp.concatenate(spread, axis=0)
    spread_hi = spread.astype(BF)
    spread_lo = (spread - spread_hi.astype(F32)).astype(BF)
    for i, part in enumerate((spread_hi, spread_lo)):
        rows = dot(part, picks)
        for n in range(3 * atoms):
            factors[n, 16 * i : 16 * i + 16] = rows[16 * n : 16 * n + 16]
    for p in range(half):
        pair = core * half + p
        atom = pair // NB
        other = near_ref[atom, pair % NB]
        for m in range(3):
            u = factors[m * atoms + atom][:, : 2 * LANES]
            v = factors[m * atoms + other][:, 2 * LANES :]
            for c in range(2):
                j = 2 * p + c
                shift = size * j % LANES
                uj = pltpu.roll(u, shift, 1) if shift else u
                vj = pltpu.roll(v, shift, 1) if shift else v
                kron = dot(rows_l, uj.astype(BF)) * dot(rows_r, vj.astype(BF))
                k_hi = kron.astype(BF)
                hi_ref[j * 3 + m] = k_hi
                lo_ref[j * 3 + m] = (kron - k_hi.astype(F32)).astype(BF)
    tiles = 3 * local_e // 8
    step = 8 * momenta
    first = momenta * (3 * local_e - 8)
    length = bases.shape[3]
    middle = 2 * local_e - 8
    dims = (window, length)
    lane = index(dims, 1)
    depth = index(dims, 0) + 1
    line = None
    for side in range(2):
        gap = lane - momenta * (middle + depth if side else middle - depth)
        for q in range(momenta):
            place = ones_at(gap == (-q) % momenta)
            weights = phonon_ref[side, q].astype(F32).reshape(3 * pairs, window).astype(BF)
            term = dot(weights, place)
            line = term if line is None else line + term
    lane = index((1, length), 1)
    k = split(lane, momenta)[1]
    for a in range(chip_k):
        moved = line
        if a:
            moved = jnp.where(k >= a, pltpu.roll(line, a, 1), pltpu.roll(line, length - momenta + a, 1))
        bases[a] = moved.reshape(3, pairs, length)
    for p in range(half):
        for m in range(3):
            grid = {}
            for a in range(chip_k):
                row = bases[a, m, pl.ds(core * half + p, 1), :]
                block = pltpu.roll(jnp.broadcast_to(row, (8, length)), 0, 1, stride=momenta, stride_axis=0)
                moved = {0: block}
                for t in range(tiles):
                    offset = first - step * t
                    part = offset % LANES
                    if part not in moved:
                        moved[part] = pltpu.roll(block, length - part, 1)
                    start = offset - part
                    grid[(t, a)] = moved[part][:, start : start + 2 * LANES]
            order = []
            per = local_e // 8
            for blk in range(3):
                for a in range(chip_k):
                    order += [grid[(blk * per + i, a)] for i in range(per)]
            t_ref[p * 3 + m] = jnp.concatenate(order, axis=0).astype(BF)


def product_kernel(*refs, half, entries, chips):
    core = my_core()
    blocks = refs[: 2 * chips]
    perm_ref, hi_ref, lo_ref, t_ref = refs[2 * chips : 2 * chips + 4]
    g1_ref, own_ref, low_ref, up_ref, gathered, result = refs[2 * chips + 4 :]
    for s in range(chips):
        gathered[2 * s + core] = blocks[2 * s][...]
        gathered[2 * s + 1 - core] = blocks[2 * s + 1][...]
    count, rows, width = gathered.shape
    depth = count * rows
    tiles = width // LANES
    g = dot(perm_ref[...], gathered[...].reshape(depth, width)).astype(BF)
    block_rows = hi_ref.shape[1]
    sums = [[None] * tiles for _ in range(3)]
    for j in range(2 * half):
        start = (entries // 2) * j // LANES * LANES
        shift = (entries // 2) * j - start
        lhs = g[:, start : start + 2 * LANES]

        def padded(ref, n):
            parts = [ref[n]]
            if shift:
                parts = [jnp.zeros((shift, 2 * LANES), BF)] + parts
            rest = 2 * LANES - shift - block_rows
            if rest:
                parts = parts + [jnp.zeros((rest, 2 * LANES), BF)]
            return jnp.concatenate(parts, axis=0)

        for m in range(3):
            r = dot(lhs, padded(hi_ref, j * 3 + m)) + dot(lhs, padded(lo_ref, j * 3 + m))
            for i in range(2):
                tile = start // LANES + i
                piece = r[:, i * LANES : (i + 1) * LANES]
                sums[m][tile] = piece if sums[m][tile] is None else sums[m][tile] + piece
    high = [[None] * tiles for _ in range(3)]
    low = [[None] * tiles for _ in range(3)]
    for m in range(3):
        for i in range(tiles):
            high[m][i] = sums[m][i].astype(BF)
            low[m][i] = (sums[m][i] - high[m][i].astype(F32)).astype(BF)
            g1_ref[m, :, i * LANES : (i + 1) * LANES] = high[m][i]
    lane = index((1, LANES), 1)
    carried = None
    for p in range(half):
        begin = entries * p
        first = begin // LANES
        last = (begin + entries - 1) // LANES
        total = None
        for m in range(3):
            t = t_ref[p * 3 + m][:, :depth]
            for part in (high, low):
                term = dot(t, jnp.concatenate(part[m][first : last + 1], axis=1))
                total = term if total is None else total + term
        for i in range(first, last + 1):
            tile = total[:, (i - first) * LANES : (i - first + 1) * LANES]
            if i == first and begin % LANES:
                tile = jnp.where(lane < begin % LANES, carried, tile)
            if i == last and (begin + entries) % LANES:
                carried = tile
            else:
                for r in range(6):
                    result[r, :, i * LANES : (i + 1) * LANES] = tile[r * rows : (r + 1) * rows]
    place = lax.axis_index("en")
    below = jnp.where(place == 0, 0.0, 1.0)
    above = jnp.where(place == lax.axis_size("en") - 1, 0.0, 1.0)
    for i, c in enumerate((core, 1 - core)):
        low_ref[i] = (result[c] * below).astype(BF)
        own_ref[i] = result[2 + c]
        up_ref[i] = (result[4 + c] * above).astype(BF)


def polar_kernel(b_own, b_far, prev_own, prev_far, turn_ref, sort_ref, g1_ref, out_ref, gathered, *, half, entries, local_k, local_e, scale):
    core = my_core()
    present = jnp.where(lax.axis_index("en") == 0, 0.0, 1.0)
    gathered[core] = (prev_own[...].astype(F32) * present).astype(BF)
    gathered[1 - core] = (prev_far[...].astype(F32) * present).astype(BF)
    gathered[2 + core] = b_own[...]
    gathered[3 - core] = b_far[...]
    count, rows, width = gathered.shape
    tiles = width // LANES
    b = dot(sort_ref[...], gathered[...].reshape(count * rows, width)).astype(BF)
    sums = [None] * tiles
    for j in range(2 * half):
        start = (entries // 2) * j // LANES * LANES
        r = dot(b[:, start : start + 2 * LANES], turn_ref[j])
        for i in range(2):
            tile = start // LANES + i
            piece = r[:, i * LANES : (i + 1) * LANES]
            sums[tile] = piece if sums[tile] is None else sums[tile] + piece
    chip_k = 2 * local_k
    group = 2 * local_e
    columns = sort_ref.shape[0]
    window = local_e
    momenta = g1_ref.shape[1] // local_e
    lane = index((1, LANES), 1)
    pieces = []
    for p in range(half):
        begin = entries * p
        first = begin // LANES
        last = (begin + entries - 1) // LANES
        parts = []
        for i in range(first, last + 1):
            tile = sums[i]
            if i == first and begin % LANES:
                tile = jnp.where(lane < begin % LANES, 0.0, tile)
            if i == last and (begin + entries) % LANES:
                tile = jnp.where(lane < (begin + entries) % LANES, tile, 0.0)
            parts.append(tile.astype(BF))
        rhs = jnp.concatenate(parts, axis=1)
        held = None
        for m in range(3):
            s = dot_t(g1_ref[m][:, first * LANES : (last + 1) * LANES], rhs)
            acc = None
            for e in range(local_e):
                row = pltpu.roll(s[e * momenta : (e + 1) * momenta], columns - (local_e - e), 1)
                acc = row if acc is None else acc + row
            total = None
            for a in range(chip_k):
                piece = acc if a == 0 else pltpu.roll(acc, columns - group * a, 1)
                piece = piece[:, :LANES]
                if a:
                    piece = pltpu.roll(piece, momenta - a, 0)
                total = piece if total is None else total + piece
            total = jnp.where(lane < window, total * scale, 0.0)
            if m:
                total = pltpu.roll(total, m * (LANES // 4), 1)
            held = total if held is None else held + total
        pieces.append(held)
    targets, en = out_ref.shape[:2]
    for t in range(targets):
        tile = jnp.concatenate(
            [pieces[p][t * local_k + i : t * local_k + i + 1] for i in range(local_k) for p in range(half)], axis=0
        )
        for e in range(en):
            out_ref[t, e] = tile


def total_kernel(in_ref, out_ref, *, half):
    targets, en = in_ref.shape[:2]
    local_k, _, _, window = out_ref.shape
    sums = []
    for c in range(2):
        total = None
        for t in range(c, targets, 2):
            for e in range(en):
                total = in_ref[t, e] if total is None else total + in_ref[t, e]
        sums.append(total)
    for i in range(local_k):
        tile = jnp.concatenate([sums[c][i * half : (i + 1) * half] for c in range(2)], axis=0)
        for m in range(3):
            moved = pltpu.roll(tile, LANES - m * (LANES // 4), 1) if m else tile
            out_ref[i, m] = moved[:, :window]


def sum_kernel(own, below, above, mine, theirs):
    for i, out in enumerate((mine, theirs)):
        out[...] = (own[i] + below[i].astype(F32) + above[i].astype(F32)).astype(BF)


def join_kernel(mine, other, perm_ref, out_ref, halves):
    core = my_core()
    pairs = out_ref.shape[2]
    entries = out_ref.shape[3]
    half = pairs // 2
    halves[core] = mine[...].astype(F32)
    halves[1 - core] = other[...].astype(F32)
    parts = []
    for p in range(pairs):
        begin = entries * (p % half)
        parts.append(halves[p // half][:, begin : begin + entries])
    stacked = jnp.concatenate(parts, axis=0).astype(BF)
    out_ref[...] = dot(perm_ref[...], stacked).astype(BF).reshape(out_ref.shape)


def body(green_less, green_greater, derivative, neighbours, phonon, *, mom, en):
    local_k, local_e, pairs, entries = green_less.shape
    momenta, window = phonon.shape[1], phonon.shape[2]
    atoms = derivative.shape[0]
    half = pairs // 2
    rows = local_k * local_e
    width = half * entries
    chips = mom // 2
    chip_k = 2 * local_k
    total_e = local_e * en
    size = NO * NO

    g_own, b_own, g_far, b_far = call(
        pack_kernel,
        [shape((rows, width), BF)] * 4,
        [green_less, green_greater],
        [
            pltpu.VMEM(green_less.shape, BF),
            pltpu.VMEM(green_less.shape, BF),
            pltpu.VMEM((2, rows, width), F32),
            pltpu.SemaphoreType.DMA((2,)),
        ],
        [HBM, HBM],
    )

    def move(value, dchip, dcore, de):
        links = []
        for m in range(mom):
            target = ((m // 2 + dchip) % chips) * 2 + (m % 2 if dcore == 0 else 1 - m % 2)
            for e in range(en):
                links.append((m * en + e, target * en + (e + de) % en))
        return lax.ppermute(value, ("mom", "en"), links)

    blocks = [g_own, move(g_far, 0, 1, 0)]
    for s in range(1, chips):
        blocks += [move(g_own, -s, 0, 0), move(g_far, -s, 1, 0)]
    b_core = move(b_far, 0, 1, 0)
    prev_own = move(b_own, 0, 0, 1)
    prev_far = move(b_far, 0, 1, 1)

    near = neighbours.astype(jnp.int32)
    deriv = derivative.transpose(1, 0, 2)
    weights = phonon.transpose(0, 1, 3, 4, 2)
    columns = -(-chip_k * 2 * local_e // LANES) * LANES
    k_hi, k_lo, toeplitz, to_energy, to_rows, turn, sort_e = call(
        functools.partial(table_kernel, half=half, local_k=local_k, local_e=local_e),
        [
            shape((6 * half, size, 2 * LANES), BF),
            shape((6 * half, size, 2 * LANES), BF),
            shape((3 * half, 3 * chip_k * local_e, 2 * LANES), BF),
            shape((momenta * local_e,) * 2, BF),
            shape((rows * pairs,) * 2, BF),
            shape((2 * half, 2 * LANES, 2 * LANES), BF),
            shape((columns, 2 * chip_k * local_e), BF),
        ],
        [near, deriv, weights],
        [
            pltpu.SMEM(near.shape, jnp.int32),
            pltpu.VMEM(deriv.shape, F32),
            pltpu.VMEM(weights.shape, BF),
            pltpu.VMEM((3 * atoms, 32, 4 * LANES), F32),
            pltpu.VMEM((chip_k, 3, pairs, 4 * local_e * momenta), F32),
            pltpu.SemaphoreType.DMA((3,)),
        ],
        [HBM, HBM, HBM],
    )

    g1, own, low, up = call(
        functools.partial(product_kernel, half=half, entries=entries, chips=chips),
        [
            shape((3, momenta * local_e, width), BF),
            shape((2, rows, width), F32),
            shape((2, rows, width), BF),
            shape((2, rows, width), BF),
        ],
        blocks + [to_energy, k_hi, k_lo, toeplitz],
        [pltpu.VMEM((2 * chips, rows, width), BF), pltpu.VMEM((6, rows, width), F32)],
    )
    from_above = move(low, 0, 0, -1)
    from_below = move(up, 0, 0, 1)

    (partial,) = call(
        functools.partial(
            polar_kernel, half=half, entries=entries, local_k=local_k, local_e=local_e,
            scale=1.0 / (NO * float(np.sqrt(momenta * total_e))),
        ),
        [shape((mom, en, local_k * half, LANES), F32)],
        [b_own, b_core, prev_own, prev_far, turn, sort_e, g1],
        [pltpu.VMEM((4, rows, width), BF)],
    )
    terms = lax.all_to_all(
        partial.reshape(mom * en, local_k * half, LANES), ("mom", "en"), split_axis=0, concat_axis=0, tiled=True
    )
    (polar,) = call(
        functools.partial(total_kernel, half=half),
        [shape((local_k, 3, pairs, window), F32)],
        [terms.reshape(mom, en, local_k * half, LANES)],
    )
    polar = polar.transpose(0, 3, 1, 2)

    mine, theirs = call(
        sum_kernel, [shape((rows, width), BF)] * 2, [own, from_below, from_above]
    )
    other = move(theirs, 0, 1, 0)
    (self_energy,) = call(
        join_kernel,
        [shape(green_less.shape, BF)],
        [mine, other, to_rows],
        [pltpu.VMEM((2, rows, width), F32)],
    )
    return (self_energy, polar)


def solution(mesh):
    return jax.shard_map(
        functools.partial(body, mom=mesh.shape["mom"], en=mesh.shape["en"]),
        mesh=mesh,
        in_specs=(P("mom", "en", None, None), P("mom", "en", None, None), P(), P(), P()),
        out_specs=(P("mom", "en", None, None), P("mom", None, None, None)),
        check_vma=False,
    )
```

```python
import functools

import jax
import jax.numpy as jnp
import numpy as np
from jax import lax
from jax.experimental import pallas as pl
from jax.experimental.pallas import tpu as pltpu
from jax.sharding import PartitionSpec as P

NO = 12
NB = 4
LANES = 128
BF = jnp.bfloat16
F32 = jnp.float32
HIGHEST = lax.Precision.HIGHEST
VMEM = pl.BlockSpec(memory_space=pltpu.VMEM)
HBM = pl.BlockSpec(memory_space=pltpu.HBM)
MIB = 1024 * 1024


def dot(a, b):
    return jnp.dot(a, b, preferred_element_type=F32)


def dot_t(a, b):
    return lax.dot_general(a, b, (((1,), (1,)), ((), ())), preferred_element_type=F32)


def call(kernel, outs, ins, work, scratch=(), specs=None, limit=24):
    return pl.pallas_call(
        kernel,
        out_shape=outs,
        in_specs=specs or [VMEM] * len(ins),
        out_specs=[VMEM] * len(outs),
        scratch_shapes=list(scratch),
        compiler_params=pltpu.CompilerParams(vmem_limit_bytes=int(limit * MIB)),
        cost_estimate=pl.CostEstimate(flops=int(work * 1e9), bytes_accessed=0, transcendentals=0),
    )(*ins)


def my_core():
    return lax.rem(lax.axis_index("mom"), 2).astype(jnp.int32)


def index(dims, axis):
    return lax.broadcasted_iota(jnp.int32, dims, axis)


def split(value, count):
    whole = jnp.floor((value.astype(F32) + 0.5) * (1.0 / count)).astype(jnp.int32)
    return whole, value - count * whole


def ones_at(condition):
    return condition.astype(F32).astype(BF)


def shape(dims, dtype):
    return jax.ShapeDtypeStruct(dims, dtype)


def pack_kernel(g_hbm, b_hbm, g_own, b_own, g_far, b_far, g_ref, b_ref, halves, sems):
    core = my_core()
    copies = []
    for i, (src, dst) in enumerate(((g_hbm, g_ref), (b_hbm, b_ref))):
        copies.append(pltpu.make_async_copy(src, dst, sems.at[i]))
        copies[-1].start()
    rows = g_own.shape[0]
    pairs = g_ref.shape[2]
    entries = g_ref.shape[3]
    half = pairs // 2
    dims = (rows, rows * pairs)
    gap = index(dims, 1) - pairs * index(dims, 0)
    perm = jnp.concatenate([ones_at(gap == p) for p in range(pairs)], axis=0)
    for copy, src, own, far in ((copies[0], g_ref, g_own, g_far), (copies[1], b_ref, b_own, b_far)):
        copy.wait()
        sorted_rows = dot(perm, src[...].reshape(rows * pairs, entries))
        for h in range(2):
            parts = [sorted_rows[(h * half + j) * rows : (h * half + j + 1) * rows] for j in range(half)]
            halves[h] = jnp.concatenate(parts, axis=1)
        own[...] = halves[core].astype(BF)
        far[...] = halves[1 - core].astype(BF)


def table_kernel(
    near_ref, deriv_ref, phonon_ref, hi_ref, lo_ref, t_ref, perm_ref, join_ref, turn_ref, sort_ref,
    factors, bases, *, half, local_k, local_e,
):
    core = my_core()
    _, momenta, _, pairs, window = phonon_ref.shape
    size = NO * NO
    chip_k = 2 * local_k
    dims = perm_ref.shape
    e, k = split(index(dims, 0), momenta)
    perm_ref[...] = ones_at(index(dims, 1) == k * local_e + e)
    dims = join_ref.shape
    row, p = split(index(dims, 0), pairs)
    join_ref[...] = ones_at(index(dims, 1) == p * (local_k * local_e) + row)
    dims = sort_ref.shape
    k, i = split(index(dims, 0), 2 * local_e)
    at = jnp.where(i < local_e, (chip_k + k) * local_e + local_e - 1 - i, k * local_e + 2 * local_e - 1 - i)
    sort_ref[...] = ones_at((index(dims, 1) == at) & (k < chip_k))
    dims = turn_ref.shape[1:]
    u, i = split(index(dims, 0), NO)
    turn = ((index(dims, 1) == i * NO + u) & (u < NO)).astype(F32)
    for j in range(2 * half):
        shift = size * j % LANES
        moved = pltpu.roll(pltpu.roll(turn, shift, 0), shift, 1) if shift else turn
        turn_ref[j] = (moved * (1.0 - 2.0 * (j % 2))).astype(BF)
    x = (size, 2 * LANES)
    outer, inner = split(index(x, 0), NO)
    lane_outer, lane_inner = split(index(x, 1), NO)
    pick_l = ones_at(outer == lane_outer)
    pick_r = ones_at((outer == lane_inner) & (lane_outer < NO))
    picks = jnp.concatenate([pick_l, pick_r], axis=1)
    x = (size, 32)
    outer, inner = split(index(x, 0), NO)
    slot = split(index(x, 1), 16)[1]
    rows_l = ones_at(outer == slot)
    rows_r = ones_at(inner == slot)
    x = (16, size)
    mask = (split(index(x, 1), NO)[1] == index(x, 0)).astype(F32)
    atoms = deriv_ref.shape[1]
    spread = []
    for m in range(3):
        for atom in range(atoms):
            spread.append(deriv_ref[m, atom : atom + 1, :] * mask)
    spread = jnp.concatenate(spread, axis=0)
    spread_hi = spread.astype(BF)
    spread_lo = (spread - spread_hi.astype(F32)).astype(BF)
    for i, part in enumerate((spread_hi, spread_lo)):
        rows = dot(part, picks)
        for n in range(3 * atoms):
            factors[n, 16 * i : 16 * i + 16] = rows[16 * n : 16 * n + 16]
    for p in range(half):
        pair = core * half + p
        atom = pair // NB
        other = near_ref[atom, pair % NB]
        for m in range(3):
            u = factors[m * atoms + atom][:, : 2 * LANES]
            v = factors[m * atoms + other][:, 2 * LANES :]
            for c in range(2):
                j = 2 * p + c
                shift = size * j % LANES
                uj = pltpu.roll(u, shift, 1) if shift else u
                vj = pltpu.roll(v, shift, 1) if shift else v
                kron = dot(rows_l, uj.astype(BF)) * dot(rows_r, vj.astype(BF))
                k_hi = kron.astype(BF)
                hi_ref[j * 3 + m] = k_hi
                lo_ref[j * 3 + m] = (kron - k_hi.astype(F32)).astype(BF)
    tiles = 3 * local_e // 8
    step = 8 * momenta
    first = momenta * (3 * local_e - 8)
    length = bases.shape[3]
    middle = 2 * local_e - 8
    dims = (window, length)
    lane = index(dims, 1)
    depth = index(dims, 0) + 1
    line = None
    for side in range(2):
        gap = lane - momenta * (middle + depth if side else middle - depth)
        for q in range(momenta):
            place = ones_at(gap == (-q) % momenta)
            weights = phonon_ref[side, q].astype(F32).reshape(3 * pairs, window).astype(BF)
            term = dot(weights, place)
            line = term if line is None else line + term
    lane = index((1, length), 1)
    k = split(lane, momenta)[1]
    for a in range(chip_k):
        moved = line
        if a:
            moved = jnp.where(k >= a, pltpu.roll(line, a, 1), pltpu.roll(line, length - momenta + a, 1))
        bases[a] = moved.reshape(3, pairs, length)
    for p in range(half):
        for m in range(3):
            grid = {}
            for a in range(chip_k):
                row = bases[a, m, pl.ds(core * half + p, 1), :]
                block = pltpu.roll(jnp.broadcast_to(row, (8, length)), 0, 1, stride=momenta, stride_axis=0)
                moved = {0: block}
                for t in range(tiles):
                    offset = first - step * t
                    part = offset % LANES
                    if part not in moved:
                        moved[part] = pltpu.roll(block, length - part, 1)
                    start = offset - part
                    grid[(t, a)] = moved[part][:, start : start + 2 * LANES]
            order = []
            per = local_e // 8
            for blk in range(3):
                for a in range(chip_k):
                    order += [grid[(blk * per + i, a)] for i in range(per)]
            t_ref[p * 3 + m] = jnp.concatenate(order, axis=0).astype(BF)


def product_kernel(*refs, half, entries, chips):
    core = my_core()
    blocks = refs[: 2 * chips]
    perm_ref, hi_ref, lo_ref, t_ref = refs[2 * chips : 2 * chips + 4]
    g1_ref, own_ref, low_ref, up_ref, gathered, result = refs[2 * chips + 4 :]
    for s in range(chips):
        gathered[2 * s + core] = blocks[2 * s][...]
        gathered[2 * s + 1 - core] = blocks[2 * s + 1][...]
    count, rows, width = gathered.shape
    depth = count * rows
    tiles = width // LANES
    g = dot(perm_ref[...], gathered[...].reshape(depth, width)).astype(BF)
    block_rows = hi_ref.shape[1]
    sums = [[None] * tiles for _ in range(3)]
    for j in range(2 * half):
        start = (entries // 2) * j // LANES * LANES
        shift = (entries // 2) * j - start
        lhs = g[:, start : start + 2 * LANES]

        def padded(ref, n):
            parts = [ref[n]]
            if shift:
                parts = [jnp.zeros((shift, 2 * LANES), BF)] + parts
            rest = 2 * LANES - shift - block_rows
            if rest:
                parts = parts + [jnp.zeros((rest, 2 * LANES), BF)]
            return jnp.concatenate(parts, axis=0)

        for m in range(3):
            r = dot(lhs, padded(hi_ref, j * 3 + m)) + dot(lhs, padded(lo_ref, j * 3 + m))
            for i in range(2):
                tile = start // LANES + i
                piece = r[:, i * LANES : (i + 1) * LANES]
                sums[m][tile] = piece if sums[m][tile] is None else sums[m][tile] + piece
    high = [[None] * tiles for _ in range(3)]
    low = [[None] * tiles for _ in range(3)]
    for m in range(3):
        for i in range(tiles):
            high[m][i] = sums[m][i].astype(BF)
            low[m][i] = (sums[m][i] - high[m][i].astype(F32)).astype(BF)
            g1_ref[m, :, i * LANES : (i + 1) * LANES] = high[m][i]
    lane = index((1, LANES), 1)
    carried = None
    for p in range(half):
        begin = entries * p
        first = begin // LANES
        last = (begin + entries - 1) // LANES
        total = None
        for m in range(3):
            t = t_ref[p * 3 + m][:, :depth]
            for part in (high, low):
                term = dot(t, jnp.concatenate(part[m][first : last + 1], axis=1))
                total = term if total is None else total + term
        for i in range(first, last + 1):
            tile = total[:, (i - first) * LANES : (i - first + 1) * LANES]
            if i == first and begin % LANES:
                tile = jnp.where(lane < begin % LANES, carried, tile)
            if i == last and (begin + entries) % LANES:
                carried = tile
            else:
                for r in range(6):
                    result[r, :, i * LANES : (i + 1) * LANES] = tile[r * rows : (r + 1) * rows]
    place = lax.axis_index("en")
    below = jnp.where(place == 0, 0.0, 1.0)
    above = jnp.where(place == lax.axis_size("en") - 1, 0.0, 1.0)
    for i, c in enumerate((core, 1 - core)):
        low_ref[i] = (result[c] * below).astype(BF)
        own_ref[i] = result[2 + c]
        up_ref[i] = (result[4 + c] * above).astype(BF)


def polar_kernel(b_own, b_far, prev_own, prev_far, turn_ref, sort_ref, g1_ref, out_ref, gathered, *, half, entries, local_k, local_e, scale):
    core = my_core()
    present = jnp.where(lax.axis_index("en") == 0, 0.0, 1.0)
    gathered[core] = (prev_own[...].astype(F32) * present).astype(BF)
    gathered[1 - core] = (prev_far[...].astype(F32) * present).astype(BF)
    gathered[2 + core] = b_own[...]
    gathered[3 - core] = b_far[...]
    count, rows, width = gathered.shape
    tiles = width // LANES
    b = dot(sort_ref[...], gathered[...].reshape(count * rows, width)).astype(BF)
    sums = [None] * tiles
    for j in range(2 * half):
        start = (entries // 2) * j // LANES * LANES
        r = dot(b[:, start : start + 2 * LANES], turn_ref[j])
        for i in range(2):
            tile = start // LANES + i
            piece = r[:, i * LANES : (i + 1) * LANES]
            sums[tile] = piece if sums[tile] is None else sums[tile] + piece
    chip_k = 2 * local_k
    group = 2 * local_e
    columns = sort_ref.shape[0]
    window = local_e
    momenta = g1_ref.shape[1] // local_e
    lane = index((1, LANES), 1)
    pieces = []
    for p in range(half):
        begin = entries * p
        first = begin // LANES
        last = (begin + entries - 1) // LANES
        parts = []
        for i in range(first, last + 1):
            tile = sums[i]
            if i == first and begin % LANES:
                tile = jnp.where(lane < begin % LANES, 0.0, tile)
            if i == last and (begin + entries) % LANES:
                tile = jnp.where(lane < (begin + entries) % LANES, tile, 0.0)
            parts.append(tile.astype(BF))
        rhs = jnp.concatenate(parts, axis=1)
        held = None
        for m in range(3):
            s = dot_t(g1_ref[m][:, first * LANES : (last + 1) * LANES], rhs)
            acc = None
            for e in range(local_e):
                row = pltpu.roll(s[e * momenta : (e + 1) * momenta], columns - (local_e - e), 1)
                acc = row if acc is None else acc + row
            total = None
            for a in range(chip_k):
                piece = acc if a == 0 else pltpu.roll(acc, columns - group * a, 1)
                piece = piece[:, :LANES]
                if a:
                    piece = pltpu.roll(piece, momenta - a, 0)
                total = piece if total is None else total + piece
            total = jnp.where(lane < window, total * scale, 0.0)
            if m:
                total = pltpu.roll(total, m * (LANES // 4), 1)
            held = total if held is None else held + total
        pieces.append(held)
    targets, en = out_ref.shape[:2]
    for t in range(targets):
        tile = jnp.concatenate(
            [pieces[p][t * local_k + i : t * local_k + i + 1] for i in range(local_k) for p in range(half)], axis=0
        )
        for e in range(en):
            out_ref[t, e] = tile


def total_kernel(in_ref, after_ref, out_ref, *, half):
    targets, en = in_ref.shape[:2]
    local_k, _, _, window = out_ref.shape
    sums = []
    for c in range(2):
        total = None
        for t in range(c, targets, 2):
            for e in range(en):
                total = in_ref[t, e] if total is None else total + in_ref[t, e]
        sums.append(total)
    for i in range(local_k):
        tile = jnp.concatenate([sums[c][i * half : (i + 1) * half] for c in range(2)], axis=0)
        for m in range(3):
            moved = pltpu.roll(tile, LANES - m * (LANES // 4), 1) if m else tile
            out_ref[i, m] = moved[:, :window]


def sum_kernel(own, below, above, mine, theirs):
    for i, out in enumerate((mine, theirs)):
        out[...] = (own[i] + below[i].astype(F32) + above[i].astype(F32)).astype(BF)


def join_kernel(mine, other, perm_ref, out_ref, mark_ref, halves):
    core = my_core()
    pairs = out_ref.shape[2]
    entries = out_ref.shape[3]
    half = pairs // 2
    halves[core] = mine[...].astype(F32)
    halves[1 - core] = other[...].astype(F32)
    parts = []
    for p in range(pairs):
        begin = entries * (p % half)
        parts.append(halves[p // half][:, begin : begin + entries])
    stacked = jnp.concatenate(parts, axis=0).astype(BF)
    mark_ref[...] = jnp.zeros(mark_ref.shape, F32)
    out_ref[...] = dot(perm_ref[...], stacked).astype(BF).reshape(out_ref.shape)


def body(green_less, green_greater, derivative, neighbours, phonon, *, mom, en):
    local_k, local_e, pairs, entries = green_less.shape
    momenta, window = phonon.shape[1], phonon.shape[2]
    atoms = derivative.shape[0]
    half = pairs // 2
    rows = local_k * local_e
    width = half * entries
    chips = mom // 2
    chip_k = 2 * local_k
    total_e = local_e * en
    size = NO * NO

    deriv = derivative.transpose(1, 0, 2)
    weights = phonon.transpose(0, 1, 3, 4, 2)
    g_own, b_own, g_far, b_far = call(
        pack_kernel,
        [shape((rows, width), BF)] * 4,
        [green_less, green_greater],
        1.5,
        [
            pltpu.VMEM(green_less.shape, BF),
            pltpu.VMEM(green_less.shape, BF),
            pltpu.VMEM((2, rows, width), F32),
            pltpu.SemaphoreType.DMA((2,)),
        ],
        [HBM] * 2,
        limit=53.25,
    )

    def move(value, dchip, dcore, de):
        links = []
        for m in range(mom):
            target = ((m // 2 + dchip) % chips) * 2 + (m % 2 if dcore == 0 else 1 - m % 2)
            for e in range(en):
                links.append((m * en + e, target * en + (e + de) % en))
        return lax.ppermute(value, ("mom", "en"), links)

    blocks = [g_own, move(g_far, 0, 1, 0)]
    for s in range(1, chips):
        blocks += [move(g_own, -s, 0, 0), move(g_far, -s, 1, 0)]
    b_core = move(b_far, 0, 1, 0)
    prev_own = move(b_own, 0, 0, 1)
    prev_far = move(b_far, 0, 1, 1)

    near = neighbours.astype(jnp.int32)
    columns = -(-chip_k * 2 * local_e // LANES) * LANES
    k_hi, k_lo, toeplitz, to_energy, to_rows, turn, sort_e = call(
        functools.partial(table_kernel, half=half, local_k=local_k, local_e=local_e),
        [
            shape((6 * half, size, 2 * LANES), BF),
            shape((6 * half, size, 2 * LANES), BF),
            shape((3 * half, 3 * chip_k * local_e, 2 * LANES), BF),
            shape((momenta * local_e,) * 2, BF),
            shape((rows * pairs,) * 2, BF),
            shape((2 * half, 2 * LANES, 2 * LANES), BF),
            shape((columns, 2 * chip_k * local_e), BF),
        ],
        [near, deriv, weights],
        3,
        [
            pltpu.VMEM((3 * atoms, 32, 4 * LANES), F32),
            pltpu.VMEM((chip_k, 3, pairs, 4 * local_e * momenta), F32),
        ],
        [pl.BlockSpec(memory_space=pltpu.SMEM), VMEM, VMEM],
    )

    g1, own, low, up = call(
        functools.partial(product_kernel, half=half, entries=entries, chips=chips),
        [
            shape((3, momenta * local_e, width), BF),
            shape((2, rows, width), F32),
            shape((2, rows, width), BF),
            shape((2, rows, width), BF),
        ],
        blocks + [to_energy, k_hi, k_lo, toeplitz],
        4,
        [pltpu.VMEM((2 * chips, rows, width), BF), pltpu.VMEM((6, rows, width), F32)],
    )
    from_above = move(low, 0, 0, -1)
    from_below = move(up, 0, 0, 1)

    (partial,) = call(
        functools.partial(
            polar_kernel, half=half, entries=entries, local_k=local_k, local_e=local_e,
            scale=1.0 / (NO * float(np.sqrt(momenta * total_e))),
        ),
        [shape((mom, en, local_k * half, LANES), F32)],
        [b_own, b_core, prev_own, prev_far, turn, sort_e, g1],
        3,
        [pltpu.VMEM((4, rows, width), BF)],
    )
    terms = lax.all_to_all(
        partial.reshape(mom * en, local_k * half, LANES), ("mom", "en"), split_axis=0, concat_axis=0, tiled=True
    )
    mine, theirs = call(
        sum_kernel, [shape((rows, width), BF)] * 2, [own, from_below, from_above], 0.1
    )
    other = move(theirs, 0, 1, 0)
    self_energy, mark = call(
        join_kernel,
        [shape(green_less.shape, BF), shape((8, LANES), F32)],
        [mine, other, to_rows],
        1,
        [pltpu.VMEM((2, rows, width), F32)],
    )
    (polar,) = call(
        functools.partial(total_kernel, half=half),
        [shape((local_k, 3, pairs, window), F32)],
        [terms.reshape(mom, en, local_k * half, LANES), mark],
        0.5,
    )
    polar = polar.transpose(0, 3, 1, 2)
    return (self_energy, polar)


def solution(mesh):
    return jax.shard_map(
        functools.partial(body, mom=mesh.shape["mom"], en=mesh.shape["en"]),
        mesh=mesh,
        in_specs=(P("mom", "en", None, None), P("mom", "en", None, None), P(), P(), P()),
        out_specs=(P("mom", "en", None, None), P("mom", None, None, None)),
        check_vma=False,
    )
```

```python
import functools

import jax
import jax.numpy as jnp
import numpy as np
from jax import lax
from jax.experimental import pallas as pl
from jax.experimental.pallas import tpu as pltpu
from jax.sharding import PartitionSpec as P

NO = 12
NB = 4
LANES = 128
BF = jnp.bfloat16
F32 = jnp.float32
HIGHEST = lax.Precision.HIGHEST
VMEM = pl.BlockSpec(memory_space=pltpu.VMEM)
HBM = pl.BlockSpec(memory_space=pltpu.HBM)
MIB = 1024 * 1024


def dot(a, b):
    return jnp.dot(a, b, preferred_element_type=F32)


def dot_t(a, b):
    return lax.dot_general(a, b, (((1,), (1,)), ((), ())), preferred_element_type=F32)


def call(kernel, outs, ins, work, scratch=(), specs=None, limit=24):
    return pl.pallas_call(
        kernel,
        out_shape=outs,
        in_specs=specs or [VMEM] * len(ins),
        out_specs=[VMEM] * len(outs),
        scratch_shapes=list(scratch),
        compiler_params=pltpu.CompilerParams(vmem_limit_bytes=int(limit * MIB)),
        cost_estimate=pl.CostEstimate(flops=int(work * 1e9), bytes_accessed=0, transcendentals=0),
    )(*ins)


def my_core():
    return lax.rem(lax.axis_index("mom"), 2).astype(jnp.int32)


def index(dims, axis):
    return lax.broadcasted_iota(jnp.int32, dims, axis)


def split(value, count):
    whole = jnp.floor((value.astype(F32) + 0.5) * (1.0 / count)).astype(jnp.int32)
    return whole, value - count * whole


def ones_at(condition):
    return condition.astype(F32).astype(BF)


def shape(dims, dtype):
    return jax.ShapeDtypeStruct(dims, dtype)


def pack_kernel(g_hbm, b_hbm, g_own, b_own, g_far, b_far, g_ref, b_ref, halves, sems):
    core = my_core()
    copies = []
    for i, (src, dst) in enumerate(((g_hbm, g_ref), (b_hbm, b_ref))):
        copies.append(pltpu.make_async_copy(src, dst, sems.at[i]))
        copies[-1].start()
    rows = g_own.shape[0]
    pairs = g_ref.shape[2]
    entries = g_ref.shape[3]
    half = pairs // 2
    dims = (rows, rows * pairs)
    gap = index(dims, 1) - pairs * index(dims, 0)
    perm = jnp.concatenate([ones_at(gap == p) for p in range(pairs)], axis=0)
    for copy, src, own, far in ((copies[0], g_ref, g_own, g_far), (copies[1], b_ref, b_own, b_far)):
        copy.wait()
        sorted_rows = dot(perm, src[...].reshape(rows * pairs, entries))
        for h in range(2):
            parts = [sorted_rows[(h * half + j) * rows : (h * half + j + 1) * rows] for j in range(half)]
            halves[h] = jnp.concatenate(parts, axis=1)
        own[...] = halves[core].astype(BF)
        far[...] = halves[1 - core].astype(BF)


def table_kernel(
    near_ref, deriv_ref, phonon_ref, hi_ref, lo_ref, t_ref, perm_ref, join_ref, turn_ref, sort_ref,
    factors, bases, *, half, local_k, local_e,
):
    core = my_core()
    _, momenta, _, pairs, window = phonon_ref.shape
    size = NO * NO
    chip_k = 2 * local_k
    dims = perm_ref.shape
    e, k = split(index(dims, 0), momenta)
    perm_ref[...] = ones_at(index(dims, 1) == k * local_e + e)
    dims = join_ref.shape
    row, p = split(index(dims, 0), pairs)
    join_ref[...] = ones_at(index(dims, 1) == p * (local_k * local_e) + row)
    dims = sort_ref.shape
    k, i = split(index(dims, 0), 2 * local_e)
    at = jnp.where(i < local_e, (chip_k + k) * local_e + local_e - 1 - i, k * local_e + 2 * local_e - 1 - i)
    sort_ref[...] = ones_at((index(dims, 1) == at) & (k < chip_k))
    dims = turn_ref.shape[1:]
    u, i = split(index(dims, 0), NO)
    turn = ((index(dims, 1) == i * NO + u) & (u < NO)).astype(F32)
    for j in range(2 * half):
        shift = size * j % LANES
        moved = pltpu.roll(pltpu.roll(turn, shift, 0), shift, 1) if shift else turn
        turn_ref[j] = (moved * (1.0 - 2.0 * (j % 2))).astype(BF)
    x = (size, 2 * LANES)
    outer, inner = split(index(x, 0), NO)
    lane_outer, lane_inner = split(index(x, 1), NO)
    pick_l = ones_at(outer == lane_outer)
    pick_r = ones_at((outer == lane_inner) & (lane_outer < NO))
    picks = jnp.concatenate([pick_l, pick_r], axis=1)
    x = (size, 32)
    outer, inner = split(index(x, 0), NO)
    slot = split(index(x, 1), 16)[1]
    rows_l = ones_at(outer == slot)
    rows_r = ones_at(inner == slot)
    x = (16, size)
    mask = (split(index(x, 1), NO)[1] == index(x, 0)).astype(F32)
    atoms = deriv_ref.shape[1]
    spread = []
    for m in range(3):
        for atom in range(atoms):
            spread.append(deriv_ref[m, atom : atom + 1, :] * mask)
    spread = jnp.concatenate(spread, axis=0)
    spread_hi = spread.astype(BF)
    spread_lo = (spread - spread_hi.astype(F32)).astype(BF)
    for i, part in enumerate((spread_hi, spread_lo)):
        rows = dot(part, picks)
        for n in range(3 * atoms):
            factors[n, 16 * i : 16 * i + 16] = rows[16 * n : 16 * n + 16]
    for p in range(half):
        pair = core * half + p
        atom = pair // NB
        other = near_ref[atom, pair % NB]
        for m in range(3):
            u = factors[m * atoms + atom][:, : 2 * LANES]
            v = factors[m * atoms + other][:, 2 * LANES :]
            for c in range(2):
                j = 2 * p + c
                shift = size * j % LANES
                uj = pltpu.roll(u, shift, 1) if shift else u
                vj = pltpu.roll(v, shift, 1) if shift else v
                kron = dot(rows_l, uj.astype(BF)) * dot(rows_r, vj.astype(BF))
                k_hi = kron.astype(BF)
                hi_ref[j * 3 + m] = k_hi
                lo_ref[j * 3 + m] = (kron - k_hi.astype(F32)).astype(BF)
    tiles = 3 * local_e // 8
    step = 8 * momenta
    first = momenta * (3 * local_e - 8)
    length = bases.shape[3]
    middle = 2 * local_e - 8
    dims = (window, length)
    lane = index(dims, 1)
    depth = index(dims, 0) + 1
    line = None
    for side in range(2):
        gap = lane - momenta * (middle + depth if side else middle - depth)
        for q in range(momenta):
            place = ones_at(gap == (-q) % momenta)
            weights = phonon_ref[side, q].astype(F32).reshape(3 * pairs, window).astype(BF)
            term = dot(weights, place)
            line = term if line is None else line + term
    lane = index((1, length), 1)
    k = split(lane, momenta)[1]
    for a in range(chip_k):
        moved = line
        if a:
            moved = jnp.where(k >= a, pltpu.roll(line, a, 1), pltpu.roll(line, length - momenta + a, 1))
        bases[a] = moved.reshape(3, pairs, length)
    for p in range(half):
        for m in range(3):
            grid = {}
            for a in range(chip_k):
                row = bases[a, m, pl.ds(core * half + p, 1), :]
                block = pltpu.roll(jnp.broadcast_to(row, (8, length)), 0, 1, stride=momenta, stride_axis=0)
                moved = {0: block}
                for t in range(tiles):
                    offset = first - step * t
                    part = offset % LANES
                    if part not in moved:
                        moved[part] = pltpu.roll(block, length - part, 1)
                    start = offset - part
                    grid[(t, a)] = moved[part][:, start : start + 2 * LANES]
            order = []
            per = local_e // 8
            for blk in (0, 2, 1):
                for a in range(chip_k):
                    order += [grid[(blk * per + i, a)] for i in range(per)]
            t_ref[p * 3 + m] = jnp.concatenate(order, axis=0).astype(BF)


def product_kernel(*refs, half, entries, chips):
    core = my_core()
    blocks = refs[: 2 * chips]
    perm_ref, hi_ref, lo_ref, t_ref = refs[2 * chips : 2 * chips + 4]
    high_ref, rest_ref, pair_ref, next_ref, gathered, result = refs[2 * chips + 4 :]
    for s in range(chips):
        gathered[2 * s + core] = blocks[2 * s][...]
        gathered[2 * s + 1 - core] = blocks[2 * s + 1][...]
    count, rows, width = gathered.shape
    depth = count * rows
    tiles = width // LANES
    g = dot(perm_ref[...], gathered[...].reshape(depth, width)).astype(BF)
    block_rows = hi_ref.shape[1]
    sums = [[None] * tiles for _ in range(3)]
    for j in range(2 * half):
        start = (entries // 2) * j // LANES * LANES
        shift = (entries // 2) * j - start
        lhs = g[:, start : start + 2 * LANES]

        def padded(ref, n):
            parts = [ref[n]]
            if shift:
                parts = [jnp.zeros((shift, 2 * LANES), BF)] + parts
            rest = 2 * LANES - shift - block_rows
            if rest:
                parts = parts + [jnp.zeros((rest, 2 * LANES), BF)]
            return jnp.concatenate(parts, axis=0)

        for m in range(3):
            r = dot(lhs, padded(hi_ref, j * 3 + m)) + dot(lhs, padded(lo_ref, j * 3 + m))
            for i in range(2):
                tile = start // LANES + i
                piece = r[:, i * LANES : (i + 1) * LANES]
                sums[m][tile] = piece if sums[m][tile] is None else sums[m][tile] + piece
    for m in range(3):
        for i in range(tiles):
            at = slice(i * LANES, (i + 1) * LANES)
            high = sums[m][i].astype(BF)
            high_ref[m, :, at] = high
            rest_ref[m, :, at] = (sums[m][i] - high.astype(F32)).astype(BF)
    correlate(t_ref, 0, 4, high_ref, rest_ref, result, entries)
    place = lax.axis_index("en")
    odd = lax.rem(place, 2)
    below = jnp.where(place == 0, 0.0, 1.0)
    above = jnp.where(place == lax.axis_size("en") - 1, 0.0, 1.0)
    keep_pair = jnp.where(odd == 1, below, above)
    keep_next = jnp.where(odd == 1, above, below)
    for i, c in enumerate((core, 1 - core)):
        pair_ref[i] = (result[2 - 2 * odd + c] * keep_pair).astype(BF)
        next_ref[i] = (result[2 * odd + c] * keep_next).astype(BF)


def correlate(t_ref, begin_row, count, high_ref, rest_ref, result, entries):
    _, rows, width = result.shape
    depth = high_ref.shape[1]
    lane = index((1, LANES), 1)
    at_rows = slice(begin_row * rows, (begin_row + count) * rows)
    carried = None
    for p in range(width // entries):
        begin = entries * p
        first = begin // LANES
        last = (begin + entries - 1) // LANES
        total = None
        for m in range(3):
            t = t_ref[p * 3 + m, at_rows, :][:, :depth]
            for part in (high_ref, rest_ref):
                term = dot(t, part[m, :, first * LANES : (last + 1) * LANES])
                total = term if total is None else total + term
        for i in range(first, last + 1):
            tile = total[:, (i - first) * LANES : (i - first + 1) * LANES]
            if i == first and begin % LANES:
                tile = jnp.where(lane < begin % LANES, carried, tile)
            if i == last and (begin + entries) % LANES:
                carried = tile
            else:
                for r in range(count):
                    result[r, :, i * LANES : (i + 1) * LANES] = tile[r * rows : (r + 1) * rows]


def own_kernel(t_ref, high_ref, rest_ref, after_ref, own_ref, *, entries):
    correlate(t_ref, 4, 2, high_ref, rest_ref, own_ref, entries)


def polar_kernel(b_own, b_far, prev_own, prev_far, turn_ref, sort_ref, g1_ref, out_ref, mark_ref, gathered, *, half, entries, local_k, local_e, scale):
    core = my_core()
    present = jnp.where(lax.axis_index("en") == 0, 0.0, 1.0)
    gathered[core] = (prev_own[...].astype(F32) * present).astype(BF)
    gathered[1 - core] = (prev_far[...].astype(F32) * present).astype(BF)
    gathered[2 + core] = b_own[...]
    gathered[3 - core] = b_far[...]
    count, rows, width = gathered.shape
    tiles = width // LANES
    b = dot(sort_ref[...], gathered[...].reshape(count * rows, width)).astype(BF)
    sums = [None] * tiles
    for j in range(2 * half):
        start = (entries // 2) * j // LANES * LANES
        r = dot(b[:, start : start + 2 * LANES], turn_ref[j])
        for i in range(2):
            tile = start // LANES + i
            piece = r[:, i * LANES : (i + 1) * LANES]
            sums[tile] = piece if sums[tile] is None else sums[tile] + piece
    chip_k = 2 * local_k
    group = 2 * local_e
    columns = sort_ref.shape[0]
    window = local_e
    momenta = g1_ref.shape[1] // local_e
    lane = index((1, LANES), 1)
    mark_ref[...] = jnp.zeros(mark_ref.shape, F32)
    pieces = []
    for p in range(half):
        begin = entries * p
        first = begin // LANES
        last = (begin + entries - 1) // LANES
        parts = []
        for i in range(first, last + 1):
            tile = sums[i]
            if i == first and begin % LANES:
                tile = jnp.where(lane < begin % LANES, 0.0, tile)
            if i == last and (begin + entries) % LANES:
                tile = jnp.where(lane < (begin + entries) % LANES, tile, 0.0)
            parts.append(tile.astype(BF))
        rhs = jnp.concatenate(parts, axis=1)
        held = None
        for m in range(3):
            s = dot_t(g1_ref[m][:, first * LANES : (last + 1) * LANES], rhs)
            acc = None
            for e in range(local_e):
                row = pltpu.roll(s[e * momenta : (e + 1) * momenta], columns - (local_e - e), 1)
                acc = row if acc is None else acc + row
            total = None
            for a in range(chip_k):
                piece = acc if a == 0 else pltpu.roll(acc, columns - group * a, 1)
                piece = piece[:, :LANES]
                if a:
                    piece = pltpu.roll(piece, momenta - a, 0)
                total = piece if total is None else total + piece
            total = jnp.where(lane < window, total * scale, 0.0)
            if m:
                total = pltpu.roll(total, m * (LANES // 4), 1)
            held = total if held is None else held + total
        pieces.append(held)
    targets, en = out_ref.shape[:2]
    for t in range(targets):
        tile = jnp.concatenate(
            [pieces[p][t * local_k + i : t * local_k + i + 1] for i in range(local_k) for p in range(half)], axis=0
        )
        for e in range(en):
            out_ref[t, e] = tile


def total_kernel(in_ref, after_ref, out_ref, *, half):
    targets, en = in_ref.shape[:2]
    local_k, _, _, window = out_ref.shape
    sums = []
    for c in range(2):
        total = None
        for t in range(c, targets, 2):
            for e in range(en):
                total = in_ref[t, e] if total is None else total + in_ref[t, e]
        sums.append(total)
    for i in range(local_k):
        tile = jnp.concatenate([sums[c][i * half : (i + 1) * half] for c in range(2)], axis=0)
        for m in range(3):
            moved = pltpu.roll(tile, LANES - m * (LANES // 4), 1) if m else tile
            out_ref[i, m] = moved[:, :window]


def sum_kernel(own, pair, after, mine, theirs):
    core = my_core()
    for n, i, out in ((0, core, mine), (1, 1 - core, theirs)):
        out[...] = (own[i] + pair[n].astype(F32) + after[n].astype(F32)).astype(BF)


def join_kernel(mine, other, perm_ref, out_ref, mark_ref, halves):
    core = my_core()
    pairs = out_ref.shape[2]
    entries = out_ref.shape[3]
    half = pairs // 2
    halves[core] = mine[...].astype(F32)
    halves[1 - core] = other[...].astype(F32)
    parts = []
    for p in range(pairs):
        begin = entries * (p % half)
        parts.append(halves[p // half][:, begin : begin + entries])
    stacked = jnp.concatenate(parts, axis=0).astype(BF)
    mark_ref[...] = jnp.zeros(mark_ref.shape, F32)
    out_ref[...] = dot(perm_ref[...], stacked).astype(BF).reshape(out_ref.shape)


def body(green_less, green_greater, derivative, neighbours, phonon, *, mom, en):
    local_k, local_e, pairs, entries = green_less.shape
    momenta, window = phonon.shape[1], phonon.shape[2]
    atoms = derivative.shape[0]
    half = pairs // 2
    rows = local_k * local_e
    width = half * entries
    chips = mom // 2
    chip_k = 2 * local_k
    total_e = local_e * en
    size = NO * NO

    deriv = derivative.transpose(1, 0, 2)
    weights = phonon.transpose(0, 1, 3, 4, 2)
    g_own, b_own, g_far, b_far = call(
        pack_kernel,
        [shape((rows, width), BF)] * 4,
        [green_less, green_greater],
        1.5,
        [
            pltpu.VMEM(green_less.shape, BF),
            pltpu.VMEM(green_less.shape, BF),
            pltpu.VMEM((2, rows, width), F32),
            pltpu.SemaphoreType.DMA((2,)),
        ],
        [HBM] * 2,
        limit=53.25,
    )

    def move(value, dchip, dcore, to=lambda e: e):
        links = []
        for m in range(mom):
            target = ((m // 2 + dchip) % chips) * 2 + (m % 2 if dcore == 0 else 1 - m % 2)
            for e in range(en):
                links.append((m * en + e, target * en + to(e)))
        return lax.ppermute(value, ("mom", "en"), links)

    def onward(e):
        return (e + 1) % en

    def to_pair(e):
        return e ^ 1 if e ^ 1 < en else e

    def to_next(e):
        other = e + 1 if e % 2 else e - 1
        return other if 0 <= other < en else e

    blocks = [g_own, move(g_far, 0, 1)]
    for s in range(1, chips):
        blocks += [move(g_own, -s, 0), move(g_far, -s, 1)]
    b_core = move(b_far, 0, 1)
    prev_own = move(b_own, 0, 0, onward)
    prev_far = move(b_far, 0, 1, onward)

    near = neighbours.astype(jnp.int32)
    columns = -(-chip_k * 2 * local_e // LANES) * LANES
    k_hi, k_lo, toeplitz, to_energy, to_rows, turn, sort_e = call(
        functools.partial(table_kernel, half=half, local_k=local_k, local_e=local_e),
        [
            shape((6 * half, size, 2 * LANES), BF),
            shape((6 * half, size, 2 * LANES), BF),
            shape((3 * half, 3 * chip_k * local_e, 2 * LANES), BF),
            shape((momenta * local_e,) * 2, BF),
            shape((rows * pairs,) * 2, BF),
            shape((2 * half, 2 * LANES, 2 * LANES), BF),
            shape((columns, 2 * chip_k * local_e), BF),
        ],
        [near, deriv, weights],
        3,
        [
            pltpu.VMEM((3 * atoms, 32, 4 * LANES), F32),
            pltpu.VMEM((chip_k, 3, pairs, 4 * local_e * momenta), F32),
        ],
        [pl.BlockSpec(memory_space=pltpu.SMEM), VMEM, VMEM],
    )

    g1, g2, to_pair_rows, to_next_rows = call(
        functools.partial(product_kernel, half=half, entries=entries, chips=chips),
        [
            shape((3, momenta * local_e, width), BF),
            shape((3, momenta * local_e, width), BF),
            shape((2, rows, width), BF),
            shape((2, rows, width), BF),
        ],
        blocks + [to_energy, k_hi, k_lo, toeplitz],
        4,
        [pltpu.VMEM((2 * chips, rows, width), BF), pltpu.VMEM((4, rows, width), F32)],
    )
    from_pair = move(to_pair_rows, 0, 0, to_pair)
    from_next = move(to_next_rows, 0, 0, to_next)
    partial, done = call(
        functools.partial(
            polar_kernel, half=half, entries=entries, local_k=local_k, local_e=local_e,
            scale=1.0 / (NO * float(np.sqrt(momenta * total_e))),
        ),
        [shape((mom, en, local_k * half, LANES), F32), shape((8, LANES), F32)],
        [b_own, b_core, prev_own, prev_far, turn, sort_e, g1],
        3,
        [pltpu.VMEM((4, rows, width), BF)],
    )
    terms = lax.all_to_all(
        partial.reshape(mom * en, local_k * half, LANES), ("mom", "en"), split_axis=0, concat_axis=0, tiled=True
    )
    (own,) = call(
        functools.partial(own_kernel, entries=entries), [shape((2, rows, width), F32)], [toeplitz, g1, g2, done], 1
    )

    mine, theirs = call(
        sum_kernel, [shape((rows, width), BF)] * 2, [own, from_pair, from_next], 0.1
    )
    other = move(theirs, 0, 1)
    self_energy, mark = call(
        join_kernel,
        [shape(green_less.shape, BF), shape((8, LANES), F32)],
        [mine, other, to_rows],
        1,
        [pltpu.VMEM((2, rows, width), F32)],
    )
    (polar,) = call(
        functools.partial(total_kernel, half=half),
        [shape((local_k, 3, pairs, window), F32)],
        [terms.reshape(mom, en, local_k * half, LANES), mark],
        0.5,
    )
    polar = polar.transpose(0, 3, 1, 2)
    return (self_energy, polar)


def solution(mesh):
    return jax.shard_map(
        functools.partial(body, mom=mesh.shape["mom"], en=mesh.shape["en"]),
        mesh=mesh,
        in_specs=(P("mom", "en", None, None), P("mom", "en", None, None), P(), P(), P()),
        out_specs=(P("mom", "en", None, None), P("mom", None, None, None)),
        check_vma=False,
    )
```

```python
import functools

import jax
import jax.numpy as jnp
import numpy as np
from jax import lax
from jax.experimental import pallas as pl
from jax.experimental.pallas import tpu as pltpu
from jax.sharding import PartitionSpec as P

NO = 12
NB = 4
LANES = 128
BF = jnp.bfloat16
F32 = jnp.float32
HIGHEST = lax.Precision.HIGHEST
VMEM = pl.BlockSpec(memory_space=pltpu.VMEM)
HBM = pl.BlockSpec(memory_space=pltpu.HBM)
MIB = 1024 * 1024


def dot(a, b):
    return jnp.dot(a, b, preferred_element_type=F32)


def dot_t(a, b):
    return lax.dot_general(a, b, (((1,), (1,)), ((), ())), preferred_element_type=F32)


def call(kernel, outs, ins, work, scratch=(), specs=None, limit=12):
    return pl.pallas_call(
        kernel,
        out_shape=outs,
        in_specs=specs or [VMEM] * len(ins),
        out_specs=[VMEM] * len(outs),
        scratch_shapes=list(scratch),
        compiler_params=pltpu.CompilerParams(vmem_limit_bytes=int(limit * MIB)),
        cost_estimate=pl.CostEstimate(flops=int(work * 1e9), bytes_accessed=0, transcendentals=0),
    )(*ins)


def my_core():
    return lax.rem(lax.axis_index("mom"), 2).astype(jnp.int32)


def index(dims, axis):
    return lax.broadcasted_iota(jnp.int32, dims, axis)


def split(value, count):
    whole = jnp.floor((value.astype(F32) + 0.5) * (1.0 / count)).astype(jnp.int32)
    return whole, value - count * whole


def ones_at(condition):
    return condition.astype(F32).astype(BF)


def shape(dims, dtype):
    return jax.ShapeDtypeStruct(dims, dtype)


def pack_kernel(g_hbm, b_hbm, g_own, b_own, g_far, b_far, g_ref, b_ref, halves, sems):
    core = my_core()
    copies = []
    for i, (src, dst) in enumerate(((g_hbm, g_ref), (b_hbm, b_ref))):
        copies.append(pltpu.make_async_copy(src, dst, sems.at[i]))
        copies[-1].start()
    rows = g_own.shape[0]
    pairs = g_ref.shape[2]
    entries = g_ref.shape[3]
    half = pairs // 2
    dims = (rows, rows * pairs)
    gap = index(dims, 1) - pairs * index(dims, 0)
    perm = jnp.concatenate([ones_at(gap == p) for p in range(pairs)], axis=0)
    for copy, src, own, far in ((copies[0], g_ref, g_own, g_far), (copies[1], b_ref, b_own, b_far)):
        copy.wait()
        sorted_rows = dot(perm, src[...].reshape(rows * pairs, entries))
        for h in range(2):
            parts = [sorted_rows[(h * half + j) * rows : (h * half + j + 1) * rows] for j in range(half)]
            halves[h] = jnp.concatenate(parts, axis=1)
        own[...] = halves[core].astype(BF)
        far[...] = halves[1 - core].astype(BF)


def table_kernel(
    near_ref, deriv_ref, phonon_ref, hi_ref, lo_ref, t_ref, perm_ref, join_ref, turn_ref, sort_ref,
    factors, bases, *, half, local_k, local_e,
):
    core = my_core()
    _, momenta, _, pairs, window = phonon_ref.shape
    size = NO * NO
    chip_k = 2 * local_k
    dims = perm_ref.shape
    e, k = split(index(dims, 0), momenta)
    perm_ref[...] = ones_at(index(dims, 1) == k * local_e + e)
    dims = join_ref.shape
    row, p = split(index(dims, 0), pairs)
    join_ref[...] = ones_at(index(dims, 1) == p * (local_k * local_e) + row)
    dims = sort_ref.shape
    k, i = split(index(dims, 0), 2 * local_e)
    at = jnp.where(i < local_e, (chip_k + k) * local_e + local_e - 1 - i, k * local_e + 2 * local_e - 1 - i)
    sort_ref[...] = ones_at((index(dims, 1) == at) & (k < chip_k))
    dims = turn_ref.shape[1:]
    u, i = split(index(dims, 0), NO)
    turn = ((index(dims, 1) == i * NO + u) & (u < NO)).astype(F32)
    for j in range(2 * half):
        shift = size * j % LANES
        moved = pltpu.roll(pltpu.roll(turn, shift, 0), shift, 1) if shift else turn
        turn_ref[j] = (moved * (1.0 - 2.0 * (j % 2))).astype(BF)
    x = (size, 2 * LANES)
    outer, inner = split(index(x, 0), NO)
    lane_outer, lane_inner = split(index(x, 1), NO)
    pick_l = ones_at(outer == lane_outer)
    pick_r = ones_at((outer == lane_inner) & (lane_outer < NO))
    picks = jnp.concatenate([pick_l, pick_r], axis=1)
    x = (size, 32)
    outer, inner = split(index(x, 0), NO)
    slot = split(index(x, 1), 16)[1]
    rows_l = ones_at(outer == slot)
    rows_r = ones_at(inner == slot)
    x = (16, size)
    mask = (split(index(x, 1), NO)[1] == index(x, 0)).astype(F32)
    atoms = deriv_ref.shape[1]
    spread = []
    for m in range(3):
        for atom in range(atoms):
            spread.append(deriv_ref[m, atom : atom + 1, :] * mask)
    spread = jnp.concatenate(spread, axis=0)
    spread_hi = spread.astype(BF)
    spread_lo = (spread - spread_hi.astype(F32)).astype(BF)
    for i, part in enumerate((spread_hi, spread_lo)):
        rows = dot(part, picks)
        for n in range(3 * atoms):
            factors[n, 16 * i : 16 * i + 16] = rows[16 * n : 16 * n + 16]
    for p in range(half):
        pair = core * half + p
        atom = pair // NB
        other = near_ref[atom, pair % NB]
        for m in range(3):
            u = factors[m * atoms + atom][:, : 2 * LANES]
            v = factors[m * atoms + other][:, 2 * LANES :]
            for c in range(2):
                j = 2 * p + c
                shift = size * j % LANES
                uj = pltpu.roll(u, shift, 1) if shift else u
                vj = pltpu.roll(v, shift, 1) if shift else v
                kron = dot(rows_l, uj.astype(BF)) * dot(rows_r, vj.astype(BF))
                k_hi = kron.astype(BF)
                hi_ref[j * 3 + m] = k_hi
                lo_ref[j * 3 + m] = (kron - k_hi.astype(F32)).astype(BF)
    tiles = 3 * local_e // 8
    step = 8 * momenta
    first = momenta * (3 * local_e - 8)
    length = bases.shape[3]
    middle = 2 * local_e - 8
    dims = (window, length)
    lane = index(dims, 1)
    depth = index(dims, 0) + 1
    line = None
    for side in range(2):
        gap = lane - momenta * (middle + depth if side else middle - depth)
        for q in range(momenta):
            place = ones_at(gap == (-q) % momenta)
            weights = phonon_ref[side, q].astype(F32).reshape(3 * pairs, window).astype(BF)
            term = dot(weights, place)
            line = term if line is None else line + term
    lane = index((1, length), 1)
    k = split(lane, momenta)[1]
    for a in range(chip_k):
        moved = line
        if a:
            moved = jnp.where(k >= a, pltpu.roll(line, a, 1), pltpu.roll(line, length - momenta + a, 1))
        bases[a] = moved.reshape(3, pairs, length)
    for p in range(half):
        for m in range(3):
            grid = {}
            for a in range(chip_k):
                row = bases[a, m, pl.ds(core * half + p, 1), :]
                block = pltpu.roll(jnp.broadcast_to(row, (8, length)), 0, 1, stride=momenta, stride_axis=0)
                moved = {0: block}
                for t in range(tiles):
                    offset = first - step * t
                    part = offset % LANES
                    if part not in moved:
                        moved[part] = pltpu.roll(block, length - part, 1)
                    start = offset - part
                    grid[(t, a)] = moved[part][:, start : start + 2 * LANES]
            order = []
            per = local_e // 8
            for blk in (0, 2, 1):
                for a in range(chip_k):
                    order += [grid[(blk * per + i, a)] for i in range(per)]
            table = jnp.where(index((1, 2 * LANES), 1) < momenta * local_e, jnp.concatenate(order, axis=0), 0.0)
            t_ref[p, :, m * 2 * LANES : (m + 1) * 2 * LANES] = table.astype(BF)


def product_kernel(*refs, half, entries, chips):
    core = my_core()
    blocks = refs[: 2 * chips]
    perm_ref, hi_ref, lo_ref, t_ref = refs[2 * chips : 2 * chips + 4]
    terms_ref, pair_ref, next_ref, gathered, result = refs[2 * chips + 4 :]
    for s in range(chips):
        n = 2 * ((s - 1) % chips)
        gathered[2 * s + core] = blocks[n][...]
        gathered[2 * s + 1 - core] = blocks[n + 1][...]
    count, rows, width = gathered.shape
    depth = count * rows
    tiles = width // LANES
    g = dot(perm_ref[...], gathered[...].reshape(depth, width)).astype(BF)
    block_rows = hi_ref.shape[1]
    sums = [[None] * tiles for _ in range(3)]
    for j in range(2 * half):
        start = (entries // 2) * j // LANES * LANES
        shift = (entries // 2) * j - start
        lhs = g[:, start : start + 2 * LANES]
        lhs = jnp.concatenate([lhs, lhs], axis=1)
        above = [jnp.zeros((shift, 2 * LANES), BF)] if shift else []
        rest = 2 * LANES - shift - block_rows
        under = [jnp.zeros((rest, 2 * LANES), BF)] if rest else []
        for m in range(3):
            parts = above + [hi_ref[j * 3 + m]] + under + above + [lo_ref[j * 3 + m]] + under
            r = dot(lhs, jnp.concatenate(parts, axis=0))
            for i in range(2):
                tile = start // LANES + i
                piece = r[:, i * LANES : (i + 1) * LANES]
                sums[m][tile] = piece if sums[m][tile] is None else sums[m][tile] + piece
    spare = 2 * LANES - depth
    for m in range(3):
        for n in range(2):
            at = (3 * n + m) * 2 * LANES
            if spare:
                terms_ref[at + depth : at + 2 * LANES, :] = jnp.zeros((spare, width), BF)
        for i in range(tiles):
            high = sums[m][i].astype(BF)
            for n, part in enumerate((high, (sums[m][i] - high.astype(F32)).astype(BF))):
                at = (3 * n + m) * 2 * LANES
                terms_ref[at : at + depth, i * LANES : (i + 1) * LANES] = part
    correlate(t_ref, 0, 4, terms_ref, result, entries)
    place = lax.axis_index("en")
    odd = lax.rem(place, 2)
    below = jnp.where(place == 0, 0.0, 1.0)
    above = jnp.where(place == lax.axis_size("en") - 1, 0.0, 1.0)
    keep_pair = jnp.where(odd == 1, below, above)
    keep_next = jnp.where(odd == 1, above, below)
    for i, c in enumerate((core, 1 - core)):
        pair_ref[i] = (result[2 - 2 * odd + c] * keep_pair).astype(BF)
        next_ref[i] = (result[2 * odd + c] * keep_next).astype(BF)


def correlate(t_ref, begin_row, count, terms_ref, result, entries):
    _, rows, width = result.shape
    lane = index((1, LANES), 1)
    carried = None
    for p in range(width // entries):
        begin = entries * p
        first = begin // LANES
        last = (begin + entries - 1) // LANES
        t = t_ref[p, begin_row * rows : (begin_row + count) * rows, :]
        total = dot(jnp.concatenate([t, t], axis=1), terms_ref[:, first * LANES : (last + 1) * LANES])
        for i in range(first, last + 1):
            tile = total[:, (i - first) * LANES : (i - first + 1) * LANES]
            if i == first and begin % LANES:
                tile = jnp.where(lane < begin % LANES, carried, tile)
            if i == last and (begin + entries) % LANES:
                carried = tile
            else:
                for r in range(count):
                    result[r, :, i * LANES : (i + 1) * LANES] = tile[r * rows : (r + 1) * rows]


def own_kernel(t_ref, terms_ref, after_ref, own_ref, *, entries):
    correlate(t_ref, 4, 2, terms_ref, own_ref, entries)


def polar_kernel(b_own, b_far, prev_own, prev_far, turn_ref, sort_ref, terms_ref, out_ref, mark_ref, gathered, *, half, entries, momenta, local_k, local_e, scale):
    core = my_core()
    present = jnp.where(lax.axis_index("en") == 0, 0.0, 1.0)
    gathered[core] = (prev_own[...].astype(F32) * present).astype(BF)
    gathered[1 - core] = (prev_far[...].astype(F32) * present).astype(BF)
    gathered[2 + core] = b_own[...]
    gathered[3 - core] = b_far[...]
    count, rows, width = gathered.shape
    tiles = width // LANES
    b = dot(sort_ref[...], gathered[...].reshape(count * rows, width)).astype(BF)
    sums = [None] * tiles
    for j in range(2 * half):
        start = (entries // 2) * j // LANES * LANES
        r = dot(b[:, start : start + 2 * LANES], turn_ref[j])
        for i in range(2):
            tile = start // LANES + i
            piece = r[:, i * LANES : (i + 1) * LANES]
            sums[tile] = piece if sums[tile] is None else sums[tile] + piece
    chip_k = 2 * local_k
    group = 2 * local_e
    columns = sort_ref.shape[0]
    window = local_e
    depth = local_e * momenta
    lane = index((1, LANES), 1)
    mark_ref[...] = jnp.zeros(mark_ref.shape, F32)
    pieces = []
    for p in range(half):
        begin = entries * p
        first = begin // LANES
        last = (begin + entries - 1) // LANES
        parts = []
        for i in range(first, last + 1):
            tile = sums[i]
            if i == first and begin % LANES:
                tile = jnp.where(lane < begin % LANES, 0.0, tile)
            if i == last and (begin + entries) % LANES:
                tile = jnp.where(lane < (begin + entries) % LANES, tile, 0.0)
            parts.append(tile.astype(BF))
        rhs = jnp.concatenate(parts, axis=1)
        held = None
        for m in range(3):
            s = dot_t(terms_ref[m * 2 * LANES : m * 2 * LANES + depth, first * LANES : (last + 1) * LANES], rhs)
            acc = None
            for e in range(local_e):
                row = pltpu.roll(s[e * momenta : (e + 1) * momenta], columns - (local_e - e), 1)
                acc = row if acc is None else acc + row
            total = None
            for a in range(chip_k):
                piece = acc if a == 0 else pltpu.roll(acc, columns - group * a, 1)
                piece = piece[:, :LANES]
                if a:
                    piece = pltpu.roll(piece, momenta - a, 0)
                total = piece if total is None else total + piece
            total = jnp.where(lane < window, total * scale, 0.0)
            if m:
                total = pltpu.roll(total, m * (LANES // 4), 1)
            held = total if held is None else held + total
        pieces.append(held)
    targets, en = out_ref.shape[:2]
    for t in range(targets):
        tile = jnp.concatenate(
            [pieces[p][t * local_k + i : t * local_k + i + 1] for i in range(local_k) for p in range(half)], axis=0
        )
        for e in range(en):
            out_ref[t, e] = tile


def total_kernel(in_ref, after_ref, out_ref, *, half):
    targets, en = in_ref.shape[:2]
    local_k, _, _, window = out_ref.shape
    sums = []
    for c in range(2):
        total = None
        for t in range(c, targets, 2):
            for e in range(en):
                total = in_ref[t, e] if total is None else total + in_ref[t, e]
        sums.append(total)
    for i in range(local_k):
        tile = jnp.concatenate([sums[c][i * half : (i + 1) * half] for c in range(2)], axis=0)
        for m in range(3):
            moved = pltpu.roll(tile, LANES - m * (LANES // 4), 1) if m else tile
            out_ref[i, m] = moved[:, :window]


def sum_kernel(own, after, pair, mine, theirs):
    core = my_core()
    for n, i, out in ((0, core, mine), (1, 1 - core, theirs)):
        out[...] = (own[i] + pair[n].astype(F32) + after[n].astype(F32)).astype(BF)


def join_kernel(mine, other, perm_ref, out_ref, mark_ref, halves):
    core = my_core()
    pairs = out_ref.shape[2]
    entries = out_ref.shape[3]
    half = pairs // 2
    halves[core] = mine[...].astype(F32)
    halves[1 - core] = other[...].astype(F32)
    parts = []
    for p in range(pairs):
        begin = entries * (p % half)
        parts.append(halves[p // half][:, begin : begin + entries])
    stacked = jnp.concatenate(parts, axis=0).astype(BF)
    mark_ref[...] = jnp.zeros(mark_ref.shape, F32)
    out_ref[...] = dot(perm_ref[...], stacked).astype(BF).reshape(out_ref.shape)


def body(green_less, green_greater, derivative, neighbours, phonon, *, mom, en):
    local_k, local_e, pairs, entries = green_less.shape
    momenta, window = phonon.shape[1], phonon.shape[2]
    atoms = derivative.shape[0]
    half = pairs // 2
    rows = local_k * local_e
    width = half * entries
    chips = mom // 2
    chip_k = 2 * local_k
    total_e = local_e * en
    size = NO * NO

    deriv = derivative.transpose(1, 0, 2)
    weights = phonon.transpose(0, 1, 3, 4, 2)
    g_own, b_own, g_far, b_far = call(
        pack_kernel,
        [shape((rows, width), BF)] * 4,
        [green_less, green_greater],
        1.5,
        [
            pltpu.VMEM(green_less.shape, BF),
            pltpu.VMEM(green_less.shape, BF),
            pltpu.VMEM((2, rows, width), F32),
            pltpu.SemaphoreType.DMA((2,)),
        ],
        [HBM] * 2,
        limit=53.25,
    )

    def move(value, dchip, dcore, to=lambda e: e):
        links = []
        for m in range(mom):
            target = ((m // 2 + dchip) % chips) * 2 + (m % 2 if dcore == 0 else 1 - m % 2)
            for e in range(en):
                links.append((m * en + e, target * en + to(e)))
        return lax.ppermute(value, ("mom", "en"), links)

    def onward(e):
        return (e + 1) % en

    def to_pair(e):
        return e ^ 1 if e ^ 1 < en else e

    def to_next(e):
        other = e + 1 if e % 2 else e - 1
        return other if 0 <= other < en else e

    blocks = []
    for s in range(1, chips):
        blocks += [move(g_far, -s, 1), move(g_own, -s, 0)][::-1]
    blocks += [g_own, move(g_far, 0, 1)]
    b_core = move(b_far, 0, 1)
    prev_own = move(b_own, 0, 0, onward)
    prev_far = move(b_far, 0, 1, onward)

    near = neighbours.astype(jnp.int32)
    columns = -(-chip_k * 2 * local_e // LANES) * LANES
    k_hi, k_lo, toeplitz, to_energy, to_rows, turn, sort_e = call(
        functools.partial(table_kernel, half=half, local_k=local_k, local_e=local_e),
        [
            shape((6 * half, size, 2 * LANES), BF),
            shape((6 * half, size, 2 * LANES), BF),
            shape((half, 3 * chip_k * local_e, 6 * LANES), BF),
            shape((momenta * local_e,) * 2, BF),
            shape((rows * pairs,) * 2, BF),
            shape((2 * half, 2 * LANES, 2 * LANES), BF),
            shape((columns, 2 * chip_k * local_e), BF),
        ],
        [near, deriv, weights],
        3,
        [
            pltpu.VMEM((3 * atoms, 32, 4 * LANES), F32),
            pltpu.VMEM((chip_k, 3, pairs, 4 * local_e * momenta), F32),
        ],
        [pl.BlockSpec(memory_space=pltpu.SMEM), VMEM, VMEM],
    )

    source_terms, to_pair_rows, to_next_rows = call(
        functools.partial(product_kernel, half=half, entries=entries, chips=chips),
        [
            shape((12 * LANES, width), BF),
            shape((2, rows, width), BF),
            shape((2, rows, width), BF),
        ],
        blocks + [to_energy, k_hi, k_lo, toeplitz],
        4,
        [pltpu.VMEM((2 * chips, rows, width), BF), pltpu.VMEM((4, rows, width), F32)],
    )
    from_next = move(to_next_rows, 0, 0, to_next)
    from_pair = move(to_pair_rows, 0, 0, to_pair)
    partial, done = call(
        functools.partial(
            polar_kernel, half=half, entries=entries, momenta=momenta, local_k=local_k, local_e=local_e,
            scale=1.0 / (NO * float(np.sqrt(momenta * total_e))),
        ),
        [shape((mom, en, local_k * half, LANES), F32), shape((8, LANES), F32)],
        [b_own, b_core, prev_own, prev_far, turn, sort_e, source_terms],
        3,
        [pltpu.VMEM((4, rows, width), BF)],
    )
    terms = lax.all_to_all(
        partial.reshape(mom * en, local_k * half, LANES), ("mom", "en"), split_axis=0, concat_axis=0, tiled=True
    )
    (own,) = call(
        functools.partial(own_kernel, entries=entries), [shape((2, rows, width), F32)], [toeplitz, source_terms, done], 1
    )

    mine, theirs = call(
        sum_kernel, [shape((rows, width), BF)] * 2, [own, from_next, from_pair], 0.1
    )
    other = move(theirs, 0, 1)
    self_energy, mark = call(
        join_kernel,
        [shape(green_less.shape, BF), shape((8, LANES), F32)],
        [mine, other, to_rows],
        1,
        [pltpu.VMEM((2, rows, width), F32)],
    )
    (polar,) = call(
        functools.partial(total_kernel, half=half),
        [shape((local_k, 3, pairs, window), F32)],
        [terms.reshape(mom, en, local_k * half, LANES), mark],
        0.5,
    )
    polar = polar.transpose(0, 3, 1, 2)
    return (self_energy, polar)


def solution(mesh):
    return jax.shard_map(
        functools.partial(body, mom=mesh.shape["mom"], en=mesh.shape["en"]),
        mesh=mesh,
        in_specs=(P("mom", "en", None, None), P("mom", "en", None, None), P(), P(), P()),
        out_specs=(P("mom", "en", None, None), P("mom", None, None, None)),
        check_vma=False,
    )
```

```python
import functools

import jax
import jax.numpy as jnp
import numpy as np
from jax import lax
from jax.experimental import pallas as pl
from jax.experimental.pallas import tpu as pltpu
from jax.sharding import PartitionSpec as P

NO = 12
NB = 4
LANES = 128
BF = jnp.bfloat16
F32 = jnp.float32
HIGHEST = lax.Precision.HIGHEST
VMEM = pl.BlockSpec(memory_space=pltpu.VMEM)
HBM = pl.BlockSpec(memory_space=pltpu.HBM)
MIB = 1024 * 1024


def dot(a, b):
    return jnp.dot(a, b, preferred_element_type=F32)


def dot_t(a, b):
    return lax.dot_general(a, b, (((1,), (1,)), ((), ())), preferred_element_type=F32)


def call(kernel, outs, ins, work, scratch=(), specs=None, limit=24):
    return pl.pallas_call(
        kernel,
        out_shape=outs,
        in_specs=specs or [VMEM] * len(ins),
        out_specs=[VMEM] * len(outs),
        scratch_shapes=list(scratch),
        compiler_params=pltpu.CompilerParams(vmem_limit_bytes=int(limit * MIB)),
        cost_estimate=pl.CostEstimate(flops=int(work * 1e9), bytes_accessed=0, transcendentals=0),
    )(*ins)


def my_core():
    return lax.rem(lax.axis_index("mom"), 2).astype(jnp.int32)


def index(dims, axis):
    return lax.broadcasted_iota(jnp.int32, dims, axis)


def split(value, count):
    whole = jnp.floor((value.astype(F32) + 0.5) * (1.0 / count)).astype(jnp.int32)
    return whole, value - count * whole


def ones_at(condition):
    return condition.astype(F32).astype(BF)


def shape(dims, dtype):
    return jax.ShapeDtypeStruct(dims, dtype)


def pack_kernel(g_hbm, b_hbm, g_own, g_send, g_far, b_own, b_far, g_ref, b_ref, halves, sems):
    core = my_core()
    copies = []
    for i, (src, dst) in enumerate(((g_hbm, g_ref), (b_hbm, b_ref))):
        copies.append(pltpu.make_async_copy(src, dst, sems.at[i]))
        copies[-1].start()
    rows = g_own.shape[0]
    pairs = g_ref.shape[2]
    entries = g_ref.shape[3]
    half = pairs // 2
    dims = (rows, rows * pairs)
    gap = index(dims, 1) - pairs * index(dims, 0)
    perm = jnp.concatenate([ones_at(gap == p) for p in range(pairs)], axis=0)
    for copy, src, own, far in ((copies[0], g_ref, g_own, g_far), (copies[1], b_ref, b_own, b_far)):
        copy.wait()
        sorted_rows = dot(perm, src[...].reshape(rows * pairs, entries))
        for h in range(2):
            parts = [sorted_rows[(h * half + j) * rows : (h * half + j + 1) * rows] for j in range(half)]
            halves[h] = jnp.concatenate(parts, axis=1)
        own[...] = halves[core].astype(BF)
        far[...] = halves[1 - core].astype(BF)
    g_send[...] = g_own[...]


def pair_kernel(first_ref, second_ref, out_ref):
    out_ref[0] = first_ref[...]
    out_ref[1] = second_ref[...]


def table_kernel(
    near_ref, deriv_ref, phonon_ref, hi_ref, lo_ref, t_ref, perm_ref, join_ref, turn_ref, sort_ref,
    factors, bases, *, half, local_k, local_e,
):
    core = my_core()
    _, momenta, _, pairs, window = phonon_ref.shape
    size = NO * NO
    chip_k = 2 * local_k
    dims = perm_ref.shape
    e, k = split(index(dims, 0), momenta)
    perm_ref[...] = ones_at(index(dims, 1) == k * local_e + e)
    dims = join_ref.shape
    row, p = split(index(dims, 0), pairs)
    join_ref[...] = ones_at(index(dims, 1) == p * (local_k * local_e) + row)
    dims = sort_ref.shape
    k, i = split(index(dims, 0), 2 * local_e)
    at = jnp.where(i < local_e, (chip_k + k) * local_e + local_e - 1 - i, k * local_e + 2 * local_e - 1 - i)
    sort_ref[...] = ones_at((index(dims, 1) == at) & (k < chip_k))
    dims = turn_ref.shape[1:]
    u, i = split(index(dims, 0), NO)
    turn = ((index(dims, 1) == i * NO + u) & (u < NO)).astype(F32)
    for j in range(2 * half):
        shift = size * j % LANES
        moved = pltpu.roll(pltpu.roll(turn, shift, 0), shift, 1) if shift else turn
        turn_ref[j] = (moved * (1.0 - 2.0 * (j % 2))).astype(BF)
    x = (size, 2 * LANES)
    outer, inner = split(index(x, 0), NO)
    lane_outer, lane_inner = split(index(x, 1), NO)
    pick_l = ones_at(outer == lane_outer)
    pick_r = ones_at((outer == lane_inner) & (lane_outer < NO))
    picks = jnp.concatenate([pick_l, pick_r], axis=1)
    x = (size, 32)
    outer, inner = split(index(x, 0), NO)
    slot = split(index(x, 1), 16)[1]
    rows_l = ones_at(outer == slot)
    rows_r = ones_at(inner == slot)
    x = (16, size)
    mask = (split(index(x, 1), NO)[1] == index(x, 0)).astype(F32)
    atoms = deriv_ref.shape[1]
    spread = []
    for m in range(3):
        for atom in range(atoms):
            spread.append(deriv_ref[m, atom : atom + 1, :] * mask)
    spread = jnp.concatenate(spread, axis=0)
    spread_hi = spread.astype(BF)
    spread_lo = (spread - spread_hi.astype(F32)).astype(BF)
    for i, part in enumerate((spread_hi, spread_lo)):
        rows = dot(part, picks)
        for n in range(3 * atoms):
            factors[n, 16 * i : 16 * i + 16] = rows[16 * n : 16 * n + 16]
    for p in range(half):
        pair = core * half + p
        atom = pair // NB
        other = near_ref[atom, pair % NB]
        for m in range(3):
            u = factors[m * atoms + atom][:, : 2 * LANES]
            v = factors[m * atoms + other][:, 2 * LANES :]
            for c in range(2):
                j = 2 * p + c
                shift = size * j % LANES
                uj = pltpu.roll(u, shift, 1) if shift else u
                vj = pltpu.roll(v, shift, 1) if shift else v
                kron = dot(rows_l, uj.astype(BF)) * dot(rows_r, vj.astype(BF))
                k_hi = kron.astype(BF)
                hi_ref[j * 3 + m] = k_hi
                lo_ref[j * 3 + m] = (kron - k_hi.astype(F32)).astype(BF)
    tiles = 3 * local_e // 8
    step = 8 * momenta
    first = momenta * (3 * local_e - 8)
    length = bases.shape[3]
    middle = 2 * local_e - 8
    dims = (window, length)
    lane = index(dims, 1)
    depth = index(dims, 0) + 1
    line = None
    for side in range(2):
        gap = lane - momenta * (middle + depth if side else middle - depth)
        for q in range(momenta):
            place = ones_at(gap == (-q) % momenta)
            weights = phonon_ref[side, q].astype(F32).reshape(3 * pairs, window).astype(BF)
            term = dot(weights, place)
            line = term if line is None else line + term
    lane = index((1, length), 1)
    k = split(lane, momenta)[1]
    for a in range(chip_k):
        moved = line
        if a:
            moved = jnp.where(k >= a, pltpu.roll(line, a, 1), pltpu.roll(line, length - momenta + a, 1))
        bases[a] = moved.reshape(3, pairs, length)
    for p in range(half):
        for m in range(3):
            grid = {}
            for a in range(chip_k):
                row = bases[a, m, pl.ds(core * half + p, 1), :]
                block = pltpu.roll(jnp.broadcast_to(row, (8, length)), 0, 1, stride=momenta, stride_axis=0)
                moved = {0: block}
                for t in range(tiles):
                    offset = first - step * t
                    part = offset % LANES
                    if part not in moved:
                        moved[part] = pltpu.roll(block, length - part, 1)
                    start = offset - part
                    grid[(t, a)] = moved[part][:, start : start + 2 * LANES]
            order = []
            per = local_e // 8
            for blk in (0, 2, 1):
                for a in range(chip_k):
                    order += [grid[(blk * per + i, a)] for i in range(per)]
            table = jnp.where(index((1, 2 * LANES), 1) < momenta * local_e, jnp.concatenate(order, axis=0), 0.0)
            t_ref[p, :, m * 2 * LANES : (m + 1) * 2 * LANES] = table.astype(BF)


def product_kernel(*refs, half, entries, chips):
    core = my_core()
    blocks = refs[: 2 * chips]
    perm_ref, hi_ref, lo_ref, t_ref = refs[2 * chips : 2 * chips + 4]
    high_ref, own_ref, pair_ref, next_ref, gathered, terms_ref, result = refs[2 * chips + 5 :]
    for s in range(chips):
        n = 2 * ((s - 1) % chips)
        gathered[2 * s + core] = blocks[n][...]
        gathered[2 * s + 1 - core] = blocks[n + 1][...]
    count, rows, width = gathered.shape
    depth = count * rows
    tiles = width // LANES
    g = dot(perm_ref[...], gathered[...].reshape(depth, width)).astype(BF)
    block_rows = hi_ref.shape[1]
    sums = [[None] * tiles for _ in range(3)]
    for j in range(2 * half):
        start = (entries // 2) * j // LANES * LANES
        shift = (entries // 2) * j - start
        lhs = g[:, start : start + 2 * LANES]
        lhs = jnp.concatenate([lhs, lhs], axis=1)
        above = [jnp.zeros((shift, 2 * LANES), BF)] if shift else []
        rest = 2 * LANES - shift - block_rows
        under = [jnp.zeros((rest, 2 * LANES), BF)] if rest else []
        for m in range(3):
            parts = above + [hi_ref[j * 3 + m]] + under + above + [lo_ref[j * 3 + m]] + under
            r = dot(lhs, jnp.concatenate(parts, axis=0))
            for i in range(2):
                tile = start // LANES + i
                piece = r[:, i * LANES : (i + 1) * LANES]
                sums[m][tile] = piece if sums[m][tile] is None else sums[m][tile] + piece
    spare = 2 * LANES - depth
    for m in range(3):
        for n in range(2):
            at = (3 * n + m) * 2 * LANES
            if spare:
                terms_ref[at + depth : at + 2 * LANES, :] = jnp.zeros((spare, width), BF)
        for i in range(tiles):
            high = sums[m][i].astype(BF)
            high_ref[m, :, i * LANES : (i + 1) * LANES] = high
            for n, part in enumerate((high, (sums[m][i] - high.astype(F32)).astype(BF))):
                at = (3 * n + m) * 2 * LANES
                terms_ref[at : at + depth, i * LANES : (i + 1) * LANES] = part
    correlate(t_ref, terms_ref, result, entries)
    place = lax.axis_index("en")
    odd = lax.rem(place, 2)
    below = jnp.where(place == 0, 0.0, 1.0)
    above = jnp.where(place == lax.axis_size("en") - 1, 0.0, 1.0)
    keep_pair = jnp.where(odd == 1, below, above)
    keep_next = jnp.where(odd == 1, above, below)
    for i, c in enumerate((core, 1 - core)):
        pair_ref[i] = (result[2 - 2 * odd + c] * keep_pair).astype(BF)
        next_ref[i] = (result[2 * odd + c] * keep_next).astype(BF)
        own_ref[i] = result[4 + c]


def correlate(t_ref, terms_ref, result, entries):
    count, rows, width = result.shape
    lane = index((1, LANES), 1)
    carried = None
    for p in range(width // entries):
        begin = entries * p
        first = begin // LANES
        last = (begin + entries - 1) // LANES
        t = t_ref[p]
        total = dot(jnp.concatenate([t, t], axis=1), terms_ref[:, first * LANES : (last + 1) * LANES])
        for i in range(first, last + 1):
            tile = total[:, (i - first) * LANES : (i - first + 1) * LANES]
            if i == first and begin % LANES:
                tile = jnp.where(lane < begin % LANES, carried, tile)
            if i == last and (begin + entries) % LANES:
                carried = tile
            else:
                for r in range(count):
                    result[r, :, i * LANES : (i + 1) * LANES] = tile[r * rows : (r + 1) * rows]


def polar_kernel(b_ref, prev_ref, turn_ref, sort_ref, high_ref, out_ref, gathered, *, half, entries, momenta, local_k, local_e, scale):
    core = my_core()
    present = jnp.where(lax.axis_index("en") == 0, 0.0, 1.0)
    for i, c in enumerate((core, 1 - core)):
        gathered[c] = (prev_ref[i].astype(F32) * present).astype(BF)
        gathered[2 + c] = b_ref[i]
    count, rows, width = gathered.shape
    tiles = width // LANES
    b = dot(sort_ref[...], gathered[...].reshape(count * rows, width)).astype(BF)
    sums = [None] * tiles
    for j in range(2 * half):
        start = (entries // 2) * j // LANES * LANES
        r = dot(b[:, start : start + 2 * LANES], turn_ref[j])
        for i in range(2):
            tile = start // LANES + i
            piece = r[:, i * LANES : (i + 1) * LANES]
            sums[tile] = piece if sums[tile] is None else sums[tile] + piece
    chip_k = 2 * local_k
    group = 2 * local_e
    columns = sort_ref.shape[0]
    window = local_e
    lane = index((1, LANES), 1)
    pieces = []
    for p in range(half):
        begin = entries * p
        first = begin // LANES
        last = (begin + entries - 1) // LANES
        parts = []
        for i in range(first, last + 1):
            tile = sums[i]
            if i == first and begin % LANES:
                tile = jnp.where(lane < begin % LANES, 0.0, tile)
            if i == last and (begin + entries) % LANES:
                tile = jnp.where(lane < (begin + entries) % LANES, tile, 0.0)
            parts.append(tile.astype(BF))
        rhs = jnp.concatenate(parts, axis=1)
        held = None
        for m in range(3):
            s = dot_t(high_ref[m, :, first * LANES : (last + 1) * LANES], rhs)
            acc = None
            for e in range(local_e):
                row = pltpu.roll(s[e * momenta : (e + 1) * momenta], columns - (local_e - e), 1)
                acc = row if acc is None else acc + row
            total = None
            for a in range(chip_k):
                piece = acc if a == 0 else pltpu.roll(acc, columns - group * a, 1)
                piece = piece[:, :LANES]
                if a:
                    piece = pltpu.roll(piece, momenta - a, 0)
                total = piece if total is None else total + piece
            total = jnp.where(lane < window, total * scale, 0.0)
            if m:
                total = pltpu.roll(total, m * (LANES // 4), 1)
            held = total if held is None else held + total
        pieces.append(held)
    targets, en = out_ref.shape[:2]
    for t in range(targets):
        tile = jnp.concatenate(
            [pieces[p][t * local_k + i : t * local_k + i + 1] for i in range(local_k) for p in range(half)], axis=0
        )
        for e in range(en):
            out_ref[t, e] = tile


def total_kernel(in_ref, after_ref, out_ref, *, half):
    targets, en = in_ref.shape[:2]
    local_k, _, _, window = out_ref.shape
    sums = []
    for c in range(2):
        total = None
        for t in range(c, targets, 2):
            for e in range(en):
                total = in_ref[t, e] if total is None else total + in_ref[t, e]
        sums.append(total)
    for i in range(local_k):
        tile = jnp.concatenate([sums[c][i * half : (i + 1) * half] for c in range(2)], axis=0)
        for m in range(3):
            moved = pltpu.roll(tile, LANES - m * (LANES // 4), 1) if m else tile
            out_ref[i, m] = moved[:, :window]


def sum_kernel(own, after, pair, mine, theirs):
    for n, out in enumerate((mine, theirs)):
        out[...] = (own[n] + pair[n].astype(F32) + after[n].astype(F32)).astype(BF)


def join_kernel(mine, other, perm_ref, out_ref, mark_ref, halves):
    core = my_core()
    pairs = out_ref.shape[2]
    entries = out_ref.shape[3]
    half = pairs // 2
    halves[core] = mine[...].astype(F32)
    halves[1 - core] = other[...].astype(F32)
    parts = []
    for p in range(pairs):
        begin = entries * (p % half)
        parts.append(halves[p // half][:, begin : begin + entries])
    stacked = jnp.concatenate(parts, axis=0).astype(BF)
    mark_ref[...] = jnp.zeros(mark_ref.shape, F32)
    out_ref[...] = dot(perm_ref[...], stacked).astype(BF).reshape(out_ref.shape)


def body(green_less, green_greater, derivative, neighbours, phonon, *, mom, en):
    local_k, local_e, pairs, entries = green_less.shape
    momenta, window = phonon.shape[1], phonon.shape[2]
    atoms = derivative.shape[0]
    half = pairs // 2
    rows = local_k * local_e
    width = half * entries
    chips = mom // 2
    chip_k = 2 * local_k
    total_e = local_e * en
    size = NO * NO

    deriv = derivative.transpose(1, 0, 2)
    weights = phonon.transpose(0, 1, 3, 4, 2)
    g_own, g_send, g_far, b_own, b_far = call(
        pack_kernel,
        [shape((rows, width), BF)] * 5,
        [green_less, green_greater],
        1.5,
        [
            pltpu.VMEM(green_less.shape, BF),
            pltpu.VMEM(green_less.shape, BF),
            pltpu.VMEM((2, rows, width), F32),
            pltpu.SemaphoreType.DMA((2,)),
        ],
        [HBM] * 2,
        limit=53.2,
    )

    def move(value, dchip, dcore, to=lambda e: e):
        links = []
        for m in range(mom):
            target = ((m // 2 + dchip) % chips) * 2 + (m % 2 if dcore == 0 else 1 - m % 2)
            for e in range(en):
                links.append((m * en + e, target * en + to(e)))
        return lax.ppermute(value, ("mom", "en"), links)

    def onward(e):
        return (e + 1) % en

    def to_pair(e):
        return e ^ 1 if e ^ 1 < en else e

    def to_next(e):
        other = e + 1 if e % 2 else e - 1
        return other if 0 <= other < en else e

    blocks = []
    for s in range(1, chips):
        blocks += [move(g_far, -s, 1), move(g_send, -s, 0)][::-1]
    blocks += [g_own, move(g_far, 0, 1)]
    (b_both,) = call(pair_kernel, [shape((2, rows, width), BF)], [b_own, move(b_far, 0, 1)], 0.2)
    prev_both = move(b_both, 0, 0, onward)

    near = neighbours.astype(jnp.int32)
    columns = -(-chip_k * 2 * local_e // LANES) * LANES
    k_hi, k_lo, toeplitz, to_energy, to_rows, turn, sort_e = call(
        functools.partial(table_kernel, half=half, local_k=local_k, local_e=local_e),
        [
            shape((6 * half, size, 2 * LANES), BF),
            shape((6 * half, size, 2 * LANES), BF),
            shape((half, 3 * chip_k * local_e, 6 * LANES), BF),
            shape((momenta * local_e,) * 2, BF),
            shape((rows * pairs,) * 2, BF),
            shape((2 * half, 2 * LANES, 2 * LANES), BF),
            shape((columns, 2 * chip_k * local_e), BF),
        ],
        [near, deriv, weights],
        3,
        [
            pltpu.VMEM((3 * atoms, 32, 4 * LANES), F32),
            pltpu.VMEM((chip_k, 3, pairs, 4 * local_e * momenta), F32),
        ],
        [pl.BlockSpec(memory_space=pltpu.SMEM), VMEM, VMEM],
    )

    high, own, to_pair_rows, to_next_rows = call(
        functools.partial(product_kernel, half=half, entries=entries, chips=chips),
        [
            shape((3, momenta * local_e, width), BF),
            shape((2, rows, width), F32),
            shape((2, rows, width), BF),
            shape((2, rows, width), BF),
        ],
        blocks + [to_energy, k_hi, k_lo, toeplitz, prev_both],
        4,
        [
            pltpu.VMEM((2 * chips, rows, width), BF),
            pltpu.VMEM((12 * LANES, width), BF),
            pltpu.VMEM((6, rows, width), F32),
        ],
    )
    from_next = move(to_next_rows, 0, 0, to_next)
    from_pair = move(to_pair_rows, 0, 0, to_pair)
    (partial,) = call(
        functools.partial(
            polar_kernel, half=half, entries=entries, momenta=momenta, local_k=local_k, local_e=local_e,
            scale=1.0 / (NO * float(np.sqrt(momenta * total_e))),
        ),
        [shape((mom, en, local_k * half, LANES), F32)],
        [b_both, prev_both, turn, sort_e, high],
        3,
        [pltpu.VMEM((4, rows, width), BF)],
    )
    terms = lax.all_to_all(
        partial.reshape(mom * en, local_k * half, LANES), ("mom", "en"), split_axis=0, concat_axis=0, tiled=True
    )
    mine, theirs = call(
        sum_kernel, [shape((rows, width), BF)] * 2, [own, from_next, from_pair], 0.1
    )
    other = move(theirs, 0, 1)
    self_energy, mark = call(
        join_kernel,
        [shape(green_less.shape, BF), shape((8, LANES), F32)],
        [mine, other, to_rows],
        1,
        [pltpu.VMEM((2, rows, width), F32)],
    )
    (polar,) = call(
        functools.partial(total_kernel, half=half),
        [shape((local_k, 3, pairs, window), F32)],
        [terms.reshape(mom, en, local_k * half, LANES), mark],
        0.5,
    )
    polar = polar.transpose(0, 3, 1, 2)
    return (self_energy, polar)


def solution(mesh):
    return jax.shard_map(
        functools.partial(body, mom=mesh.shape["mom"], en=mesh.shape["en"]),
        mesh=mesh,
        in_specs=(P("mom", "en", None, None), P("mom", "en", None, None), P(), P(), P()),
        out_specs=(P("mom", "en", None, None), P("mom", None, None, None)),
        check_vma=False,
    )
```

```python
import functools

import jax
import jax.numpy as jnp
import numpy as np
from jax import lax
from jax.experimental import pallas as pl
from jax.experimental.pallas import tpu as pltpu
from jax.sharding import PartitionSpec as P

NO = 12
NB = 4
LANES = 128
BF = jnp.bfloat16
F32 = jnp.float32
HIGHEST = lax.Precision.HIGHEST
VMEM = pl.BlockSpec(memory_space=pltpu.VMEM)
HBM = pl.BlockSpec(memory_space=pltpu.HBM)
MIB = 1024 * 1024


def dot(a, b):
    return jnp.dot(a, b, preferred_element_type=F32)


def dot_t(a, b):
    return lax.dot_general(a, b, (((1,), (1,)), ((), ())), preferred_element_type=F32)


def call(kernel, outs, ins, work, scratch=(), specs=None, limit=24):
    return pl.pallas_call(
        kernel,
        out_shape=outs,
        in_specs=specs or [VMEM] * len(ins),
        out_specs=[VMEM] * len(outs),
        scratch_shapes=list(scratch),
        compiler_params=pltpu.CompilerParams(vmem_limit_bytes=int(limit * MIB)),
        cost_estimate=pl.CostEstimate(flops=int(work * 1e9), bytes_accessed=0, transcendentals=0),
    )(*ins)


def my_core():
    return lax.rem(lax.axis_index("mom"), 2).astype(jnp.int32)


def index(dims, axis):
    return lax.broadcasted_iota(jnp.int32, dims, axis)


def split(value, count):
    whole = jnp.floor((value.astype(F32) + 0.5) * (1.0 / count)).astype(jnp.int32)
    return whole, value - count * whole


def ones_at(condition):
    return condition.astype(F32).astype(BF)


def shape(dims, dtype):
    return jax.ShapeDtypeStruct(dims, dtype)


def pack_kernel(g_hbm, b_hbm, g_own, g_far, b_own, b_far, both_far, g_ref, b_ref, halves, sems):
    core = my_core()
    copies = []
    for i, (src, dst) in enumerate(((g_hbm, g_ref), (b_hbm, b_ref))):
        copies.append(pltpu.make_async_copy(src, dst, sems.at[i]))
        copies[-1].start()
    rows = g_own.shape[0]
    pairs = g_ref.shape[2]
    entries = g_ref.shape[3]
    half = pairs // 2
    dims = (rows, rows * pairs)
    gap = index(dims, 1) - pairs * index(dims, 0)
    perm = jnp.concatenate([ones_at(gap == p) for p in range(pairs)], axis=0)
    for copy, src, own, far in ((copies[0], g_ref, g_own, g_far), (copies[1], b_ref, b_own, b_far)):
        copy.wait()
        sorted_rows = dot(perm, src[...].reshape(rows * pairs, entries))
        for h in range(2):
            parts = [sorted_rows[(h * half + j) * rows : (h * half + j + 1) * rows] for j in range(half)]
            halves[h] = jnp.concatenate(parts, axis=1)
        own[...] = halves[core].astype(BF)
        far[...] = halves[1 - core].astype(BF)
    both_far[0] = g_far[...]
    both_far[1] = b_far[...]


def table_kernel(
    near_ref, deriv_ref, phonon_ref, hi_ref, lo_ref, t_ref, perm_ref, join_ref, turn_ref, sort_ref,
    factors, bases, *, half, local_k, local_e,
):
    core = my_core()
    _, momenta, _, pairs, window = phonon_ref.shape
    size = NO * NO
    chip_k = 2 * local_k
    dims = perm_ref.shape
    e, k = split(index(dims, 0), momenta)
    perm_ref[...] = ones_at(index(dims, 1) == k * local_e + e)
    dims = join_ref.shape
    row, p = split(index(dims, 0), pairs)
    join_ref[...] = ones_at(index(dims, 1) == p * (local_k * local_e) + row)
    dims = sort_ref.shape
    k, i = split(index(dims, 0), 2 * local_e)
    at = jnp.where(i < local_e, (chip_k + k) * local_e + local_e - 1 - i, k * local_e + 2 * local_e - 1 - i)
    sort_ref[...] = ones_at((index(dims, 1) == at) & (k < chip_k))
    dims = turn_ref.shape[1:]
    u, i = split(index(dims, 0), NO)
    turn = ((index(dims, 1) == i * NO + u) & (u < NO)).astype(F32)
    for j in range(2 * half):
        shift = size * j % LANES
        moved = pltpu.roll(pltpu.roll(turn, shift, 0), shift, 1) if shift else turn
        turn_ref[j] = (moved * (1.0 - 2.0 * (j % 2))).astype(BF)
    x = (size, 2 * LANES)
    outer, inner = split(index(x, 0), NO)
    lane_outer, lane_inner = split(index(x, 1), NO)
    pick_l = ones_at(outer == lane_outer)
    pick_r = ones_at((outer == lane_inner) & (lane_outer < NO))
    picks = jnp.concatenate([pick_l, pick_r], axis=1)
    x = (size, 32)
    outer, inner = split(index(x, 0), NO)
    slot = split(index(x, 1), 16)[1]
    rows_l = ones_at(outer == slot)
    rows_r = ones_at(inner == slot)
    x = (16, size)
    mask = (split(index(x, 1), NO)[1] == index(x, 0)).astype(F32)
    atoms = deriv_ref.shape[1]
    spread = []
    for m in range(3):
        for atom in range(atoms):
            spread.append(deriv_ref[m, atom : atom + 1, :] * mask)
    spread = jnp.concatenate(spread, axis=0)
    spread_hi = spread.astype(BF)
    spread_lo = (spread - spread_hi.astype(F32)).astype(BF)
    for i, part in enumerate((spread_hi, spread_lo)):
        rows = dot(part, picks)
        for n in range(3 * atoms):
            factors[n, 16 * i : 16 * i + 16] = rows[16 * n : 16 * n + 16]
    for p in range(half):
        pair = core * half + p
        atom = pair // NB
        other = near_ref[atom, pair % NB]
        for m in range(3):
            u = factors[m * atoms + atom][:, : 2 * LANES]
            v = factors[m * atoms + other][:, 2 * LANES :]
            for c in range(2):
                j = 2 * p + c
                shift = size * j % LANES
                uj = pltpu.roll(u, shift, 1) if shift else u
                vj = pltpu.roll(v, shift, 1) if shift else v
                kron = dot(rows_l, uj.astype(BF)) * dot(rows_r, vj.astype(BF))
                k_hi = kron.astype(BF)
                hi_ref[j * 3 + m] = k_hi
                lo_ref[j * 3 + m] = (kron - k_hi.astype(F32)).astype(BF)
    tiles = 3 * local_e // 8
    step = 8 * momenta
    first = momenta * (3 * local_e - 8)
    length = bases.shape[3]
    middle = 2 * local_e - 8
    dims = (window, length)
    lane = index(dims, 1)
    depth = index(dims, 0) + 1
    line = None
    for side in range(2):
        gap = lane - momenta * (middle + depth if side else middle - depth)
        for q in range(momenta):
            place = ones_at(gap == (-q) % momenta)
            weights = phonon_ref[side, q].astype(F32).reshape(3 * pairs, window).astype(BF)
            term = dot(weights, place)
            line = term if line is None else line + term
    lane = index((1, length), 1)
    k = split(lane, momenta)[1]
    for a in range(chip_k):
        moved = line
        if a:
            moved = jnp.where(k >= a, pltpu.roll(line, a, 1), pltpu.roll(line, length - momenta + a, 1))
        bases[a] = moved.reshape(3, pairs, length)
    for p in range(half):
        for m in range(3):
            grid = {}
            for a in range(chip_k):
                row = bases[a, m, pl.ds(core * half + p, 1), :]
                block = pltpu.roll(jnp.broadcast_to(row, (8, length)), 0, 1, stride=momenta, stride_axis=0)
                moved = {0: block}
                for t in range(tiles):
                    offset = first - step * t
                    part = offset % LANES
                    if part not in moved:
                        moved[part] = pltpu.roll(block, length - part, 1)
                    start = offset - part
                    grid[(t, a)] = moved[part][:, start : start + 2 * LANES]
            order = []
            per = local_e // 8
            for blk in (0, 2, 1):
                for a in range(chip_k):
                    order += [grid[(blk * per + i, a)] for i in range(per)]
            table = jnp.where(index((1, 2 * LANES), 1) < momenta * local_e, jnp.concatenate(order, axis=0), 0.0)
            t_ref[p, :, m * 2 * LANES : (m + 1) * 2 * LANES] = table.astype(BF)


def product_kernel(*refs, half, entries, chips):
    core = my_core()
    blocks = refs[: 2 * chips]
    perm_ref, hi_ref, lo_ref, t_ref = refs[2 * chips : 2 * chips + 4]
    high_ref, own_ref, low_ref, up_ref, gathered, terms_ref, result = refs[2 * chips + 4 :]
    for s in range(chips):
        n = 2 * ((s - 1) % chips)
        gathered[2 * s + core] = blocks[n][...]
        gathered[2 * s + 1 - core] = blocks[n + 1][...] if s else blocks[n + 1][0]
    count, rows, width = gathered.shape
    depth = count * rows
    tiles = width // LANES
    g = dot(perm_ref[...], gathered[...].reshape(depth, width)).astype(BF)
    block_rows = hi_ref.shape[1]
    sums = [[None] * tiles for _ in range(3)]
    for j in range(2 * half):
        start = (entries // 2) * j // LANES * LANES
        shift = (entries // 2) * j - start
        lhs = g[:, start : start + 2 * LANES]
        lhs = jnp.concatenate([lhs, lhs], axis=1)
        above = [jnp.zeros((shift, 2 * LANES), BF)] if shift else []
        rest = 2 * LANES - shift - block_rows
        under = [jnp.zeros((rest, 2 * LANES), BF)] if rest else []
        for m in range(3):
            parts = above + [hi_ref[j * 3 + m]] + under + above + [lo_ref[j * 3 + m]] + under
            r = dot(lhs, jnp.concatenate(parts, axis=0))
            for i in range(2):
                tile = start // LANES + i
                piece = r[:, i * LANES : (i + 1) * LANES]
                sums[m][tile] = piece if sums[m][tile] is None else sums[m][tile] + piece
    spare = 2 * LANES - depth
    for m in range(3):
        for n in range(2):
            at = (3 * n + m) * 2 * LANES
            if spare:
                terms_ref[at + depth : at + 2 * LANES, :] = jnp.zeros((spare, width), BF)
        for i in range(tiles):
            high = sums[m][i].astype(BF)
            high_ref[m, :, i * LANES : (i + 1) * LANES] = high
            for n, part in enumerate((high, (sums[m][i] - high.astype(F32)).astype(BF))):
                at = (3 * n + m) * 2 * LANES
                terms_ref[at : at + depth, i * LANES : (i + 1) * LANES] = part
    correlate(t_ref, terms_ref, result, entries)
    place = lax.axis_index("en")
    below = jnp.where(place == 0, 0.0, 1.0)
    above = jnp.where(place == lax.axis_size("en") - 1, 0.0, 1.0)
    for i, c in enumerate((core, 1 - core)):
        low_ref[i] = (result[c] * below).astype(BF)
        up_ref[i] = (result[2 + c] * above).astype(BF)
        own_ref[i] = result[4 + c]


def correlate(t_ref, terms_ref, result, entries):
    count, rows, width = result.shape
    lane = index((1, LANES), 1)
    carried = None
    for p in range(width // entries):
        begin = entries * p
        first = begin // LANES
        last = (begin + entries - 1) // LANES
        t = t_ref[p]
        total = dot(jnp.concatenate([t, t], axis=1), terms_ref[:, first * LANES : (last + 1) * LANES])
        for i in range(first, last + 1):
            tile = total[:, (i - first) * LANES : (i - first + 1) * LANES]
            if i == first and begin % LANES:
                tile = jnp.where(lane < begin % LANES, carried, tile)
            if i == last and (begin + entries) % LANES:
                carried = tile
            else:
                for r in range(count):
                    result[r, :, i * LANES : (i + 1) * LANES] = tile[r * rows : (r + 1) * rows]


def polar_kernel(b_own, both_core, prev_own, prev_far, turn_ref, sort_ref, high_ref, out_ref, gathered, *, half, entries, momenta, local_k, local_e, scale):
    core = my_core()
    present = jnp.where(lax.axis_index("en") == 0, 0.0, 1.0)
    gathered[core] = (prev_own[...].astype(F32) * present).astype(BF)
    gathered[1 - core] = (prev_far[...].astype(F32) * present).astype(BF)
    gathered[2 + core] = b_own[...]
    gathered[3 - core] = both_core[1]
    count, rows, width = gathered.shape
    tiles = width // LANES
    b = dot(sort_ref[...], gathered[...].reshape(count * rows, width)).astype(BF)
    sums = [None] * tiles
    for j in range(2 * half):
        start = (entries // 2) * j // LANES * LANES
        r = dot(b[:, start : start + 2 * LANES], turn_ref[j])
        for i in range(2):
            tile = start // LANES + i
            piece = r[:, i * LANES : (i + 1) * LANES]
            sums[tile] = piece if sums[tile] is None else sums[tile] + piece
    chip_k = 2 * local_k
    group = 2 * local_e
    columns = sort_ref.shape[0]
    window = local_e
    lane = index((1, LANES), 1)
    pieces = []
    for p in range(half):
        begin = entries * p
        first = begin // LANES
        last = (begin + entries - 1) // LANES
        parts = []
        for i in range(first, last + 1):
            tile = sums[i]
            if i == first and begin % LANES:
                tile = jnp.where(lane < begin % LANES, 0.0, tile)
            if i == last and (begin + entries) % LANES:
                tile = jnp.where(lane < (begin + entries) % LANES, tile, 0.0)
            parts.append(tile.astype(BF))
        rhs = jnp.concatenate(parts, axis=1)
        held = None
        for m in range(3):
            s = dot_t(high_ref[m, :, first * LANES : (last + 1) * LANES], rhs)
            acc = None
            for e in range(local_e):
                row = pltpu.roll(s[e * momenta : (e + 1) * momenta], columns - (local_e - e), 1)
                acc = row if acc is None else acc + row
            total = None
            for a in range(chip_k):
                piece = acc if a == 0 else pltpu.roll(acc, columns - group * a, 1)
                piece = piece[:, :LANES]
                if a:
                    piece = pltpu.roll(piece, momenta - a, 0)
                total = piece if total is None else total + piece
            total = jnp.where(lane < window, total * scale, 0.0)
            if m:
                total = pltpu.roll(total, m * (LANES // 4), 1)
            held = total if held is None else held + total
        pieces.append(held)
    targets, en = out_ref.shape[:2]
    for t in range(targets):
        tile = jnp.concatenate(
            [pieces[p][t * local_k + i : t * local_k + i + 1] for i in range(local_k) for p in range(half)], axis=0
        )
        for e in range(en):
            out_ref[t, e] = tile


def total_kernel(in_ref, after_ref, out_ref, *, half):
    targets, en = in_ref.shape[:2]
    local_k, _, _, window = out_ref.shape
    sums = []
    for c in range(2):
        total = None
        for t in range(c, targets, 2):
            for e in range(en):
                total = in_ref[t, e] if total is None else total + in_ref[t, e]
        sums.append(total)
    for i in range(local_k):
        tile = jnp.concatenate([sums[c][i * half : (i + 1) * half] for c in range(2)], axis=0)
        for m in range(3):
            moved = pltpu.roll(tile, LANES - m * (LANES // 4), 1) if m else tile
            out_ref[i, m] = moved[:, :window]


def sum_kernel(own, below, above, mine, theirs):
    for n, out in enumerate((mine, theirs)):
        out[...] = (own[n] + below[n].astype(F32) + above[n].astype(F32)).astype(BF)


def join_kernel(mine, other, perm_ref, out_ref, mark_ref, halves):
    core = my_core()
    pairs = out_ref.shape[2]
    entries = out_ref.shape[3]
    half = pairs // 2
    halves[core] = mine[...].astype(F32)
    halves[1 - core] = other[...].astype(F32)
    parts = []
    for p in range(pairs):
        begin = entries * (p % half)
        parts.append(halves[p // half][:, begin : begin + entries])
    stacked = jnp.concatenate(parts, axis=0).astype(BF)
    mark_ref[...] = jnp.zeros(mark_ref.shape, F32)
    out_ref[...] = dot(perm_ref[...], stacked).astype(BF).reshape(out_ref.shape)


def body(green_less, green_greater, derivative, neighbours, phonon, *, mom, en):
    local_k, local_e, pairs, entries = green_less.shape
    momenta, window = phonon.shape[1], phonon.shape[2]
    atoms = derivative.shape[0]
    half = pairs // 2
    rows = local_k * local_e
    width = half * entries
    chips = mom // 2
    chip_k = 2 * local_k
    total_e = local_e * en
    size = NO * NO

    deriv = derivative.transpose(1, 0, 2)
    weights = phonon.transpose(0, 1, 3, 4, 2)
    g_own, g_far, b_own, b_far, both_far = call(
        pack_kernel,
        [shape((rows, width), BF)] * 4 + [shape((2, rows, width), BF)],
        [green_less, green_greater],
        1.5,
        [
            pltpu.VMEM(green_less.shape, BF),
            pltpu.VMEM(green_less.shape, BF),
            pltpu.VMEM((2, rows, width), F32),
            pltpu.SemaphoreType.DMA((2,)),
        ],
        [HBM] * 2,
        limit=53.12,
    )

    def move(value, dchip, dcore, to=lambda e: e):
        links = []
        for m in range(mom):
            target = ((m // 2 + dchip) % chips) * 2 + (m % 2 if dcore == 0 else 1 - m % 2)
            for e in range(en):
                links.append((m * en + e, target * en + to(e)))
        return lax.ppermute(value, ("mom", "en"), links)

    def onward(e):
        return (e + 1) % en

    def back(e):
        return (e - 1) % en

    blocks = []
    for s in range(1, chips):
        blocks += [move(g_far, -s, 1), move(g_own, -s, 0)][::-1]
    both_core = move(both_far, 0, 1)
    blocks += [g_own, both_core]
    prev_far = move(b_far, 0, 1, onward)
    prev_own = move(b_own, 0, 0, onward)

    near = neighbours.astype(jnp.int32)
    columns = -(-chip_k * 2 * local_e // LANES) * LANES
    k_hi, k_lo, toeplitz, to_energy, to_rows, turn, sort_e = call(
        functools.partial(table_kernel, half=half, local_k=local_k, local_e=local_e),
        [
            shape((6 * half, size, 2 * LANES), BF),
            shape((6 * half, size, 2 * LANES), BF),
            shape((half, 3 * chip_k * local_e, 6 * LANES), BF),
            shape((momenta * local_e,) * 2, BF),
            shape((rows * pairs,) * 2, BF),
            shape((2 * half, 2 * LANES, 2 * LANES), BF),
            shape((columns, 2 * chip_k * local_e), BF),
        ],
        [near, deriv, weights],
        3,
        [
            pltpu.VMEM((3 * atoms, 32, 4 * LANES), F32),
            pltpu.VMEM((chip_k, 3, pairs, 4 * local_e * momenta), F32),
        ],
        [pl.BlockSpec(memory_space=pltpu.SMEM), VMEM, VMEM],
    )

    high, own, low, up = call(
        functools.partial(product_kernel, half=half, entries=entries, chips=chips),
        [
            shape((3, momenta * local_e, width), BF),
            shape((2, rows, width), F32),
            shape((2, rows, width), BF),
            shape((2, rows, width), BF),
        ],
        blocks + [to_energy, k_hi, k_lo, toeplitz],
        4,
        [
            pltpu.VMEM((2 * chips, rows, width), BF),
            pltpu.VMEM((12 * LANES, width), BF),
            pltpu.VMEM((6, rows, width), F32),
        ],
    )
    from_below = move(up, 0, 0, onward)
    from_above = move(low, 0, 0, back)
    (partial,) = call(
        functools.partial(
            polar_kernel, half=half, entries=entries, momenta=momenta, local_k=local_k, local_e=local_e,
            scale=1.0 / (NO * float(np.sqrt(momenta * total_e))),
        ),
        [shape((mom, en, local_k * half, LANES), F32)],
        [b_own, both_core, prev_own, prev_far, turn, sort_e, high],
        3,
        [pltpu.VMEM((4, rows, width), BF)],
    )
    terms = lax.all_to_all(
        partial.reshape(mom * en, local_k * half, LANES), ("mom", "en"), split_axis=0, concat_axis=0, tiled=True
    )
    mine, theirs = call(
        sum_kernel, [shape((rows, width), BF)] * 2, [own, from_below, from_above], 0.1
    )
    other = move(theirs, 0, 1)
    self_energy, mark = call(
        join_kernel,
        [shape(green_less.shape, BF), shape((8, LANES), F32)],
        [mine, other, to_rows],
        1,
        [pltpu.VMEM((2, rows, width), F32)],
    )
    (polar,) = call(
        functools.partial(total_kernel, half=half),
        [shape((local_k, 3, pairs, window), F32)],
        [terms.reshape(mom, en, local_k * half, LANES), mark],
        0.5,
    )
    polar = polar.transpose(0, 3, 1, 2)
    return (self_energy, polar)


def solution(mesh):
    return jax.shard_map(
        functools.partial(body, mom=mesh.shape["mom"], en=mesh.shape["en"]),
        mesh=mesh,
        in_specs=(P("mom", "en", None, None), P("mom", "en", None, None), P(), P(), P()),
        out_specs=(P("mom", "en", None, None), P("mom", None, None, None)),
        check_vma=False,
    )
```

```python
import functools

import jax
import jax.numpy as jnp
import numpy as np
from jax import lax
from jax.experimental import pallas as pl
from jax.experimental.pallas import tpu as pltpu
from jax.sharding import PartitionSpec as P

NO = 12
NB = 4
LANES = 128
BF = jnp.bfloat16
F32 = jnp.float32
HIGHEST = lax.Precision.HIGHEST
VMEM = pl.BlockSpec(memory_space=pltpu.VMEM)
HBM = pl.BlockSpec(memory_space=pltpu.HBM)
MIB = 1024 * 1024


def dot(a, b):
    return jnp.dot(a, b, preferred_element_type=F32)


def dot_t(a, b):
    return lax.dot_general(a, b, (((1,), (1,)), ((), ())), preferred_element_type=F32)


def call(kernel, outs, ins, work, scratch=(), specs=None, limit=24):
    return pl.pallas_call(
        kernel,
        out_shape=outs,
        in_specs=specs or [VMEM] * len(ins),
        out_specs=[VMEM] * len(outs),
        scratch_shapes=list(scratch),
        compiler_params=pltpu.CompilerParams(vmem_limit_bytes=int(limit * MIB)),
        cost_estimate=pl.CostEstimate(flops=int(work * 1e9), bytes_accessed=0, transcendentals=0),
    )(*ins)


def my_core():
    return lax.rem(lax.axis_index("mom"), 2).astype(jnp.int32)


def index(dims, axis):
    return lax.broadcasted_iota(jnp.int32, dims, axis)


def split(value, count):
    whole = jnp.floor((value.astype(F32) + 0.5) * (1.0 / count)).astype(jnp.int32)
    return whole, value - count * whole


def ones_at(condition):
    return condition.astype(F32).astype(BF)


def shape(dims, dtype):
    return jax.ShapeDtypeStruct(dims, dtype)


def pack_kernel(g_hbm, b_hbm, g_own, g_far, b_own, b_far, both_far, g_ref, b_ref, halves, sems):
    core = my_core()
    copies = []
    for i, (src, dst) in enumerate(((g_hbm, g_ref), (b_hbm, b_ref))):
        copies.append(pltpu.make_async_copy(src, dst, sems.at[i]))
        copies[-1].start()
    rows = g_own.shape[0]
    pairs = g_ref.shape[2]
    entries = g_ref.shape[3]
    half = pairs // 2
    dims = (rows, rows * pairs)
    gap = index(dims, 1) - pairs * index(dims, 0)
    perm = jnp.concatenate([ones_at(gap == p) for p in range(pairs)], axis=0)
    for copy, src, own, far in ((copies[0], g_ref, g_own, g_far), (copies[1], b_ref, b_own, b_far)):
        copy.wait()
        sorted_rows = dot(perm, src[...].reshape(rows * pairs, entries))
        for h in range(2):
            parts = [sorted_rows[(h * half + j) * rows : (h * half + j + 1) * rows] for j in range(half)]
            halves[h] = jnp.concatenate(parts, axis=1)
        own[...] = halves[core].astype(BF)
        far[...] = halves[1 - core].astype(BF)
    both_far[0] = g_far[...]
    both_far[1] = b_far[...]


def table_kernel(
    near_ref, deriv_ref, phonon_ref, hi_ref, lo_ref, t_ref, perm_ref, join_ref, turn_ref, sort_ref,
    factors, bases, *, half, local_k, local_e,
):
    core = my_core()
    _, momenta, _, pairs, window = phonon_ref.shape
    size = NO * NO
    chip_k = 2 * local_k
    dims = perm_ref.shape
    e, k = split(index(dims, 0), momenta)
    perm_ref[...] = ones_at(index(dims, 1) == k * local_e + e)
    dims = join_ref.shape
    row, p = split(index(dims, 0), pairs)
    join_ref[...] = ones_at(index(dims, 1) == p * (local_k * local_e) + row)
    dims = sort_ref.shape
    k, i = split(index(dims, 0), 2 * local_e)
    at = jnp.where(i < local_e, (chip_k + k) * local_e + local_e - 1 - i, k * local_e + 2 * local_e - 1 - i)
    sort_ref[...] = ones_at((index(dims, 1) == at) & (k < chip_k))
    dims = turn_ref.shape[1:]
    u, i = split(index(dims, 0), NO)
    turn = ((index(dims, 1) == i * NO + u) & (u < NO)).astype(F32)
    for j in range(2 * half):
        shift = size * j % LANES
        moved = pltpu.roll(pltpu.roll(turn, shift, 0), shift, 1) if shift else turn
        turn_ref[j] = (moved * (1.0 - 2.0 * (j % 2))).astype(BF)
    x = (size, 2 * LANES)
    outer, inner = split(index(x, 0), NO)
    lane_outer, lane_inner = split(index(x, 1), NO)
    pick_l = ones_at(outer == lane_outer)
    pick_r = ones_at((outer == lane_inner) & (lane_outer < NO))
    picks = jnp.concatenate([pick_l, pick_r], axis=1)
    x = (size, 32)
    outer, inner = split(index(x, 0), NO)
    slot = split(index(x, 1), 16)[1]
    rows_l = ones_at(outer == slot)
    rows_r = ones_at(inner == slot)
    x = (16, size)
    mask = (split(index(x, 1), NO)[1] == index(x, 0)).astype(F32)
    atoms = deriv_ref.shape[1]
    spread = []
    for m in range(3):
        for atom in range(atoms):
            spread.append(deriv_ref[m, atom : atom + 1, :] * mask)
    spread = jnp.concatenate(spread, axis=0)
    spread_hi = spread.astype(BF)
    spread_lo = (spread - spread_hi.astype(F32)).astype(BF)
    for i, part in enumerate((spread_hi, spread_lo)):
        rows = dot(part, picks)
        for n in range(3 * atoms):
            factors[n, 16 * i : 16 * i + 16] = rows[16 * n : 16 * n + 16]
    for p in range(half):
        pair = core * half + p
        atom = pair // NB
        other = near_ref[atom, pair % NB]
        for m in range(3):
            u = factors[m * atoms + atom][:, : 2 * LANES]
            v = factors[m * atoms + other][:, 2 * LANES :]
            for c in range(2):
                j = 2 * p + c
                shift = size * j % LANES
                uj = pltpu.roll(u, shift, 1) if shift else u
                vj = pltpu.roll(v, shift, 1) if shift else v
                kron = dot(rows_l, uj.astype(BF)) * dot(rows_r, vj.astype(BF))
                k_hi = kron.astype(BF)
                hi_ref[j * 3 + m] = k_hi
                lo_ref[j * 3 + m] = (kron - k_hi.astype(F32)).astype(BF)
    tiles = 3 * local_e // 8
    step = 8 * momenta
    first = momenta * (3 * local_e - 8)
    length = bases.shape[3]
    middle = 2 * local_e - 8
    dims = (window, length)
    lane = index(dims, 1)
    depth = index(dims, 0) + 1
    line = None
    for side in range(2):
        gap = lane - momenta * (middle + depth if side else middle - depth)
        for q in range(momenta):
            place = ones_at(gap == (-q) % momenta)
            weights = phonon_ref[side, q].astype(F32).reshape(3 * pairs, window).astype(BF)
            term = dot(weights, place)
            line = term if line is None else line + term
    lane = index((1, length), 1)
    k = split(lane, momenta)[1]
    for a in range(chip_k):
        moved = line
        if a:
            moved = jnp.where(k >= a, pltpu.roll(line, a, 1), pltpu.roll(line, length - momenta + a, 1))
        bases[a] = moved.reshape(3, pairs, length)
    for p in range(half):
        for m in range(3):
            grid = {}
            for a in range(chip_k):
                row = bases[a, m, pl.ds(core * half + p, 1), :]
                block = pltpu.roll(jnp.broadcast_to(row, (8, length)), 0, 1, stride=momenta, stride_axis=0)
                moved = {0: block}
                for t in range(tiles):
                    offset = first - step * t
                    part = offset % LANES
                    if part not in moved:
                        moved[part] = pltpu.roll(block, length - part, 1)
                    start = offset - part
                    grid[(t, a)] = moved[part][:, start : start + 2 * LANES]
            order = []
            per = local_e // 8
            for blk in (0, 2, 1):
                for a in range(chip_k):
                    order += [grid[(blk * per + i, a)] for i in range(per)]
            table = jnp.where(index((1, 2 * LANES), 1) < momenta * local_e, jnp.concatenate(order, axis=0), 0.0)
            t_ref[p, :, m * 2 * LANES : (m + 1) * 2 * LANES] = table.astype(BF)


def product_kernel(*refs, half, entries, chips):
    core = my_core()
    blocks = refs[: 2 * chips]
    perm_ref, hi_ref, lo_ref, t_ref = refs[2 * chips : 2 * chips + 4]
    high_ref, own_ref, low_ref, up_ref, gathered, terms_ref, result = refs[2 * chips + 4 :]
    for s in range(chips):
        n = 2 * ((s - 1) % chips)
        gathered[2 * s + core] = blocks[n][...]
        gathered[2 * s + 1 - core] = blocks[n + 1][...] if s else blocks[n + 1][0]
    count, rows, width = gathered.shape
    depth = count * rows
    tiles = width // LANES
    g = dot(perm_ref[...], gathered[...].reshape(depth, width)).astype(BF)
    block_rows = hi_ref.shape[1]
    sums = [[None] * tiles for _ in range(3)]
    for j in range(2 * half):
        start = (entries // 2) * j // LANES * LANES
        shift = (entries // 2) * j - start
        lhs = g[:, start : start + 2 * LANES]
        lhs = jnp.concatenate([lhs, lhs], axis=1)
        above = [jnp.zeros((shift, 2 * LANES), BF)] if shift else []
        rest = 2 * LANES - shift - block_rows
        under = [jnp.zeros((rest, 2 * LANES), BF)] if rest else []
        for m in range(3):
            parts = above + [hi_ref[j * 3 + m]] + under + above + [lo_ref[j * 3 + m]] + under
            r = dot(lhs, jnp.concatenate(parts, axis=0))
            for i in range(2):
                tile = start // LANES + i
                piece = r[:, i * LANES : (i + 1) * LANES]
                sums[m][tile] = piece if sums[m][tile] is None else sums[m][tile] + piece
    spare = 2 * LANES - depth
    for m in range(3):
        for n in range(2):
            at = (3 * n + m) * 2 * LANES
            if spare:
                terms_ref[at + depth : at + 2 * LANES, :] = jnp.zeros((spare, width), BF)
        for i in range(tiles):
            high = sums[m][i].astype(BF)
            high_ref[m, :, i * LANES : (i + 1) * LANES] = high
            for n, part in enumerate((high, (sums[m][i] - high.astype(F32)).astype(BF))):
                at = (3 * n + m) * 2 * LANES
                terms_ref[at : at + depth, i * LANES : (i + 1) * LANES] = part
    correlate(t_ref, terms_ref, result, entries)
    place = lax.axis_index("en")
    below = jnp.where(place == 0, 0.0, 1.0)
    above = jnp.where(place == lax.axis_size("en") - 1, 0.0, 1.0)
    for i, c in enumerate((core, 1 - core)):
        low_ref[i] = (result[c] * below).astype(BF)
        up_ref[i] = (result[2 + c] * above).astype(BF)
        own_ref[i] = result[4 + c]


def correlate(t_ref, terms_ref, result, entries):
    count, rows, width = result.shape
    lane = index((1, LANES), 1)
    carried = None
    for p in range(width // entries):
        begin = entries * p
        first = begin // LANES
        last = (begin + entries - 1) // LANES
        t = t_ref[p]
        total = dot(jnp.concatenate([t, t], axis=1), terms_ref[:, first * LANES : (last + 1) * LANES])
        for i in range(first, last + 1):
            tile = total[:, (i - first) * LANES : (i - first + 1) * LANES]
            if i == first and begin % LANES:
                tile = jnp.where(lane < begin % LANES, carried, tile)
            if i == last and (begin + entries) % LANES:
                carried = tile
            else:
                for r in range(count):
                    result[r, :, i * LANES : (i + 1) * LANES] = tile[r * rows : (r + 1) * rows]


def polar_kernel(b_own, both_core, prev_own, prev_far, turn_ref, sort_ref, high_ref, out_ref, mark_ref, gathered, *, half, entries, momenta, local_k, local_e, scale):
    mark_ref[...] = jnp.zeros(mark_ref.shape, F32)
    core = my_core()
    present = jnp.where(lax.axis_index("en") == 0, 0.0, 1.0)
    gathered[core] = (prev_own[...].astype(F32) * present).astype(BF)
    gathered[1 - core] = (prev_far[...].astype(F32) * present).astype(BF)
    gathered[2 + core] = b_own[...]
    gathered[3 - core] = both_core[1]
    count, rows, width = gathered.shape
    tiles = width // LANES
    b = dot(sort_ref[...], gathered[...].reshape(count * rows, width)).astype(BF)
    sums = [None] * tiles
    for j in range(2 * half):
        start = (entries // 2) * j // LANES * LANES
        r = dot(b[:, start : start + 2 * LANES], turn_ref[j])
        for i in range(2):
            tile = start // LANES + i
            piece = r[:, i * LANES : (i + 1) * LANES]
            sums[tile] = piece if sums[tile] is None else sums[tile] + piece
    chip_k = 2 * local_k
    group = 2 * local_e
    columns = sort_ref.shape[0]
    window = local_e
    lane = index((1, LANES), 1)
    pieces = []
    for p in range(half):
        begin = entries * p
        first = begin // LANES
        last = (begin + entries - 1) // LANES
        parts = []
        for i in range(first, last + 1):
            tile = sums[i]
            if i == first and begin % LANES:
                tile = jnp.where(lane < begin % LANES, 0.0, tile)
            if i == last and (begin + entries) % LANES:
                tile = jnp.where(lane < (begin + entries) % LANES, tile, 0.0)
            parts.append(tile.astype(BF))
        rhs = jnp.concatenate(parts, axis=1)
        held = None
        for m in range(3):
            s = dot_t(high_ref[m, :, first * LANES : (last + 1) * LANES], rhs)
            acc = None
            for e in range(local_e):
                row = pltpu.roll(s[e * momenta : (e + 1) * momenta], columns - (local_e - e), 1)
                acc = row if acc is None else acc + row
            total = None
            for a in range(chip_k):
                piece = acc if a == 0 else pltpu.roll(acc, columns - group * a, 1)
                piece = piece[:, :LANES]
                if a:
                    piece = pltpu.roll(piece, momenta - a, 0)
                total = piece if total is None else total + piece
            total = jnp.where(lane < window, total * scale, 0.0)
            if m:
                total = pltpu.roll(total, m * (LANES // 4), 1)
            held = total if held is None else held + total
        pieces.append(held)
    targets, en = out_ref.shape[:2]
    for t in range(targets):
        tile = jnp.concatenate(
            [pieces[p][t * local_k + i : t * local_k + i + 1] for i in range(local_k) for p in range(half)], axis=0
        )
        for e in range(en):
            out_ref[t, e] = tile


def total_kernel(in_ref, out_ref, *, half):
    targets, en = in_ref.shape[:2]
    local_k, _, _, window = out_ref.shape
    sums = []
    for c in range(2):
        total = None
        for t in range(c, targets, 2):
            for e in range(en):
                total = in_ref[t, e] if total is None else total + in_ref[t, e]
        sums.append(total)
    for i in range(local_k):
        tile = jnp.concatenate([sums[c][i * half : (i + 1) * half] for c in range(2)], axis=0)
        for m in range(3):
            moved = pltpu.roll(tile, LANES - m * (LANES // 4), 1) if m else tile
            out_ref[i, m] = moved[:, :window]


def first_kernel(own, below, low, mark_ref, sum_ref, low_ref):
    sum_ref[...] = own[...] + below[...].astype(F32)
    low_ref[...] = low[...]


def sum_kernel(own, above, mine, theirs):
    for n, out in enumerate((mine, theirs)):
        out[...] = (own[n] + above[n].astype(F32)).astype(BF)


def join_kernel(mine, other, perm_ref, out_ref, halves):
    core = my_core()
    pairs = out_ref.shape[2]
    entries = out_ref.shape[3]
    half = pairs // 2
    halves[core] = mine[...].astype(F32)
    halves[1 - core] = other[...].astype(F32)
    parts = []
    for p in range(pairs):
        begin = entries * (p % half)
        parts.append(halves[p // half][:, begin : begin + entries])
    stacked = jnp.concatenate(parts, axis=0).astype(BF)
    out_ref[...] = dot(perm_ref[...], stacked).astype(BF).reshape(out_ref.shape)


def body(green_less, green_greater, derivative, neighbours, phonon, *, mom, en):
    local_k, local_e, pairs, entries = green_less.shape
    momenta, window = phonon.shape[1], phonon.shape[2]
    atoms = derivative.shape[0]
    half = pairs // 2
    rows = local_k * local_e
    width = half * entries
    chips = mom // 2
    chip_k = 2 * local_k
    total_e = local_e * en
    size = NO * NO

    deriv = derivative.transpose(1, 0, 2)
    weights = phonon.transpose(0, 1, 3, 4, 2)
    g_own, g_far, b_own, b_far, both_far = call(
        pack_kernel,
        [shape((rows, width), BF)] * 4 + [shape((2, rows, width), BF)],
        [green_less, green_greater],
        1.5,
        [
            pltpu.VMEM(green_less.shape, BF),
            pltpu.VMEM(green_less.shape, BF),
            pltpu.VMEM((2, rows, width), F32),
            pltpu.SemaphoreType.DMA((2,)),
        ],
        [HBM] * 2,
        limit=53.12,
    )

    def move(value, dchip, dcore, to=lambda e: e):
        links = []
        for m in range(mom):
            target = ((m // 2 + dchip) % chips) * 2 + (m % 2 if dcore == 0 else 1 - m % 2)
            for e in range(en):
                links.append((m * en + e, target * en + to(e)))
        return lax.ppermute(value, ("mom", "en"), links)

    def onward(e):
        return (e + 1) % en

    def back(e):
        return (e - 1) % en

    blocks = []
    for s in range(1, chips):
        blocks += [move(g_far, -s, 1), move(g_own, -s, 0)][::-1]
    both_core = move(both_far, 0, 1)
    blocks += [g_own, both_core]
    prev_far = move(b_far, 0, 1, onward)
    prev_own = move(b_own, 0, 0, onward)

    near = neighbours.astype(jnp.int32)
    columns = -(-chip_k * 2 * local_e // LANES) * LANES
    k_hi, k_lo, toeplitz, to_energy, to_rows, turn, sort_e = call(
        functools.partial(table_kernel, half=half, local_k=local_k, local_e=local_e),
        [
            shape((6 * half, size, 2 * LANES), BF),
            shape((6 * half, size, 2 * LANES), BF),
            shape((half, 3 * chip_k * local_e, 6 * LANES), BF),
            shape((momenta * local_e,) * 2, BF),
            shape((rows * pairs,) * 2, BF),
            shape((2 * half, 2 * LANES, 2 * LANES), BF),
            shape((columns, 2 * chip_k * local_e), BF),
        ],
        [near, deriv, weights],
        3,
        [
            pltpu.VMEM((3 * atoms, 32, 4 * LANES), F32),
            pltpu.VMEM((chip_k, 3, pairs, 4 * local_e * momenta), F32),
        ],
        [pl.BlockSpec(memory_space=pltpu.SMEM), VMEM, VMEM],
    )

    high, own, low, up = call(
        functools.partial(product_kernel, half=half, entries=entries, chips=chips),
        [
            shape((3, momenta * local_e, width), BF),
            shape((2, rows, width), F32),
            shape((2, rows, width), BF),
            shape((2, rows, width), BF),
        ],
        blocks + [to_energy, k_hi, k_lo, toeplitz],
        4,
        [
            pltpu.VMEM((2 * chips, rows, width), BF),
            pltpu.VMEM((12 * LANES, width), BF),
            pltpu.VMEM((6, rows, width), F32),
        ],
    )
    from_below = move(up, 0, 0, onward)
    partial, done = call(
        functools.partial(
            polar_kernel, half=half, entries=entries, momenta=momenta, local_k=local_k, local_e=local_e,
            scale=1.0 / (NO * float(np.sqrt(momenta * total_e))),
        ),
        [shape((mom, en, local_k * half, LANES), F32), shape((8, LANES), F32)],
        [b_own, both_core, prev_own, prev_far, turn, sort_e, high],
        3,
        [pltpu.VMEM((4, rows, width), BF)],
    )
    terms = lax.all_to_all(
        partial.reshape(mom * en, local_k * half, LANES), ("mom", "en"), split_axis=0, concat_axis=0, tiled=True
    )
    own, low = call(
        first_kernel, [shape((2, rows, width), F32), shape(low.shape, BF)], [own, from_below, low, done], 0.2
    )
    from_above = move(low, 0, 0, back)
    mine, theirs = call(
        sum_kernel, [shape((rows, width), BF)] * 2, [own, from_above], 0.1
    )
    other = move(theirs, 0, 1)
    (self_energy,) = call(
        join_kernel,
        [shape(green_less.shape, BF)],
        [mine, other, to_rows],
        1,
        [pltpu.VMEM((2, rows, width), F32)],
    )
    (polar,) = call(
        functools.partial(total_kernel, half=half),
        [shape((local_k, 3, pairs, window), F32)],
        [terms.reshape(mom, en, local_k * half, LANES)],
        0.5,
    )
    polar = polar.transpose(0, 3, 1, 2)
    return (self_energy, polar)


def solution(mesh):
    return jax.shard_map(
        functools.partial(body, mom=mesh.shape["mom"], en=mesh.shape["en"]),
        mesh=mesh,
        in_specs=(P("mom", "en", None, None), P("mom", "en", None, None), P(), P(), P()),
        out_specs=(P("mom", "en", None, None), P("mom", None, None, None)),
        check_vma=False,
    )
```

```python
import functools

import jax
import jax.numpy as jnp
import numpy as np
from jax import lax
from jax.experimental import pallas as pl
from jax.experimental.pallas import tpu as pltpu
from jax.sharding import PartitionSpec as P

NO = 12
NB = 4
LANES = 128
BF = jnp.bfloat16
F32 = jnp.float32
HIGHEST = lax.Precision.HIGHEST
VMEM = pl.BlockSpec(memory_space=pltpu.VMEM)
HBM = pl.BlockSpec(memory_space=pltpu.HBM)
MIB = 1024 * 1024


def dot(a, b):
    return jnp.dot(a, b, preferred_element_type=F32)


def dot_t(a, b):
    return lax.dot_general(a, b, (((1,), (1,)), ((), ())), preferred_element_type=F32)


def call(kernel, outs, ins, work, scratch=(), specs=None, limit=24):
    return pl.pallas_call(
        kernel,
        out_shape=outs,
        in_specs=specs or [VMEM] * len(ins),
        out_specs=[VMEM] * len(outs),
        scratch_shapes=list(scratch),
        compiler_params=pltpu.CompilerParams(vmem_limit_bytes=int(limit * MIB)),
        cost_estimate=pl.CostEstimate(flops=int(work * 1e9), bytes_accessed=0, transcendentals=0),
    )(*ins)


def my_core():
    return lax.rem(lax.axis_index("mom"), 2).astype(jnp.int32)


def index(dims, axis):
    return lax.broadcasted_iota(jnp.int32, dims, axis)


def split(value, count):
    whole = jnp.floor((value.astype(F32) + 0.5) * (1.0 / count)).astype(jnp.int32)
    return whole, value - count * whole


def ones_at(condition):
    return condition.astype(F32).astype(BF)


def shape(dims, dtype):
    return jax.ShapeDtypeStruct(dims, dtype)


def pack_kernel(g_hbm, b_hbm, g_own, g_far, b_own, b_far, both_far, g_ref, b_ref, halves, sems):
    core = my_core()
    copies = []
    for i, (src, dst) in enumerate(((g_hbm, g_ref), (b_hbm, b_ref))):
        copies.append(pltpu.make_async_copy(src, dst, sems.at[i]))
        copies[-1].start()
    rows = g_own.shape[0]
    pairs = g_ref.shape[2]
    entries = g_ref.shape[3]
    half = pairs // 2
    dims = (rows, rows * pairs)
    gap = index(dims, 1) - pairs * index(dims, 0)
    perm = jnp.concatenate([ones_at(gap == p) for p in range(pairs)], axis=0)
    for copy, src, own, far in ((copies[0], g_ref, g_own, g_far), (copies[1], b_ref, b_own, b_far)):
        copy.wait()
        sorted_rows = dot(perm, src[...].reshape(rows * pairs, entries))
        for h in range(2):
            parts = [sorted_rows[(h * half + j) * rows : (h * half + j + 1) * rows] for j in range(half)]
            halves[h] = jnp.concatenate(parts, axis=1)
        own[...] = halves[core].astype(BF)
        far[...] = halves[1 - core].astype(BF)
    both_far[0] = g_far[...]
    both_far[1] = b_far[...]


def table_kernel(
    near_ref, deriv_ref, phonon_ref, hi_ref, lo_ref, t_ref, perm_ref, join_ref, turn_ref, sort_ref,
    factors, bases, *, half, local_k, local_e,
):
    core = my_core()
    _, momenta, _, pairs, window = phonon_ref.shape
    size = NO * NO
    chip_k = 2 * local_k
    dims = perm_ref.shape
    e, k = split(index(dims, 0), momenta)
    perm_ref[...] = ones_at(index(dims, 1) == k * local_e + e)
    dims = join_ref.shape
    row, p = split(index(dims, 0), pairs)
    join_ref[...] = ones_at(index(dims, 1) == p * (local_k * local_e) + row)
    dims = sort_ref.shape
    k, i = split(index(dims, 0), 2 * local_e)
    at = jnp.where(i < local_e, (chip_k + k) * local_e + local_e - 1 - i, k * local_e + 2 * local_e - 1 - i)
    sort_ref[...] = ones_at((index(dims, 1) == at) & (k < chip_k))
    dims = turn_ref.shape[1:]
    u, i = split(index(dims, 0), NO)
    turn = ((index(dims, 1) == i * NO + u) & (u < NO)).astype(F32)
    for j in range(2 * half):
        shift = size * j % LANES
        moved = pltpu.roll(pltpu.roll(turn, shift, 0), shift, 1) if shift else turn
        turn_ref[j] = (moved * (1.0 - 2.0 * (j % 2))).astype(BF)
    x = (size, 2 * LANES)
    outer, inner = split(index(x, 0), NO)
    lane_outer, lane_inner = split(index(x, 1), NO)
    pick_l = ones_at(outer == lane_outer)
    pick_r = ones_at((outer == lane_inner) & (lane_outer < NO))
    picks = jnp.concatenate([pick_l, pick_r], axis=1)
    x = (size, 32)
    outer, inner = split(index(x, 0), NO)
    slot = split(index(x, 1), 16)[1]
    rows_l = ones_at(outer == slot)
    rows_r = ones_at(inner == slot)
    x = (16, size)
    mask = (split(index(x, 1), NO)[1] == index(x, 0)).astype(F32)
    atoms = deriv_ref.shape[1]
    spread = []
    for m in range(3):
        for atom in range(atoms):
            spread.append(deriv_ref[m, atom : atom + 1, :] * mask)
    spread = jnp.concatenate(spread, axis=0)
    spread_hi = spread.astype(BF)
    spread_lo = (spread - spread_hi.astype(F32)).astype(BF)
    for i, part in enumerate((spread_hi, spread_lo)):
        rows = dot(part, picks)
        for n in range(3 * atoms):
            factors[n, 16 * i : 16 * i + 16] = rows[16 * n : 16 * n + 16]
    for p in range(half):
        pair = core * half + p
        atom = pair // NB
        other = near_ref[atom, pair % NB]
        for m in range(3):
            u = factors[m * atoms + atom][:, : 2 * LANES]
            v = factors[m * atoms + other][:, 2 * LANES :]
            for c in range(2):
                j = 2 * p + c
                shift = size * j % LANES
                uj = pltpu.roll(u, shift, 1) if shift else u
                vj = pltpu.roll(v, shift, 1) if shift else v
                kron = dot(rows_l, uj.astype(BF)) * dot(rows_r, vj.astype(BF))
                k_hi = kron.astype(BF)
                hi_ref[j * 3 + m] = k_hi
                lo_ref[j * 3 + m] = (kron - k_hi.astype(F32)).astype(BF)
    tiles = 3 * local_e // 8
    step = 8 * momenta
    first = momenta * (3 * local_e - 8)
    length = bases.shape[3]
    middle = 2 * local_e - 8
    dims = (window, length)
    lane = index(dims, 1)
    depth = index(dims, 0) + 1
    line = None
    for side in range(2):
        gap = lane - momenta * (middle + depth if side else middle - depth)
        for q in range(momenta):
            place = ones_at(gap == (-q) % momenta)
            weights = phonon_ref[side, q].astype(F32).reshape(3 * pairs, window).astype(BF)
            term = dot(weights, place)
            line = term if line is None else line + term
    lane = index((1, length), 1)
    k = split(lane, momenta)[1]
    for a in range(chip_k):
        moved = line
        if a:
            moved = jnp.where(k >= a, pltpu.roll(line, a, 1), pltpu.roll(line, length - momenta + a, 1))
        bases[a] = moved.reshape(3, pairs, length)
    for p in range(half):
        for m in range(3):
            grid = {}
            for a in range(chip_k):
                row = bases[a, m, pl.ds(core * half + p, 1), :]
                block = pltpu.roll(jnp.broadcast_to(row, (8, length)), 0, 1, stride=momenta, stride_axis=0)
                moved = {0: block}
                for t in range(tiles):
                    offset = first - step * t
                    part = offset % LANES
                    if part not in moved:
                        moved[part] = pltpu.roll(block, length - part, 1)
                    start = offset - part
                    grid[(t, a)] = moved[part][:, start : start + 2 * LANES]
            order = []
            per = local_e // 8
            for blk in (0, 2, 1):
                for a in range(chip_k):
                    order += [grid[(blk * per + i, a)] for i in range(per)]
            table = jnp.where(index((1, 2 * LANES), 1) < momenta * local_e, jnp.concatenate(order, axis=0), 0.0)
            t_ref[p, :, m * 2 * LANES : (m + 1) * 2 * LANES] = table.astype(BF)


def product_kernel(*refs, half, entries, chips):
    core = my_core()
    blocks = refs[: 2 * chips]
    perm_ref, hi_ref, lo_ref, t_ref = refs[2 * chips : 2 * chips + 4]
    high_ref, own_ref, far_ref, pair_ref, gathered, terms_ref, result = refs[2 * chips + 4 :]
    for s in range(chips):
        n = 2 * ((s - 1) % chips)
        gathered[2 * s + core] = blocks[n][...]
        gathered[2 * s + 1 - core] = blocks[n + 1][...] if s else blocks[n + 1][0]
    count, rows, width = gathered.shape
    depth = count * rows
    tiles = width // LANES
    g = dot(perm_ref[...], gathered[...].reshape(depth, width)).astype(BF)
    block_rows = hi_ref.shape[1]
    sums = [[None] * tiles for _ in range(3)]
    for j in range(2 * half):
        start = (entries // 2) * j // LANES * LANES
        shift = (entries // 2) * j - start
        lhs = g[:, start : start + 2 * LANES]
        lhs = jnp.concatenate([lhs, lhs], axis=1)
        above = [jnp.zeros((shift, 2 * LANES), BF)] if shift else []
        rest = 2 * LANES - shift - block_rows
        under = [jnp.zeros((rest, 2 * LANES), BF)] if rest else []
        for m in range(3):
            parts = above + [hi_ref[j * 3 + m]] + under + above + [lo_ref[j * 3 + m]] + under
            r = dot(lhs, jnp.concatenate(parts, axis=0))
            for i in range(2):
                tile = start // LANES + i
                piece = r[:, i * LANES : (i + 1) * LANES]
                sums[m][tile] = piece if sums[m][tile] is None else sums[m][tile] + piece
    spare = 2 * LANES - depth
    for m in range(3):
        for n in range(2):
            at = (3 * n + m) * 2 * LANES
            if spare:
                terms_ref[at + depth : at + 2 * LANES, :] = jnp.zeros((spare, width), BF)
        for i in range(tiles):
            high = sums[m][i].astype(BF)
            high_ref[m, :, i * LANES : (i + 1) * LANES] = high
            for n, part in enumerate((high, (sums[m][i] - high.astype(F32)).astype(BF))):
                at = (3 * n + m) * 2 * LANES
                terms_ref[at : at + depth, i * LANES : (i + 1) * LANES] = part
    correlate(t_ref, terms_ref, result, entries)
    place = lax.axis_index("en")
    below = jnp.where(place == 0, 0.0, 1.0)
    above = jnp.where(place == lax.axis_size("en") - 1, 0.0, 1.0)
    odd = lax.rem(place, 2)
    keep_pair = jnp.where(odd == 1, below, above)
    keep_far = jnp.where(odd == 1, above, below)
    for i, c in enumerate((core, 1 - core)):
        pair_ref[i] = (result[2 - 2 * odd + c] * keep_pair).astype(BF)
        far_ref[i] = (result[2 * odd + c] * keep_far).astype(BF)
        own_ref[i] = result[4 + c]


def correlate(t_ref, terms_ref, result, entries):
    count, rows, width = result.shape
    lane = index((1, LANES), 1)
    carried = None
    for p in range(width // entries):
        begin = entries * p
        first = begin // LANES
        last = (begin + entries - 1) // LANES
        t = t_ref[p]
        total = dot(jnp.concatenate([t, t], axis=1), terms_ref[:, first * LANES : (last + 1) * LANES])
        for i in range(first, last + 1):
            tile = total[:, (i - first) * LANES : (i - first + 1) * LANES]
            if i == first and begin % LANES:
                tile = jnp.where(lane < begin % LANES, carried, tile)
            if i == last and (begin + entries) % LANES:
                carried = tile
            else:
                for r in range(count):
                    result[r, :, i * LANES : (i + 1) * LANES] = tile[r * rows : (r + 1) * rows]


def polar_kernel(b_own, both_core, prev_own, prev_far, turn_ref, sort_ref, high_ref, out_ref, gathered, *, half, entries, momenta, local_k, local_e, scale):
    core = my_core()
    present = jnp.where(lax.axis_index("en") == 0, 0.0, 1.0)
    gathered[core] = (prev_own[...].astype(F32) * present).astype(BF)
    gathered[1 - core] = (prev_far[...].astype(F32) * present).astype(BF)
    gathered[2 + core] = b_own[...]
    gathered[3 - core] = both_core[1]
    count, rows, width = gathered.shape
    tiles = width // LANES
    b = dot(sort_ref[...], gathered[...].reshape(count * rows, width)).astype(BF)
    sums = [None] * tiles
    for j in range(2 * half):
        start = (entries // 2) * j // LANES * LANES
        r = dot(b[:, start : start + 2 * LANES], turn_ref[j])
        for i in range(2):
            tile = start // LANES + i
            piece = r[:, i * LANES : (i + 1) * LANES]
            sums[tile] = piece if sums[tile] is None else sums[tile] + piece
    chip_k = 2 * local_k
    group = 2 * local_e
    columns = sort_ref.shape[0]
    window = local_e
    lane = index((1, LANES), 1)
    pieces = []
    for p in range(half):
        begin = entries * p
        first = begin // LANES
        last = (begin + entries - 1) // LANES
        parts = []
        for i in range(first, last + 1):
            tile = sums[i]
            if i == first and begin % LANES:
                tile = jnp.where(lane < begin % LANES, 0.0, tile)
            if i == last and (begin + entries) % LANES:
                tile = jnp.where(lane < (begin + entries) % LANES, tile, 0.0)
            parts.append(tile.astype(BF))
        rhs = jnp.concatenate(parts, axis=1)
        held = None
        for m in range(3):
            s = dot_t(high_ref[m, :, first * LANES : (last + 1) * LANES], rhs)
            acc = None
            for e in range(local_e):
                row = pltpu.roll(s[e * momenta : (e + 1) * momenta], columns - (local_e - e), 1)
                acc = row if acc is None else acc + row
            total = None
            for a in range(chip_k):
                piece = acc if a == 0 else pltpu.roll(acc, columns - group * a, 1)
                piece = piece[:, :LANES]
                if a:
                    piece = pltpu.roll(piece, momenta - a, 0)
                total = piece if total is None else total + piece
            total = jnp.where(lane < window, total * scale, 0.0)
            if m:
                total = pltpu.roll(total, m * (LANES // 4), 1)
            held = total if held is None else held + total
        pieces.append(held)
    targets, en = out_ref.shape[:2]
    for t in range(targets):
        tile = jnp.concatenate(
            [pieces[p][t * local_k + i : t * local_k + i + 1] for i in range(local_k) for p in range(half)], axis=0
        )
        for e in range(en):
            out_ref[t, e] = tile


def total_kernel(in_ref, after_ref, out_ref, *, half):
    targets, en = in_ref.shape[:2]
    local_k, _, _, window = out_ref.shape
    sums = []
    for c in range(2):
        total = None
        for t in range(c, targets, 2):
            for e in range(en):
                total = in_ref[t, e] if total is None else total + in_ref[t, e]
        sums.append(total)
    for i in range(local_k):
        tile = jnp.concatenate([sums[c][i * half : (i + 1) * half] for c in range(2)], axis=0)
        for m in range(3):
            moved = pltpu.roll(tile, LANES - m * (LANES // 4), 1) if m else tile
            out_ref[i, m] = moved[:, :window]


def sum_kernel(own, far, pair, mine, theirs):
    for n, out in enumerate((mine, theirs)):
        out[...] = (own[n] + far[n].astype(F32) + pair[n].astype(F32)).astype(BF)


def join_kernel(mine, other, perm_ref, out_ref, mark_ref, halves):
    core = my_core()
    pairs = out_ref.shape[2]
    entries = out_ref.shape[3]
    half = pairs // 2
    halves[core] = mine[...].astype(F32)
    halves[1 - core] = other[...].astype(F32)
    parts = []
    for p in range(pairs):
        begin = entries * (p % half)
        parts.append(halves[p // half][:, begin : begin + entries])
    stacked = jnp.concatenate(parts, axis=0).astype(BF)
    mark_ref[...] = jnp.zeros(mark_ref.shape, F32)
    out_ref[...] = dot(perm_ref[...], stacked).astype(BF).reshape(out_ref.shape)


def body(green_less, green_greater, derivative, neighbours, phonon, *, mom, en):
    local_k, local_e, pairs, entries = green_less.shape
    momenta, window = phonon.shape[1], phonon.shape[2]
    atoms = derivative.shape[0]
    half = pairs // 2
    rows = local_k * local_e
    width = half * entries
    chips = mom // 2
    chip_k = 2 * local_k
    total_e = local_e * en
    size = NO * NO

    deriv = derivative.transpose(1, 0, 2)
    weights = phonon.transpose(0, 1, 3, 4, 2)
    g_own, g_far, b_own, b_far, both_far = call(
        pack_kernel,
        [shape((rows, width), BF)] * 4 + [shape((2, rows, width), BF)],
        [green_less, green_greater],
        1.5,
        [
            pltpu.VMEM(green_less.shape, BF),
            pltpu.VMEM(green_less.shape, BF),
            pltpu.VMEM((2, rows, width), F32),
            pltpu.SemaphoreType.DMA((2,)),
        ],
        [HBM] * 2,
        limit=53.12,
    )

    def move(value, dchip, dcore, to=lambda e: e):
        links = []
        for m in range(mom):
            target = ((m // 2 + dchip) % chips) * 2 + (m % 2 if dcore == 0 else 1 - m % 2)
            for e in range(en):
                links.append((m * en + e, target * en + to(e)))
        return lax.ppermute(value, ("mom", "en"), links)

    def onward(e):
        return (e + 1) % en

    def to_pair(e):
        return e ^ 1 if e ^ 1 < en else e

    def to_far(e):
        other = e + 1 if e % 2 else e - 1
        return other if 0 <= other < en else e

    blocks = []
    for s in range(1, chips):
        blocks += [move(g_far, -s, 1), move(g_own, -s, 0)][::-1]
    both_core = move(both_far, 0, 1)
    blocks += [g_own, both_core]
    prev_far = move(b_far, 0, 1, onward)
    prev_own = move(b_own, 0, 0, onward)

    near = neighbours.astype(jnp.int32)
    columns = -(-chip_k * 2 * local_e // LANES) * LANES
    k_hi, k_lo, toeplitz, to_energy, to_rows, turn, sort_e = call(
        functools.partial(table_kernel, half=half, local_k=local_k, local_e=local_e),
        [
            shape((6 * half, size, 2 * LANES), BF),
            shape((6 * half, size, 2 * LANES), BF),
            shape((half, 3 * chip_k * local_e, 6 * LANES), BF),
            shape((momenta * local_e,) * 2, BF),
            shape((rows * pairs,) * 2, BF),
            shape((2 * half, 2 * LANES, 2 * LANES), BF),
            shape((columns, 2 * chip_k * local_e), BF),
        ],
        [near, deriv, weights],
        3,
        [
            pltpu.VMEM((3 * atoms, 32, 4 * LANES), F32),
            pltpu.VMEM((chip_k, 3, pairs, 4 * local_e * momenta), F32),
        ],
        [pl.BlockSpec(memory_space=pltpu.SMEM), VMEM, VMEM],
    )

    high, own, far, pair = call(
        functools.partial(product_kernel, half=half, entries=entries, chips=chips),
        [
            shape((3, momenta * local_e, width), BF),
            shape((2, rows, width), F32),
            shape((2, rows, width), BF),
            shape((2, rows, width), BF),
        ],
        blocks + [to_energy, k_hi, k_lo, toeplitz],
        4,
        [
            pltpu.VMEM((2 * chips, rows, width), BF),
            pltpu.VMEM((12 * LANES, width), BF),
            pltpu.VMEM((6, rows, width), F32),
        ],
    )
    from_far = move(far, 0, 0, to_far)
    from_pair = move(pair, 0, 0, to_pair)
    (partial,) = call(
        functools.partial(
            polar_kernel, half=half, entries=entries, momenta=momenta, local_k=local_k, local_e=local_e,
            scale=1.0 / (NO * float(np.sqrt(momenta * total_e))),
        ),
        [shape((mom, en, local_k * half, LANES), F32)],
        [b_own, both_core, prev_own, prev_far, turn, sort_e, high],
        3,
        [pltpu.VMEM((4, rows, width), BF)],
    )
    terms = lax.all_to_all(
        partial.reshape(mom * en, local_k * half, LANES), ("mom", "en"), split_axis=0, concat_axis=0, tiled=True
    )
    mine, theirs = call(
        sum_kernel, [shape((rows, width), BF)] * 2, [own, from_far, from_pair], 0.1
    )
    other = move(theirs, 0, 1)
    self_energy, mark = call(
        join_kernel,
        [shape(green_less.shape, BF), shape((8, LANES), F32)],
        [mine, other, to_rows],
        1,
        [pltpu.VMEM((2, rows, width), F32)],
    )
    (polar,) = call(
        functools.partial(total_kernel, half=half),
        [shape((local_k, 3, pairs, window), F32)],
        [terms.reshape(mom, en, local_k * half, LANES), mark],
        0.5,
    )
    polar = polar.transpose(0, 3, 1, 2)
    return (self_energy, polar)


def solution(mesh):
    return jax.shard_map(
        functools.partial(body, mom=mesh.shape["mom"], en=mesh.shape["en"]),
        mesh=mesh,
        in_specs=(P("mom", "en", None, None), P("mom", "en", None, None), P(), P(), P()),
        out_specs=(P("mom", "en", None, None), P("mom", None, None, None)),
        check_vma=False,
    )
```

```python
import functools

import jax
import jax.numpy as jnp
import numpy as np
from jax import lax
from jax.experimental import pallas as pl
from jax.experimental.pallas import tpu as pltpu
from jax.sharding import PartitionSpec as P

NO = 12
NB = 4
LANES = 128
BF = jnp.bfloat16
F32 = jnp.float32
HIGHEST = lax.Precision.HIGHEST
VMEM = pl.BlockSpec(memory_space=pltpu.VMEM)
HBM = pl.BlockSpec(memory_space=pltpu.HBM)
MIB = 1024 * 1024


def dot(a, b):
    return jnp.dot(a, b, preferred_element_type=F32)


def dot_t(a, b):
    return lax.dot_general(a, b, (((1,), (1,)), ((), ())), preferred_element_type=F32)


def call(kernel, outs, ins, work, scratch=(), specs=None, limit=24):
    return pl.pallas_call(
        kernel,
        out_shape=outs,
        in_specs=specs or [VMEM] * len(ins),
        out_specs=[VMEM] * len(outs),
        scratch_shapes=list(scratch),
        compiler_params=pltpu.CompilerParams(vmem_limit_bytes=int(limit * MIB)),
        cost_estimate=pl.CostEstimate(flops=int(work * 1e9), bytes_accessed=0, transcendentals=0),
    )(*ins)


def my_core():
    return lax.rem(lax.axis_index("mom"), 2).astype(jnp.int32)


def index(dims, axis):
    return lax.broadcasted_iota(jnp.int32, dims, axis)


def split(value, count):
    whole = jnp.floor((value.astype(F32) + 0.5) * (1.0 / count)).astype(jnp.int32)
    return whole, value - count * whole


def ones_at(condition):
    return condition.astype(F32).astype(BF)


def shape(dims, dtype):
    return jax.ShapeDtypeStruct(dims, dtype)


def pack_kernel(g_hbm, b_hbm, g_own, g_far, b_own, b_far, both_far, g_ref, b_ref, halves, sems):
    core = my_core()
    copies = []
    for i, (src, dst) in enumerate(((g_hbm, g_ref), (b_hbm, b_ref))):
        copies.append(pltpu.make_async_copy(src, dst, sems.at[i]))
        copies[-1].start()
    rows = g_own.shape[0]
    pairs = g_ref.shape[2]
    entries = g_ref.shape[3]
    half = pairs // 2
    dims = (rows, rows * pairs)
    gap = index(dims, 1) - pairs * index(dims, 0)
    perm = jnp.concatenate([ones_at(gap == p) for p in range(pairs)], axis=0)
    for copy, src, own, far in ((copies[0], g_ref, g_own, g_far), (copies[1], b_ref, b_own, b_far)):
        copy.wait()
        sorted_rows = dot(perm, src[...].reshape(rows * pairs, entries))
        for h in range(2):
            parts = [sorted_rows[(h * half + j) * rows : (h * half + j + 1) * rows] for j in range(half)]
            halves[h] = jnp.concatenate(parts, axis=1)
        own[...] = halves[core].astype(BF)
        far[...] = halves[1 - core].astype(BF)
    both_far[0] = g_far[...]
    both_far[1] = b_far[...]


def table_kernel(
    near_ref, deriv_ref, phonon_ref, hi_ref, lo_ref, t_ref, perm_ref, join_ref, turn_ref, sort_ref,
    factors, bases, *, half, local_k, local_e,
):
    core = my_core()
    _, momenta, _, pairs, window = phonon_ref.shape
    size = NO * NO
    chip_k = 2 * local_k
    dims = perm_ref.shape
    e, k = split(index(dims, 0), momenta)
    perm_ref[...] = ones_at(index(dims, 1) == k * local_e + e)
    dims = join_ref.shape
    row, p = split(index(dims, 0), pairs)
    join_ref[...] = ones_at(index(dims, 1) == p * (local_k * local_e) + row)
    dims = sort_ref.shape
    k, i = split(index(dims, 0), 2 * local_e)
    at = jnp.where(i < local_e, (chip_k + k) * local_e + local_e - 1 - i, k * local_e + 2 * local_e - 1 - i)
    sort_ref[...] = ones_at((index(dims, 1) == at) & (k < chip_k))
    dims = turn_ref.shape[1:]
    u, i = split(index(dims, 0), NO)
    turn = ((index(dims, 1) == i * NO + u) & (u < NO)).astype(F32)
    for j in range(2 * half):
        shift = size * j % LANES
        moved = pltpu.roll(pltpu.roll(turn, shift, 0), shift, 1) if shift else turn
        turn_ref[j] = (moved * (1.0 - 2.0 * (j % 2))).astype(BF)
    x = (size, 2 * LANES)
    outer, inner = split(index(x, 0), NO)
    lane_outer, lane_inner = split(index(x, 1), NO)
    pick_l = ones_at(outer == lane_outer)
    pick_r = ones_at((outer == lane_inner) & (lane_outer < NO))
    picks = jnp.concatenate([pick_l, pick_r], axis=1)
    x = (size, 32)
    outer, inner = split(index(x, 0), NO)
    slot = split(index(x, 1), 16)[1]
    rows_l = ones_at(outer == slot)
    rows_r = ones_at(inner == slot)
    x = (16, size)
    mask = (split(index(x, 1), NO)[1] == index(x, 0)).astype(F32)
    atoms = deriv_ref.shape[1]
    spread = []
    for m in range(3):
        for atom in range(atoms):
            spread.append(deriv_ref[m, atom : atom + 1, :] * mask)
    spread = jnp.concatenate(spread, axis=0)
    spread_hi = spread.astype(BF)
    spread_lo = (spread - spread_hi.astype(F32)).astype(BF)
    for i, part in enumerate((spread_hi, spread_lo)):
        rows = dot(part, picks)
        for n in range(3 * atoms):
            factors[n, 16 * i : 16 * i + 16] = rows[16 * n : 16 * n + 16]
    for p in range(half):
        pair = core * half + p
        atom = pair // NB
        other = near_ref[atom, pair % NB]
        for m in range(3):
            u = factors[m * atoms + atom][:, : 2 * LANES]
            v = factors[m * atoms + other][:, 2 * LANES :]
            for c in range(2):
                j = 2 * p + c
                shift = size * j % LANES
                uj = pltpu.roll(u, shift, 1) if shift else u
                vj = pltpu.roll(v, shift, 1) if shift else v
                kron = dot(rows_l, uj.astype(BF)) * dot(rows_r, vj.astype(BF))
                k_hi = kron.astype(BF)
                hi_ref[j * 3 + m] = k_hi
                lo_ref[j * 3 + m] = (kron - k_hi.astype(F32)).astype(BF)
    tiles = 3 * local_e // 8
    step = 8 * momenta
    first = momenta * (3 * local_e - 8)
    length = bases.shape[3]
    middle = 2 * local_e - 8
    dims = (window, length)
    lane = index(dims, 1)
    depth = index(dims, 0) + 1
    line = None
    for side in range(2):
        gap = lane - momenta * (middle + depth if side else middle - depth)
        for q in range(momenta):
            place = ones_at(gap == (-q) % momenta)
            weights = phonon_ref[side, q].astype(F32).reshape(3 * pairs, window).astype(BF)
            term = dot(weights, place)
            line = term if line is None else line + term
    lane = index((1, length), 1)
    k = split(lane, momenta)[1]
    for a in range(chip_k):
        moved = line
        if a:
            moved = jnp.where(k >= a, pltpu.roll(line, a, 1), pltpu.roll(line, length - momenta + a, 1))
        bases[a] = moved.reshape(3, pairs, length)
    for p in range(half):
        for m in range(3):
            grid = {}
            for a in range(chip_k):
                row = bases[a, m, pl.ds(core * half + p, 1), :]
                block = pltpu.roll(jnp.broadcast_to(row, (8, length)), 0, 1, stride=momenta, stride_axis=0)
                moved = {0: block}
                for t in range(tiles):
                    offset = first - step * t
                    part = offset % LANES
                    if part not in moved:
                        moved[part] = pltpu.roll(block, length - part, 1)
                    start = offset - part
                    grid[(t, a)] = moved[part][:, start : start + 2 * LANES]
            order = []
            per = local_e // 8
            for blk in (0, 2, 1):
                for a in range(chip_k):
                    order += [grid[(blk * per + i, a)] for i in range(per)]
            table = jnp.where(index((1, 2 * LANES), 1) < momenta * local_e, jnp.concatenate(order, axis=0), 0.0)
            t_ref[p, :, m * 2 * LANES : (m + 1) * 2 * LANES] = table.astype(BF)


def product_kernel(*refs, half, entries, chips):
    core = my_core()
    blocks = refs[: 2 * chips]
    perm_ref, hi_ref, lo_ref, t_ref = refs[2 * chips : 2 * chips + 4]
    high_ref, own_ref, low_ref, up_ref, gathered, terms_ref, result = refs[2 * chips + 4 :]
    for s in range(chips):
        n = 2 * ((s - 1) % chips)
        gathered[2 * s + core] = blocks[n][...]
        gathered[2 * s + 1 - core] = blocks[n + 1][...] if s else blocks[n + 1][0]
    count, rows, width = gathered.shape
    depth = count * rows
    tiles = width // LANES
    g = dot(perm_ref[...], gathered[...].reshape(depth, width)).astype(BF)
    block_rows = hi_ref.shape[1]
    sums = [[None] * tiles for _ in range(3)]
    for j in range(2 * half):
        start = (entries // 2) * j // LANES * LANES
        shift = (entries // 2) * j - start
        lhs = g[:, start : start + 2 * LANES]
        lhs = jnp.concatenate([lhs, lhs], axis=1)
        above = [jnp.zeros((shift, 2 * LANES), BF)] if shift else []
        rest = 2 * LANES - shift - block_rows
        under = [jnp.zeros((rest, 2 * LANES), BF)] if rest else []
        for m in range(3):
            parts = above + [hi_ref[j * 3 + m]] + under + above + [lo_ref[j * 3 + m]] + under
            r = dot(lhs, jnp.concatenate(parts, axis=0))
            for i in range(2):
                tile = start // LANES + i
                piece = r[:, i * LANES : (i + 1) * LANES]
                sums[m][tile] = piece if sums[m][tile] is None else sums[m][tile] + piece
    spare = 2 * LANES - depth
    for m in range(3):
        for n in range(2):
            at = (3 * n + m) * 2 * LANES
            if spare:
                terms_ref[at + depth : at + 2 * LANES, :] = jnp.zeros((spare, width), BF)
        for i in range(tiles):
            high = sums[m][i].astype(BF)
            high_ref[m, :, i * LANES : (i + 1) * LANES] = high
            for n, part in enumerate((high, (sums[m][i] - high.astype(F32)).astype(BF))):
                at = (3 * n + m) * 2 * LANES
                terms_ref[at : at + depth, i * LANES : (i + 1) * LANES] = part
    correlate(t_ref, terms_ref, result, entries)
    place = lax.axis_index("en")
    below = jnp.where(place == 0, 0.0, 1.0)
    above = jnp.where(place == lax.axis_size("en") - 1, 0.0, 1.0)
    for i, c in enumerate((core, 1 - core)):
        low_ref[i] = (result[c] * below).astype(BF)
        up_ref[i] = (result[2 + c] * above).astype(BF)
        own_ref[i] = result[4 + c]


def correlate(t_ref, terms_ref, result, entries):
    count, rows, width = result.shape
    lane = index((1, LANES), 1)
    carried = None
    for p in range(width // entries):
        begin = entries * p
        first = begin // LANES
        last = (begin + entries - 1) // LANES
        t = t_ref[p]
        total = dot(jnp.concatenate([t, t], axis=1), terms_ref[:, first * LANES : (last + 1) * LANES])
        for i in range(first, last + 1):
            tile = total[:, (i - first) * LANES : (i - first + 1) * LANES]
            if i == first and begin % LANES:
                tile = jnp.where(lane < begin % LANES, carried, tile)
            if i == last and (begin + entries) % LANES:
                carried = tile
            else:
                for r in range(count):
                    result[r, :, i * LANES : (i + 1) * LANES] = tile[r * rows : (r + 1) * rows]


def polar_kernel(b_own, both_core, prev_own, prev_far, turn_ref, sort_ref, high_ref, out_ref, gathered, *, half, entries, momenta, local_k, local_e, scale):
    core = my_core()
    present = jnp.where(lax.axis_index("en") == 0, 0.0, 1.0)
    gathered[core] = (prev_own[...].astype(F32) * present).astype(BF)
    gathered[1 - core] = (prev_far[...].astype(F32) * present).astype(BF)
    gathered[2 + core] = b_own[...]
    gathered[3 - core] = both_core[1]
    count, rows, width = gathered.shape
    tiles = width // LANES
    b = dot(sort_ref[...], gathered[...].reshape(count * rows, width)).astype(BF)
    sums = [None] * tiles
    for j in range(2 * half):
        start = (entries // 2) * j // LANES * LANES
        r = dot(b[:, start : start + 2 * LANES], turn_ref[j])
        for i in range(2):
            tile = start // LANES + i
            piece = r[:, i * LANES : (i + 1) * LANES]
            sums[tile] = piece if sums[tile] is None else sums[tile] + piece
    chip_k = 2 * local_k
    group = 2 * local_e
    columns = sort_ref.shape[0]
    window = local_e
    lane = index((1, LANES), 1)
    pieces = []
    for p in range(half):
        begin = entries * p
        first = begin // LANES
        last = (begin + entries - 1) // LANES
        parts = []
        for i in range(first, last + 1):
            tile = sums[i]
            if i == first and begin % LANES:
                tile = jnp.where(lane < begin % LANES, 0.0, tile)
            if i == last and (begin + entries) % LANES:
                tile = jnp.where(lane < (begin + entries) % LANES, tile, 0.0)
            parts.append(tile.astype(BF))
        rhs = jnp.concatenate(parts, axis=1)
        held = None
        sources = high_ref[:, :, first * LANES : (last + 1) * LANES]
        products = dot_t(sources.reshape(-1, sources.shape[2]), rhs)
        for m in range(3):
            s = products[m * momenta * local_e : (m + 1) * momenta * local_e]
            acc = None
            for e in range(local_e):
                row = pltpu.roll(s[e * momenta : (e + 1) * momenta], columns - (local_e - e), 1)
                acc = row if acc is None else acc + row
            total = None
            for a in range(chip_k):
                piece = acc if a == 0 else pltpu.roll(acc, columns - group * a, 1)
                piece = piece[:, :LANES]
                if a:
                    piece = pltpu.roll(piece, momenta - a, 0)
                total = piece if total is None else total + piece
            total = jnp.where(lane < window, total * scale, 0.0)
            if m:
                total = pltpu.roll(total, m * (LANES // 4), 1)
            held = total if held is None else held + total
        pieces.append(held)
    targets, en = out_ref.shape[:2]
    for t in range(targets):
        tile = jnp.concatenate(
            [pieces[p][t * local_k + i : t * local_k + i + 1] for i in range(local_k) for p in range(half)], axis=0
        )
        for e in range(en):
            out_ref[t, e] = tile


def total_kernel(in_ref, after_ref, out_ref, *, half):
    targets, en = in_ref.shape[:2]
    local_k, _, _, window = out_ref.shape
    sums = []
    for c in range(2):
        total = None
        for t in range(c, targets, 2):
            for e in range(en):
                total = in_ref[t, e] if total is None else total + in_ref[t, e]
        sums.append(total)
    for i in range(local_k):
        tile = jnp.concatenate([sums[c][i * half : (i + 1) * half] for c in range(2)], axis=0)
        for m in range(3):
            moved = pltpu.roll(tile, LANES - m * (LANES // 4), 1) if m else tile
            out_ref[i, m] = moved[:, :window]


def sum_kernel(own, below, above, mine, theirs):
    for n, out in enumerate((mine, theirs)):
        out[...] = (own[n] + below[n].astype(F32) + above[n].astype(F32)).astype(BF)


def join_kernel(mine, other, perm_ref, out_ref, mark_ref, halves):
    core = my_core()
    pairs = out_ref.shape[2]
    entries = out_ref.shape[3]
    half = pairs // 2
    halves[core] = mine[...].astype(F32)
    halves[1 - core] = other[...].astype(F32)
    parts = []
    for p in range(pairs):
        begin = entries * (p % half)
        parts.append(halves[p // half][:, begin : begin + entries])
    stacked = jnp.concatenate(parts, axis=0).astype(BF)
    mark_ref[...] = jnp.zeros(mark_ref.shape, F32)
    out_ref[...] = dot(perm_ref[...], stacked).astype(BF).reshape(out_ref.shape)


def body(green_less, green_greater, derivative, neighbours, phonon, *, mom, en):
    local_k, local_e, pairs, entries = green_less.shape
    momenta, window = phonon.shape[1], phonon.shape[2]
    atoms = derivative.shape[0]
    half = pairs // 2
    rows = local_k * local_e
    width = half * entries
    chips = mom // 2
    chip_k = 2 * local_k
    total_e = local_e * en
    size = NO * NO

    deriv = derivative.transpose(1, 0, 2)
    weights = phonon.transpose(0, 1, 3, 4, 2)
    g_own, g_far, b_own, b_far, both_far = call(
        pack_kernel,
        [shape((rows, width), BF)] * 4 + [shape((2, rows, width), BF)],
        [green_less, green_greater],
        1.5,
        [
            pltpu.VMEM(green_less.shape, BF),
            pltpu.VMEM(green_less.shape, BF),
            pltpu.VMEM((2, rows, width), F32),
            pltpu.SemaphoreType.DMA((2,)),
        ],
        [HBM] * 2,
        limit=53.12,
    )

    def move(value, dchip, dcore, to=lambda e: e):
        links = []
        for m in range(mom):
            target = ((m // 2 + dchip) % chips) * 2 + (m % 2 if dcore == 0 else 1 - m % 2)
            for e in range(en):
                if 0 <= to(e) < en:
                    links.append((m * en + e, target * en + to(e)))
        return lax.ppermute(value, ("mom", "en"), links)

    def onward(e):
        return (e + 1) % en

    def back(e):
        return e - 1

    blocks = []
    for s in range(1, chips):
        blocks += [move(g_far, -s, 1), move(g_own, -s, 0)][::-1]
    both_core = move(both_far, 0, 1)
    blocks += [g_own, both_core]
    prev_far = move(b_far, 0, 1, onward)
    prev_own = move(b_own, 0, 0, onward)

    near = neighbours.astype(jnp.int32)
    columns = -(-chip_k * 2 * local_e // LANES) * LANES
    k_hi, k_lo, toeplitz, to_energy, to_rows, turn, sort_e = call(
        functools.partial(table_kernel, half=half, local_k=local_k, local_e=local_e),
        [
            shape((6 * half, size, 2 * LANES), BF),
            shape((6 * half, size, 2 * LANES), BF),
            shape((half, 3 * chip_k * local_e, 6 * LANES), BF),
            shape((momenta * local_e,) * 2, BF),
            shape((rows * pairs,) * 2, BF),
            shape((2 * half, 2 * LANES, 2 * LANES), BF),
            shape((columns, 2 * chip_k * local_e), BF),
        ],
        [near, deriv, weights],
        3,
        [
            pltpu.VMEM((3 * atoms, 32, 4 * LANES), F32),
            pltpu.VMEM((chip_k, 3, pairs, 4 * local_e * momenta), F32),
        ],
        [pl.BlockSpec(memory_space=pltpu.SMEM), VMEM, VMEM],
    )

    high, own, low, up = call(
        functools.partial(product_kernel, half=half, entries=entries, chips=chips),
        [
            shape((3, momenta * local_e, width), BF),
            shape((2, rows, width), F32),
            shape((2, rows, width), BF),
            shape((2, rows, width), BF),
        ],
        blocks + [to_energy, k_hi, k_lo, toeplitz],
        4,
        [
            pltpu.VMEM((2 * chips, rows, width), BF),
            pltpu.VMEM((12 * LANES, width), BF),
            pltpu.VMEM((6, rows, width), F32),
        ],
    )
    from_below = move(up, 0, 0, onward)
    from_above = move(low, 0, 0, back)
    (partial,) = call(
        functools.partial(
            polar_kernel, half=half, entries=entries, momenta=momenta, local_k=local_k, local_e=local_e,
            scale=1.0 / (NO * float(np.sqrt(momenta * total_e))),
        ),
        [shape((mom, en, local_k * half, LANES), F32)],
        [b_own, both_core, prev_own, prev_far, turn, sort_e, high],
        3,
        [pltpu.VMEM((4, rows, width), BF)],
    )
    terms = lax.all_to_all(
        partial.reshape(mom * en, local_k * half, LANES), ("mom", "en"), split_axis=0, concat_axis=0, tiled=True
    )
    mine, theirs = call(
        sum_kernel, [shape((rows, width), BF)] * 2, [own, from_below, from_above], 0.1
    )
    other = move(theirs, 0, 1)
    self_energy, mark = call(
        join_kernel,
        [shape(green_less.shape, BF), shape((8, LANES), F32)],
        [mine, other, to_rows],
        1,
        [pltpu.VMEM((2, rows, width), F32)],
    )
    (polar,) = call(
        functools.partial(total_kernel, half=half),
        [shape((local_k, 3, pairs, window), F32)],
        [terms.reshape(mom, en, local_k * half, LANES), mark],
        0.5,
    )
    polar = polar.transpose(0, 3, 1, 2)
    return (self_energy, polar)


def solution(mesh):
    return jax.shard_map(
        functools.partial(body, mom=mesh.shape["mom"], en=mesh.shape["en"]),
        mesh=mesh,
        in_specs=(P("mom", "en", None, None), P("mom", "en", None, None), P(), P(), P()),
        out_specs=(P("mom", "en", None, None), P("mom", None, None, None)),
        check_vma=False,
    )
```

```python
import functools

import jax
import jax.numpy as jnp
import numpy as np
from jax import lax
from jax.experimental import pallas as pl
from jax.experimental.pallas import tpu as pltpu
from jax.sharding import PartitionSpec as P

NO = 12
NB = 4
LANES = 128
BF = jnp.bfloat16
F32 = jnp.float32
HIGHEST = lax.Precision.HIGHEST
VMEM = pl.BlockSpec(memory_space=pltpu.VMEM)
HBM = pl.BlockSpec(memory_space=pltpu.HBM)
MIB = 1024 * 1024


def dot(a, b):
    return jnp.dot(a, b, preferred_element_type=F32)


def dot_t(a, b):
    return lax.dot_general(a, b, (((1,), (1,)), ((), ())), preferred_element_type=F32)


def call(kernel, outs, ins, work, scratch=(), specs=None, limit=24):
    return pl.pallas_call(
        kernel,
        out_shape=outs,
        in_specs=specs or [VMEM] * len(ins),
        out_specs=[VMEM] * len(outs),
        scratch_shapes=list(scratch),
        compiler_params=pltpu.CompilerParams(vmem_limit_bytes=int(limit * MIB)),
        cost_estimate=pl.CostEstimate(flops=int(work * 1e9), bytes_accessed=0, transcendentals=0),
    )(*ins)


def my_core():
    return lax.rem(lax.axis_index("mom"), 2).astype(jnp.int32)


def index(dims, axis):
    return lax.broadcasted_iota(jnp.int32, dims, axis)


def split(value, count):
    whole = jnp.floor((value.astype(F32) + 0.5) * (1.0 / count)).astype(jnp.int32)
    return whole, value - count * whole


def ones_at(condition):
    return condition.astype(F32).astype(BF)


def shape(dims, dtype):
    return jax.ShapeDtypeStruct(dims, dtype)


def pack_kernel(g_hbm, b_hbm, g_own, g_far, b_own, b_far, both_far, g_ref, b_ref, halves, sems):
    core = my_core()
    copies = []
    for i, (src, dst) in enumerate(((g_hbm, g_ref), (b_hbm, b_ref))):
        copies.append(pltpu.make_async_copy(src, dst, sems.at[i]))
        copies[-1].start()
    rows = g_own.shape[0]
    pairs = g_ref.shape[2]
    entries = g_ref.shape[3]
    half = pairs // 2
    dims = (rows, rows * pairs)
    gap = index(dims, 1) - pairs * index(dims, 0)
    perm = jnp.concatenate([ones_at(gap == p) for p in range(pairs)], axis=0)
    for copy, src, own, far in ((copies[0], g_ref, g_own, g_far), (copies[1], b_ref, b_own, b_far)):
        copy.wait()
        sorted_rows = dot(perm, src[...].reshape(rows * pairs, entries))
        for h in range(2):
            parts = [sorted_rows[(h * half + j) * rows : (h * half + j + 1) * rows] for j in range(half)]
            halves[h] = jnp.concatenate(parts, axis=1)
        own[...] = halves[core].astype(BF)
        far[...] = halves[1 - core].astype(BF)
    both_far[0] = g_far[...]
    both_far[1] = b_far[...]


def table_kernel(
    near_ref, deriv_ref, phonon_ref, hi_ref, lo_ref, t_ref, perm_ref, join_ref, turn_ref, sort_ref,
    factors, bases, *, half, local_k, local_e,
):
    core = my_core()
    _, momenta, _, pairs, window = phonon_ref.shape
    size = NO * NO
    chip_k = 2 * local_k
    dims = perm_ref.shape
    e, k = split(index(dims, 0), momenta)
    perm_ref[...] = ones_at(index(dims, 1) == k * local_e + e)
    dims = join_ref.shape
    row, p = split(index(dims, 0), pairs)
    join_ref[...] = ones_at(index(dims, 1) == p * (local_k * local_e) + row)
    dims = sort_ref.shape
    k, i = split(index(dims, 0), 2 * local_e)
    at = jnp.where(i < local_e, (chip_k + k) * local_e + local_e - 1 - i, k * local_e + 2 * local_e - 1 - i)
    sort_ref[...] = ones_at((index(dims, 1) == at) & (k < chip_k))
    dims = turn_ref.shape[1:]
    u, i = split(index(dims, 0), NO)
    turn = ((index(dims, 1) == i * NO + u) & (u < NO)).astype(F32)
    for j in range(2 * half):
        shift = size * j % LANES
        moved = pltpu.roll(pltpu.roll(turn, shift, 0), shift, 1) if shift else turn
        turn_ref[j] = (moved * (1.0 - 2.0 * (j % 2))).astype(BF)
    x = (size, 2 * LANES)
    outer, inner = split(index(x, 0), NO)
    lane_outer, lane_inner = split(index(x, 1), NO)
    pick_l = ones_at(outer == lane_outer)
    pick_r = ones_at((outer == lane_inner) & (lane_outer < NO))
    picks = jnp.concatenate([pick_l, pick_r], axis=1)
    x = (size, 32)
    outer, inner = split(index(x, 0), NO)
    slot = split(index(x, 1), 16)[1]
    rows_l = ones_at(outer == slot)
    rows_r = ones_at(inner == slot)
    x = (16, size)
    mask = (split(index(x, 1), NO)[1] == index(x, 0)).astype(F32)
    atoms = deriv_ref.shape[1]
    spread = []
    for m in range(3):
        for atom in range(atoms):
            spread.append(deriv_ref[m, atom : atom + 1, :] * mask)
    spread = jnp.concatenate(spread, axis=0)
    spread_hi = spread.astype(BF)
    spread_lo = (spread - spread_hi.astype(F32)).astype(BF)
    for i, part in enumerate((spread_hi, spread_lo)):
        rows = dot(part, picks)
        for n in range(3 * atoms):
            factors[n, 16 * i : 16 * i + 16] = rows[16 * n : 16 * n + 16]
    for p in range(half):
        pair = core * half + p
        atom = pair // NB
        other = near_ref[atom, pair % NB]
        for m in range(3):
            u = factors[m * atoms + atom][:, : 2 * LANES]
            v = factors[m * atoms + other][:, 2 * LANES :]
            for c in range(2):
                j = 2 * p + c
                shift = size * j % LANES
                uj = pltpu.roll(u, shift, 1) if shift else u
                vj = pltpu.roll(v, shift, 1) if shift else v
                kron = dot(rows_l, uj.astype(BF)) * dot(rows_r, vj.astype(BF))
                k_hi = kron.astype(BF)
                hi_ref[j * 3 + m] = k_hi
                lo_ref[j * 3 + m] = (kron - k_hi.astype(F32)).astype(BF)
    tiles = 3 * local_e // 8
    step = 8 * momenta
    first = momenta * (3 * local_e - 8)
    length = bases.shape[3]
    middle = 2 * local_e - 8
    dims = (window, length)
    lane = index(dims, 1)
    depth = index(dims, 0) + 1
    line = None
    for side in range(2):
        gap = lane - momenta * (middle + depth if side else middle - depth)
        for q in range(momenta):
            place = ones_at(gap == (-q) % momenta)
            weights = phonon_ref[side, q].astype(F32).reshape(3 * pairs, window).astype(BF)
            term = dot(weights, place)
            line = term if line is None else line + term
    lane = index((1, length), 1)
    k = split(lane, momenta)[1]
    for a in range(chip_k):
        moved = line
        if a:
            moved = jnp.where(k >= a, pltpu.roll(line, a, 1), pltpu.roll(line, length - momenta + a, 1))
        bases[a] = moved.reshape(3, pairs, length)
    for p in range(half):
        for m in range(3):
            grid = {}
            for a in range(chip_k):
                row = bases[a, m, pl.ds(core * half + p, 1), :]
                block = pltpu.roll(jnp.broadcast_to(row, (8, length)), 0, 1, stride=momenta, stride_axis=0)
                moved = {0: block}
                for t in range(tiles):
                    offset = first - step * t
                    part = offset % LANES
                    if part not in moved:
                        moved[part] = pltpu.roll(block, length - part, 1)
                    start = offset - part
                    grid[(t, a)] = moved[part][:, start : start + 2 * LANES]
            order = []
            per = local_e // 8
            for blk in (0, 2, 1):
                for a in range(chip_k):
                    order += [grid[(blk * per + i, a)] for i in range(per)]
            table = jnp.where(index((1, 2 * LANES), 1) < momenta * local_e, jnp.concatenate(order, axis=0), 0.0)
            t_ref[p, :, m * 2 * LANES : (m + 1) * 2 * LANES] = table.astype(BF)


def product_kernel(*refs, half, entries, chips):
    core = my_core()
    blocks = refs[: 2 * chips]
    perm_ref, hi_ref, lo_ref, t_ref = refs[2 * chips : 2 * chips + 4]
    high_ref, own_ref, low_ref, up_ref, gathered, terms_ref, result = refs[2 * chips + 4 :]
    for s in range(chips):
        n = 2 * ((s - 1) % chips)
        gathered[2 * s + core] = blocks[n][...]
        gathered[2 * s + 1 - core] = blocks[n + 1][...] if s else blocks[n + 1][0]
    count, rows, width = gathered.shape
    depth = count * rows
    tiles = width // LANES
    g = dot(perm_ref[...], gathered[...].reshape(depth, width)).astype(BF)
    block_rows = hi_ref.shape[1]
    sums = [[None] * tiles for _ in range(3)]
    for j in range(2 * half):
        start = (entries // 2) * j // LANES * LANES
        shift = (entries // 2) * j - start
        lhs = g[:, start : start + 2 * LANES]
        lhs = jnp.concatenate([lhs, lhs], axis=1)
        above = [jnp.zeros((shift, 2 * LANES), BF)] if shift else []
        rest = 2 * LANES - shift - block_rows
        under = [jnp.zeros((rest, 2 * LANES), BF)] if rest else []
        for m in range(3):
            parts = above + [hi_ref[j * 3 + m]] + under + above + [lo_ref[j * 3 + m]] + under
            r = dot(lhs, jnp.concatenate(parts, axis=0))
            for i in range(2):
                tile = start // LANES + i
                piece = r[:, i * LANES : (i + 1) * LANES]
                sums[m][tile] = piece if sums[m][tile] is None else sums[m][tile] + piece
    spare = 2 * LANES - depth
    for m in range(3):
        for n in range(2):
            at = (3 * n + m) * 2 * LANES
            if spare:
                terms_ref[at + depth : at + 2 * LANES, :] = jnp.zeros((spare, width), BF)
        for i in range(tiles):
            high = sums[m][i].astype(BF)
            high_ref[m, :, i * LANES : (i + 1) * LANES] = high
            for n, part in enumerate((high, (sums[m][i] - high.astype(F32)).astype(BF))):
                at = (3 * n + m) * 2 * LANES
                terms_ref[at : at + depth, i * LANES : (i + 1) * LANES] = part
    correlate(t_ref, terms_ref, result, entries)
    place = lax.axis_index("en")
    below = jnp.where(place == 0, 0.0, 1.0)
    above = jnp.where(place == lax.axis_size("en") - 1, 0.0, 1.0)
    for i, c in enumerate((core, 1 - core)):
        low_ref[i] = (result[c] * below).astype(BF)
        up_ref[i] = (result[2 + c] * above).astype(BF)
        own_ref[i] = result[4 + c]


def correlate(t_ref, terms_ref, result, entries):
    count, rows, width = result.shape
    lane = index((1, LANES), 1)
    carried = None
    for p in range(width // entries):
        begin = entries * p
        first = begin // LANES
        last = (begin + entries - 1) // LANES
        t = t_ref[p]
        total = dot(jnp.concatenate([t, t], axis=1), terms_ref[:, first * LANES : (last + 1) * LANES])
        for i in range(first, last + 1):
            tile = total[:, (i - first) * LANES : (i - first + 1) * LANES]
            if i == first and begin % LANES:
                tile = jnp.where(lane < begin % LANES, carried, tile)
            if i == last and (begin + entries) % LANES:
                carried = tile
            else:
                for r in range(count):
                    result[r, :, i * LANES : (i + 1) * LANES] = tile[r * rows : (r + 1) * rows]


def polar_kernel(b_own, both_core, prev_own, prev_far, turn_ref, sort_ref, high_ref, out_ref, gathered, *, half, entries, momenta, local_k, local_e, scale):
    core = my_core()
    present = jnp.where(lax.axis_index("en") == 0, 0.0, 1.0)
    gathered[core] = (prev_own[...].astype(F32) * present).astype(BF)
    gathered[1 - core] = (prev_far[...].astype(F32) * present).astype(BF)
    gathered[2 + core] = b_own[...]
    gathered[3 - core] = both_core[1]
    count, rows, width = gathered.shape
    tiles = width // LANES
    b = dot(sort_ref[...], gathered[...].reshape(count * rows, width)).astype(BF)
    sums = [None] * tiles
    for j in range(2 * half):
        start = (entries // 2) * j // LANES * LANES
        r = dot(b[:, start : start + 2 * LANES], turn_ref[j])
        for i in range(2):
            tile = start // LANES + i
            piece = r[:, i * LANES : (i + 1) * LANES]
            sums[tile] = piece if sums[tile] is None else sums[tile] + piece
    chip_k = 2 * local_k
    group = 2 * local_e
    columns = sort_ref.shape[0]
    window = local_e
    lane = index((1, LANES), 1)
    pieces = []
    for p in range(half):
        begin = entries * p
        first = begin // LANES
        last = (begin + entries - 1) // LANES
        parts = []
        for i in range(first, last + 1):
            tile = sums[i]
            if i == first and begin % LANES:
                tile = jnp.where(lane < begin % LANES, 0.0, tile)
            if i == last and (begin + entries) % LANES:
                tile = jnp.where(lane < (begin + entries) % LANES, tile, 0.0)
            parts.append(tile.astype(BF))
        rhs = jnp.concatenate(parts, axis=1)
        held = None
        sources = high_ref[:, :, first * LANES : (last + 1) * LANES]
        products = dot_t(sources.reshape(-1, sources.shape[2]), rhs)
        for m in range(3):
            s = products[m * momenta * local_e : (m + 1) * momenta * local_e]
            acc = None
            for e in range(local_e):
                row = pltpu.roll(s[e * momenta : (e + 1) * momenta], columns - (local_e - e), 1)
                acc = row if acc is None else acc + row
            total = None
            for a in range(chip_k):
                piece = acc if a == 0 else pltpu.roll(acc, columns - group * a, 1)
                piece = piece[:, :LANES]
                if a:
                    piece = pltpu.roll(piece, momenta - a, 0)
                total = piece if total is None else total + piece
            total = jnp.where(lane < window, total * scale, 0.0)
            if m:
                total = pltpu.roll(total, m * (LANES // 4), 1)
            held = total if held is None else held + total
        pieces.append(held)
    for t in range(out_ref.shape[0]):
        out_ref[t] = jnp.concatenate(
            [pieces[p][t * local_k + i : t * local_k + i + 1] for i in range(local_k) for p in range(half)], axis=0
        )


def spread_kernel(in_ref, out_ref):
    for c in range(2):
        total = in_ref[c]
        for t in range(c + 2, in_ref.shape[0], 2):
            total = total + in_ref[t]
        for e in range(out_ref.shape[0]):
            out_ref[e, c] = total


def total_kernel(in_ref, out_ref, *, half):
    local_k, _, _, window = out_ref.shape
    sums = []
    for c in range(2):
        total = in_ref[0, c]
        for e in range(1, in_ref.shape[0]):
            total = total + in_ref[e, c]
        sums.append(total)
    for i in range(local_k):
        tile = jnp.concatenate([sums[c][i * half : (i + 1) * half] for c in range(2)], axis=0)
        for m in range(3):
            moved = pltpu.roll(tile, LANES - m * (LANES // 4), 1) if m else tile
            out_ref[i, m] = moved[:, :window]


def sum_kernel(own, below, above, mine, theirs):
    for n, out in enumerate((mine, theirs)):
        out[...] = (own[n] + below[n].astype(F32) + above[n].astype(F32)).astype(BF)


def join_kernel(mine, other, perm_ref, out_ref, halves):
    core = my_core()
    pairs = out_ref.shape[2]
    entries = out_ref.shape[3]
    half = pairs // 2
    halves[core] = mine[...].astype(F32)
    halves[1 - core] = other[...].astype(F32)
    parts = []
    for p in range(pairs):
        begin = entries * (p % half)
        parts.append(halves[p // half][:, begin : begin + entries])
    stacked = jnp.concatenate(parts, axis=0).astype(BF)
    out_ref[...] = dot(perm_ref[...], stacked).astype(BF).reshape(out_ref.shape)


def body(green_less, green_greater, derivative, neighbours, phonon, *, mom, en):
    local_k, local_e, pairs, entries = green_less.shape
    momenta, window = phonon.shape[1], phonon.shape[2]
    atoms = derivative.shape[0]
    half = pairs // 2
    rows = local_k * local_e
    width = half * entries
    chips = mom // 2
    chip_k = 2 * local_k
    total_e = local_e * en
    size = NO * NO

    deriv = derivative.transpose(1, 0, 2)
    weights = phonon.transpose(0, 1, 3, 4, 2)
    g_own, g_far, b_own, b_far, both_far = call(
        pack_kernel,
        [shape((rows, width), BF)] * 4 + [shape((2, rows, width), BF)],
        [green_less, green_greater],
        1.5,
        [
            pltpu.VMEM(green_less.shape, BF),
            pltpu.VMEM(green_less.shape, BF),
            pltpu.VMEM((2, rows, width), F32),
            pltpu.SemaphoreType.DMA((2,)),
        ],
        [HBM] * 2,
        limit=53.12,
    )

    def move(value, dchip, dcore, to=lambda e: e):
        links = []
        for m in range(mom):
            target = ((m // 2 + dchip) % chips) * 2 + (m % 2 if dcore == 0 else 1 - m % 2)
            for e in range(en):
                links.append((m * en + e, target * en + to(e)))
        return lax.ppermute(value, ("mom", "en"), links)

    def onward(e):
        return (e + 1) % en

    def back(e):
        return (e - 1) % en

    blocks = []
    for s in range(1, chips):
        blocks += [move(g_far, -s, 1), move(g_own, -s, 0)][::-1]
    both_core = move(both_far, 0, 1)
    blocks += [g_own, both_core]
    prev_far = move(b_far, 0, 1, onward)
    prev_own = move(b_own, 0, 0, onward)

    near = neighbours.astype(jnp.int32)
    columns = -(-chip_k * 2 * local_e // LANES) * LANES
    k_hi, k_lo, toeplitz, to_energy, to_rows, turn, sort_e = call(
        functools.partial(table_kernel, half=half, local_k=local_k, local_e=local_e),
        [
            shape((6 * half, size, 2 * LANES), BF),
            shape((6 * half, size, 2 * LANES), BF),
            shape((half, 3 * chip_k * local_e, 6 * LANES), BF),
            shape((momenta * local_e,) * 2, BF),
            shape((rows * pairs,) * 2, BF),
            shape((2 * half, 2 * LANES, 2 * LANES), BF),
            shape((columns, 2 * chip_k * local_e), BF),
        ],
        [near, deriv, weights],
        3,
        [
            pltpu.VMEM((3 * atoms, 32, 4 * LANES), F32),
            pltpu.VMEM((chip_k, 3, pairs, 4 * local_e * momenta), F32),
        ],
        [pl.BlockSpec(memory_space=pltpu.SMEM), VMEM, VMEM],
    )

    high, own, low, up = call(
        functools.partial(product_kernel, half=half, entries=entries, chips=chips),
        [
            shape((3, momenta * local_e, width), BF),
            shape((2, rows, width), F32),
            shape((2, rows, width), BF),
            shape((2, rows, width), BF),
        ],
        blocks + [to_energy, k_hi, k_lo, toeplitz],
        4,
        [
            pltpu.VMEM((2 * chips, rows, width), BF),
            pltpu.VMEM((12 * LANES, width), BF),
            pltpu.VMEM((6, rows, width), F32),
        ],
    )
    from_below = move(up, 0, 0, onward)
    from_above = move(low, 0, 0, back)
    (partial,) = call(
        functools.partial(
            polar_kernel, half=half, entries=entries, momenta=momenta, local_k=local_k, local_e=local_e,
            scale=1.0 / (NO * float(np.sqrt(momenta * total_e))),
        ),
        [shape((mom, local_k * half, LANES), F32)],
        [b_own, both_core, prev_own, prev_far, turn, sort_e, high],
        3,
        [pltpu.VMEM((4, rows, width), BF)],
    )
    terms = lax.all_to_all(partial, "mom", split_axis=0, concat_axis=0, tiled=True)
    (copies,) = call(spread_kernel, [shape((en, 2, local_k * half, LANES), F32)], [terms], 0.2)
    terms = lax.all_to_all(copies, "en", split_axis=0, concat_axis=0, tiled=True)
    mine, theirs = call(
        sum_kernel, [shape((rows, width), BF)] * 2, [own, from_below, from_above], 0.1
    )
    other = move(theirs, 0, 1)
    (self_energy,) = call(
        join_kernel,
        [shape(green_less.shape, BF)],
        [mine, other, to_rows],
        1,
        [pltpu.VMEM((2, rows, width), F32)],
    )
    (polar,) = call(
        functools.partial(total_kernel, half=half),
        [shape((local_k, 3, pairs, window), F32)],
        [terms],
        0.5,
    )
    polar = polar.transpose(0, 3, 1, 2)
    return (self_energy, polar)


def solution(mesh):
    return jax.shard_map(
        functools.partial(body, mom=mesh.shape["mom"], en=mesh.shape["en"]),
        mesh=mesh,
        in_specs=(P("mom", "en", None, None), P("mom", "en", None, None), P(), P(), P()),
        out_specs=(P("mom", "en", None, None), P("mom", None, None, None)),
        check_vma=False,
    )
```

```python
import functools

import jax
import jax.numpy as jnp
import numpy as np
from jax import lax
from jax.experimental import pallas as pl
from jax.experimental.pallas import tpu as pltpu
from jax.sharding import PartitionSpec as P

NO = 12
NB = 4
LANES = 128
BF = jnp.bfloat16
F32 = jnp.float32
HIGHEST = lax.Precision.HIGHEST
VMEM = pl.BlockSpec(memory_space=pltpu.VMEM)
HBM = pl.BlockSpec(memory_space=pltpu.HBM)
MIB = 1024 * 1024


def dot(a, b):
    return jnp.dot(a, b, preferred_element_type=F32)


def dot_t(a, b):
    return lax.dot_general(a, b, (((1,), (1,)), ((), ())), preferred_element_type=F32)


def call(kernel, outs, ins, work, scratch=(), specs=None, limit=24):
    return pl.pallas_call(
        kernel,
        out_shape=outs,
        in_specs=specs or [VMEM] * len(ins),
        out_specs=[VMEM] * len(outs),
        scratch_shapes=list(scratch),
        compiler_params=pltpu.CompilerParams(vmem_limit_bytes=int(limit * MIB)),
        cost_estimate=pl.CostEstimate(flops=int(work * 1e9), bytes_accessed=0, transcendentals=0),
    )(*ins)


def my_core():
    return lax.rem(lax.axis_index("mom"), 2).astype(jnp.int32)


def index(dims, axis):
    return lax.broadcasted_iota(jnp.int32, dims, axis)


def split(value, count):
    whole = jnp.floor((value.astype(F32) + 0.5) * (1.0 / count)).astype(jnp.int32)
    return whole, value - count * whole


def ones_at(condition):
    return condition.astype(F32).astype(BF)


def shape(dims, dtype):
    return jax.ShapeDtypeStruct(dims, dtype)


def pack_kernel(g_hbm, b_hbm, g_own, g_far, b_own, b_far, both_far, g_ref, b_ref, halves, sems):
    core = my_core()
    copies = []
    for i, (src, dst) in enumerate(((g_hbm, g_ref), (b_hbm, b_ref))):
        copies.append(pltpu.make_async_copy(src, dst, sems.at[i]))
        copies[-1].start()
    rows = g_own.shape[0]
    pairs = g_ref.shape[2]
    entries = g_ref.shape[3]
    half = pairs // 2
    dims = (rows, rows * pairs)
    gap = index(dims, 1) - pairs * index(dims, 0)
    perm = jnp.concatenate([ones_at(gap == p) for p in range(pairs)], axis=0)
    for copy, src, own, far in ((copies[0], g_ref, g_own, g_far), (copies[1], b_ref, b_own, b_far)):
        copy.wait()
        sorted_rows = dot(perm, src[...].reshape(rows * pairs, entries))
        for h in range(2):
            parts = [sorted_rows[(h * half + j) * rows : (h * half + j + 1) * rows] for j in range(half)]
            halves[h] = jnp.concatenate(parts, axis=1)
        own[...] = halves[core].astype(BF)
        far[...] = halves[1 - core].astype(BF)
    both_far[0] = g_far[...]
    both_far[1] = b_far[...]


def table_kernel(
    near_ref, deriv_ref, phonon_ref, hi_ref, lo_ref, t_ref, perm_ref, join_ref, turn_ref, sort_ref,
    factors, bases, *, half, local_k, local_e,
):
    core = my_core()
    _, momenta, _, pairs, window = phonon_ref.shape
    size = NO * NO
    chip_k = 2 * local_k
    dims = perm_ref.shape
    e, k = split(index(dims, 0), momenta)
    perm_ref[...] = ones_at(index(dims, 1) == k * local_e + e)
    dims = join_ref.shape
    row, p = split(index(dims, 0), pairs)
    join_ref[...] = ones_at(index(dims, 1) == p * (local_k * local_e) + row)
    dims = sort_ref.shape
    k, i = split(index(dims, 0), 2 * local_e)
    at = jnp.where(i < local_e, (chip_k + k) * local_e + local_e - 1 - i, k * local_e + 2 * local_e - 1 - i)
    sort_ref[...] = ones_at((index(dims, 1) == at) & (k < chip_k))
    dims = turn_ref.shape[1:]
    u, i = split(index(dims, 0), NO)
    turn = ((index(dims, 1) == i * NO + u) & (u < NO)).astype(F32)
    for j in range(2 * half):
        shift = size * j % LANES
        moved = pltpu.roll(pltpu.roll(turn, shift, 0), shift, 1) if shift else turn
        turn_ref[j] = (moved * (1.0 - 2.0 * (j % 2))).astype(BF)
    x = (size, 2 * LANES)
    outer, inner = split(index(x, 0), NO)
    lane_outer, lane_inner = split(index(x, 1), NO)
    pick_l = ones_at(outer == lane_outer)
    pick_r = ones_at((outer == lane_inner) & (lane_outer < NO))
    picks = jnp.concatenate([pick_l, pick_r], axis=1)
    x = (size, 32)
    outer, inner = split(index(x, 0), NO)
    slot = split(index(x, 1), 16)[1]
    rows_l = ones_at(outer == slot)
    rows_r = ones_at(inner == slot)
    x = (16, size)
    mask = (split(index(x, 1), NO)[1] == index(x, 0)).astype(F32)
    atoms = deriv_ref.shape[1]
    spread = []
    for m in range(3):
        for atom in range(atoms):
            spread.append(deriv_ref[m, atom : atom + 1, :] * mask)
    spread = jnp.concatenate(spread, axis=0)
    spread_hi = spread.astype(BF)
    spread_lo = (spread - spread_hi.astype(F32)).astype(BF)
    for i, part in enumerate((spread_hi, spread_lo)):
        rows = dot(part, picks)
        for n in range(3 * atoms):
            factors[n, 16 * i : 16 * i + 16] = rows[16 * n : 16 * n + 16]
    for p in range(half):
        pair = core * half + p
        atom = pair // NB
        other = near_ref[atom, pair % NB]
        for m in range(3):
            u = factors[m * atoms + atom][:, : 2 * LANES]
            v = factors[m * atoms + other][:, 2 * LANES :]
            for c in range(2):
                j = 2 * p + c
                shift = size * j % LANES
                uj = pltpu.roll(u, shift, 1) if shift else u
                vj = pltpu.roll(v, shift, 1) if shift else v
                kron = dot(rows_l, uj.astype(BF)) * dot(rows_r, vj.astype(BF))
                k_hi = kron.astype(BF)
                hi_ref[j * 3 + m] = k_hi
                lo_ref[j * 3 + m] = (kron - k_hi.astype(F32)).astype(BF)
    tiles = 3 * local_e // 8
    step = 8 * momenta
    first = momenta * (3 * local_e - 8)
    length = bases.shape[3]
    middle = 2 * local_e - 8
    dims = (window, length)
    lane = index(dims, 1)
    depth = index(dims, 0) + 1
    line = None
    for side in range(2):
        gap = lane - momenta * (middle + depth if side else middle - depth)
        for q in range(momenta):
            place = ones_at(gap == (-q) % momenta)
            weights = phonon_ref[side, q].astype(F32).reshape(3 * pairs, window).astype(BF)
            term = dot(weights, place)
            line = term if line is None else line + term
    lane = index((1, length), 1)
    k = split(lane, momenta)[1]
    for a in range(chip_k):
        moved = line
        if a:
            moved = jnp.where(k >= a, pltpu.roll(line, a, 1), pltpu.roll(line, length - momenta + a, 1))
        bases[a] = moved.reshape(3, pairs, length)
    for p in range(half):
        for m in range(3):
            grid = {}
            for a in range(chip_k):
                row = bases[a, m, pl.ds(core * half + p, 1), :]
                block = pltpu.roll(jnp.broadcast_to(row, (8, length)), 0, 1, stride=momenta, stride_axis=0)
                moved = {0: block}
                for t in range(tiles):
                    offset = first - step * t
                    part = offset % LANES
                    if part not in moved:
                        moved[part] = pltpu.roll(block, length - part, 1)
                    start = offset - part
                    grid[(t, a)] = moved[part][:, start : start + 2 * LANES]
            order = []
            per = local_e // 8
            for blk in (0, 2, 1):
                for a in range(chip_k):
                    order += [grid[(blk * per + i, a)] for i in range(per)]
            table = jnp.where(index((1, 2 * LANES), 1) < momenta * local_e, jnp.concatenate(order, axis=0), 0.0)
            t_ref[p, :, m * 2 * LANES : (m + 1) * 2 * LANES] = table.astype(BF)


def product_kernel(*refs, half, entries, chips):
    core = my_core()
    blocks = refs[: 2 * chips]
    perm_ref, hi_ref, lo_ref, t_ref = refs[2 * chips : 2 * chips + 4]
    high_ref, own_ref, far_ref, pair_ref, gathered, terms_ref, result = refs[2 * chips + 4 :]
    for s in range(chips):
        n = 2 * ((s - 1) % chips)
        gathered[2 * s + core] = blocks[n][...]
        gathered[2 * s + 1 - core] = blocks[n + 1][...] if s else blocks[n + 1][0]
    count, rows, width = gathered.shape
    depth = count * rows
    tiles = width // LANES
    g = dot(perm_ref[...], gathered[...].reshape(depth, width)).astype(BF)
    block_rows = hi_ref.shape[1]
    sums = [[None] * tiles for _ in range(3)]
    for j in range(2 * half):
        start = (entries // 2) * j // LANES * LANES
        shift = (entries // 2) * j - start
        lhs = g[:, start : start + 2 * LANES]
        lhs = jnp.concatenate([lhs, lhs], axis=1)
        above = [jnp.zeros((shift, 2 * LANES), BF)] if shift else []
        rest = 2 * LANES - shift - block_rows
        under = [jnp.zeros((rest, 2 * LANES), BF)] if rest else []
        for m in range(3):
            parts = above + [hi_ref[j * 3 + m]] + under + above + [lo_ref[j * 3 + m]] + under
            r = dot(lhs, jnp.concatenate(parts, axis=0))
            for i in range(2):
                tile = start // LANES + i
                piece = r[:, i * LANES : (i + 1) * LANES]
                sums[m][tile] = piece if sums[m][tile] is None else sums[m][tile] + piece
    spare = 2 * LANES - depth
    for m in range(3):
        for n in range(2):
            at = (3 * n + m) * 2 * LANES
            if spare:
                terms_ref[at + depth : at + 2 * LANES, :] = jnp.zeros((spare, width), BF)
        for i in range(tiles):
            high = sums[m][i].astype(BF)
            high_ref[m, :, i * LANES : (i + 1) * LANES] = high
            for n, part in enumerate((high, (sums[m][i] - high.astype(F32)).astype(BF))):
                at = (3 * n + m) * 2 * LANES
                terms_ref[at : at + depth, i * LANES : (i + 1) * LANES] = part
    correlate(t_ref, terms_ref, result, entries)
    place = lax.axis_index("en")
    below = jnp.where(place == 0, 0.0, 1.0)
    above = jnp.where(place == lax.axis_size("en") - 1, 0.0, 1.0)
    odd = lax.rem(place, 2)
    keep_pair = jnp.where(odd == 1, below, above)
    keep_far = jnp.where(odd == 1, above, below)
    for i, c in enumerate((core, 1 - core)):
        pair_ref[i] = (result[2 - 2 * odd + c] * keep_pair).astype(BF)
        far_ref[i] = (result[2 * odd + c] * keep_far).astype(BF)
        own_ref[i] = result[4 + c]


def correlate(t_ref, terms_ref, result, entries):
    count, rows, width = result.shape
    lane = index((1, LANES), 1)
    carried = None
    for p in range(width // entries):
        begin = entries * p
        first = begin // LANES
        last = (begin + entries - 1) // LANES
        t = t_ref[p]
        total = dot(jnp.concatenate([t, t], axis=1), terms_ref[:, first * LANES : (last + 1) * LANES])
        for i in range(first, last + 1):
            tile = total[:, (i - first) * LANES : (i - first + 1) * LANES]
            if i == first and begin % LANES:
                tile = jnp.where(lane < begin % LANES, carried, tile)
            if i == last and (begin + entries) % LANES:
                carried = tile
            else:
                for r in range(count):
                    result[r, :, i * LANES : (i + 1) * LANES] = tile[r * rows : (r + 1) * rows]


def polar_kernel(b_own, both_core, prev_own, prev_far, turn_ref, sort_ref, high_ref, out_ref, gathered, *, half, entries, momenta, local_k, local_e, scale):
    core = my_core()
    present = jnp.where(lax.axis_index("en") == 0, 0.0, 1.0)
    gathered[core] = (prev_own[...].astype(F32) * present).astype(BF)
    gathered[1 - core] = (prev_far[...].astype(F32) * present).astype(BF)
    gathered[2 + core] = b_own[...]
    gathered[3 - core] = both_core[1]
    count, rows, width = gathered.shape
    tiles = width // LANES
    b = dot(sort_ref[...], gathered[...].reshape(count * rows, width)).astype(BF)
    sums = [None] * tiles
    for j in range(2 * half):
        start = (entries // 2) * j // LANES * LANES
        r = dot(b[:, start : start + 2 * LANES], turn_ref[j])
        for i in range(2):
            tile = start // LANES + i
            piece = r[:, i * LANES : (i + 1) * LANES]
            sums[tile] = piece if sums[tile] is None else sums[tile] + piece
    chip_k = 2 * local_k
    group = 2 * local_e
    columns = sort_ref.shape[0]
    window = local_e
    lane = index((1, LANES), 1)
    pieces = []
    for p in range(half):
        begin = entries * p
        first = begin // LANES
        last = (begin + entries - 1) // LANES
        parts = []
        for i in range(first, last + 1):
            tile = sums[i]
            if i == first and begin % LANES:
                tile = jnp.where(lane < begin % LANES, 0.0, tile)
            if i == last and (begin + entries) % LANES:
                tile = jnp.where(lane < (begin + entries) % LANES, tile, 0.0)
            parts.append(tile.astype(BF))
        rhs = jnp.concatenate(parts, axis=1)
        held = None
        sources = high_ref[:, :, first * LANES : (last + 1) * LANES]
        products = dot_t(sources.reshape(-1, sources.shape[2]), rhs)
        for m in range(3):
            s = products[m * momenta * local_e : (m + 1) * momenta * local_e]
            acc = None
            for e in range(local_e):
                row = pltpu.roll(s[e * momenta : (e + 1) * momenta], columns - (local_e - e), 1)
                acc = row if acc is None else acc + row
            total = None
            for a in range(chip_k):
                piece = acc if a == 0 else pltpu.roll(acc, columns - group * a, 1)
                piece = piece[:, :LANES]
                if a:
                    piece = pltpu.roll(piece, momenta - a, 0)
                total = piece if total is None else total + piece
            total = jnp.where(lane < window, total * scale, 0.0)
            if m:
                total = pltpu.roll(total, m * (LANES // 4), 1)
            held = total if held is None else held + total
        pieces.append(held)
    targets, en = out_ref.shape[:2]
    for t in range(targets):
        tile = jnp.concatenate(
            [pieces[p][t * local_k + i : t * local_k + i + 1] for i in range(local_k) for p in range(half)], axis=0
        )
        for e in range(en):
            out_ref[t, e] = tile


def total_kernel(in_ref, after_ref, out_ref, *, half):
    targets, en = in_ref.shape[:2]
    local_k, _, _, window = out_ref.shape
    sums = []
    for c in range(2):
        total = None
        for t in range(c, targets, 2):
            for e in range(en):
                total = in_ref[t, e] if total is None else total + in_ref[t, e]
        sums.append(total)
    for i in range(local_k):
        tile = jnp.concatenate([sums[c][i * half : (i + 1) * half] for c in range(2)], axis=0)
        for m in range(3):
            moved = pltpu.roll(tile, LANES - m * (LANES // 4), 1) if m else tile
            out_ref[i, m] = moved[:, :window]


def sum_kernel(own, far, pair, mine, theirs):
    for n, out in enumerate((mine, theirs)):
        out[...] = (own[n] + far[n].astype(F32) + pair[n].astype(F32)).astype(BF)


def join_kernel(mine, other, perm_ref, out_ref, mark_ref, halves):
    core = my_core()
    pairs = out_ref.shape[2]
    entries = out_ref.shape[3]
    half = pairs // 2
    halves[core] = mine[...].astype(F32)
    halves[1 - core] = other[...].astype(F32)
    parts = []
    for p in range(pairs):
        begin = entries * (p % half)
        parts.append(halves[p // half][:, begin : begin + entries])
    stacked = jnp.concatenate(parts, axis=0).astype(BF)
    mark_ref[...] = jnp.zeros(mark_ref.shape, F32)
    out_ref[...] = dot(perm_ref[...], stacked).astype(BF).reshape(out_ref.shape)


def body(green_less, green_greater, derivative, neighbours, phonon, *, mom, en):
    local_k, local_e, pairs, entries = green_less.shape
    momenta, window = phonon.shape[1], phonon.shape[2]
    atoms = derivative.shape[0]
    half = pairs // 2
    rows = local_k * local_e
    width = half * entries
    chips = mom // 2
    chip_k = 2 * local_k
    total_e = local_e * en
    size = NO * NO

    deriv = derivative.transpose(1, 0, 2)
    weights = phonon.transpose(0, 1, 3, 4, 2)
    g_own, g_far, b_own, b_far, both_far = call(
        pack_kernel,
        [shape((rows, width), BF)] * 4 + [shape((2, rows, width), BF)],
        [green_less, green_greater],
        1.5,
        [
            pltpu.VMEM(green_less.shape, BF),
            pltpu.VMEM(green_less.shape, BF),
            pltpu.VMEM((2, rows, width), F32),
            pltpu.SemaphoreType.DMA((2,)),
        ],
        [HBM] * 2,
        limit=53.12,
    )

    def move(value, dchip, dcore, to=lambda e: e):
        links = []
        for m in range(mom):
            target = ((m // 2 + dchip) % chips) * 2 + (m % 2 if dcore == 0 else 1 - m % 2)
            for e in range(en):
                links.append((m * en + e, target * en + to(e)))
        return lax.ppermute(value, ("mom", "en"), links)

    def onward(e):
        return (e + 1) % en

    def to_pair(e):
        return e ^ 1 if e ^ 1 < en else e

    def to_far(e):
        other = e + 1 if e % 2 else e - 1
        return other % en if en % 2 == 0 else max(other, 0)

    blocks = []
    for s in range(1, chips):
        blocks += [move(g_far, -s, 1), move(g_own, -s, 0)][::-1]
    both_core = move(both_far, 0, 1)
    blocks += [g_own, both_core]
    prev_far = move(b_far, 0, 1, onward)
    prev_own = move(b_own, 0, 0, onward)

    near = neighbours.astype(jnp.int32)
    columns = -(-chip_k * 2 * local_e // LANES) * LANES
    k_hi, k_lo, toeplitz, to_energy, to_rows, turn, sort_e = call(
        functools.partial(table_kernel, half=half, local_k=local_k, local_e=local_e),
        [
            shape((6 * half, size, 2 * LANES), BF),
            shape((6 * half, size, 2 * LANES), BF),
            shape((half, 3 * chip_k * local_e, 6 * LANES), BF),
            shape((momenta * local_e,) * 2, BF),
            shape((rows * pairs,) * 2, BF),
            shape((2 * half, 2 * LANES, 2 * LANES), BF),
            shape((columns, 2 * chip_k * local_e), BF),
        ],
        [near, deriv, weights],
        3,
        [
            pltpu.VMEM((3 * atoms, 32, 4 * LANES), F32),
            pltpu.VMEM((chip_k, 3, pairs, 4 * local_e * momenta), F32),
        ],
        [pl.BlockSpec(memory_space=pltpu.SMEM), VMEM, VMEM],
    )

    high, own, far, pair = call(
        functools.partial(product_kernel, half=half, entries=entries, chips=chips),
        [
            shape((3, momenta * local_e, width), BF),
            shape((2, rows, width), F32),
            shape((2, rows, width), BF),
            shape((2, rows, width), BF),
        ],
        blocks + [to_energy, k_hi, k_lo, toeplitz],
        4,
        [
            pltpu.VMEM((2 * chips, rows, width), BF),
            pltpu.VMEM((12 * LANES, width), BF),
            pltpu.VMEM((6, rows, width), F32),
        ],
    )
    from_far = move(far, 0, 0, to_far)
    from_pair = move(pair, 0, 0, to_pair)
    (partial,) = call(
        functools.partial(
            polar_kernel, half=half, entries=entries, momenta=momenta, local_k=local_k, local_e=local_e,
            scale=1.0 / (NO * float(np.sqrt(momenta * total_e))),
        ),
        [shape((mom, en, local_k * half, LANES), F32)],
        [b_own, both_core, prev_own, prev_far, turn, sort_e, high],
        3,
        [pltpu.VMEM((4, rows, width), BF)],
    )
    terms = lax.all_to_all(
        partial.reshape(mom * en, local_k * half, LANES), ("mom", "en"), split_axis=0, concat_axis=0, tiled=True
    )
    mine, theirs = call(
        sum_kernel, [shape((rows, width), BF)] * 2, [own, from_far, from_pair], 0.1
    )
    other = move(theirs, 0, 1)
    self_energy, mark = call(
        join_kernel,
        [shape(green_less.shape, BF), shape((8, LANES), F32)],
        [mine, other, to_rows],
        1,
        [pltpu.VMEM((2, rows, width), F32)],
    )
    (polar,) = call(
        functools.partial(total_kernel, half=half),
        [shape((local_k, 3, pairs, window), F32)],
        [terms.reshape(mom, en, local_k * half, LANES), mark],
        0.5,
    )
    polar = polar.transpose(0, 3, 1, 2)
    return (self_energy, polar)


def solution(mesh):
    return jax.shard_map(
        functools.partial(body, mom=mesh.shape["mom"], en=mesh.shape["en"]),
        mesh=mesh,
        in_specs=(P("mom", "en", None, None), P("mom", "en", None, None), P(), P(), P()),
        out_specs=(P("mom", "en", None, None), P("mom", None, None, None)),
        check_vma=False,
    )
```

```python
import functools

import jax
import jax.numpy as jnp
import numpy as np
from jax import lax
from jax.experimental import pallas as pl
from jax.experimental.pallas import tpu as pltpu
from jax.sharding import PartitionSpec as P

NO = 12
NB = 4
LANES = 128
BF = jnp.bfloat16
F32 = jnp.float32
HIGHEST = lax.Precision.HIGHEST
VMEM = pl.BlockSpec(memory_space=pltpu.VMEM)
HBM = pl.BlockSpec(memory_space=pltpu.HBM)
MIB = 1024 * 1024


def dot(a, b):
    return jnp.dot(a, b, preferred_element_type=F32)


def dot_t(a, b):
    return lax.dot_general(a, b, (((1,), (1,)), ((), ())), preferred_element_type=F32)


def call(kernel, outs, ins, work, scratch=(), specs=None, limit=24):
    return pl.pallas_call(
        kernel,
        out_shape=outs,
        in_specs=specs or [VMEM] * len(ins),
        out_specs=[VMEM] * len(outs),
        scratch_shapes=list(scratch),
        compiler_params=pltpu.CompilerParams(vmem_limit_bytes=int(limit * MIB)),
        cost_estimate=pl.CostEstimate(flops=int(work * 1e9), bytes_accessed=0, transcendentals=0),
    )(*ins)


def my_core():
    return lax.rem(lax.axis_index("mom"), 2).astype(jnp.int32)


def index(dims, axis):
    return lax.broadcasted_iota(jnp.int32, dims, axis)


def split(value, count):
    whole = jnp.floor((value.astype(F32) + 0.5) * (1.0 / count)).astype(jnp.int32)
    return whole, value - count * whole


def ones_at(condition):
    return condition.astype(F32).astype(BF)


def shape(dims, dtype):
    return jax.ShapeDtypeStruct(dims, dtype)


def pack_kernel(g_hbm, b_hbm, g_own, g_far, b_own, b_far, both_far, g_ref, b_ref, halves, sems):
    core = my_core()
    copies = []
    for i, (src, dst) in enumerate(((g_hbm, g_ref), (b_hbm, b_ref))):
        copies.append(pltpu.make_async_copy(src, dst, sems.at[i]))
        copies[-1].start()
    rows = g_own.shape[0]
    pairs = g_ref.shape[2]
    entries = g_ref.shape[3]
    half = pairs // 2
    dims = (rows, rows * pairs)
    gap = index(dims, 1) - pairs * index(dims, 0)
    perm = jnp.concatenate([ones_at(gap == p) for p in range(pairs)], axis=0)
    for copy, src, own, far in ((copies[0], g_ref, g_own, g_far), (copies[1], b_ref, b_own, b_far)):
        copy.wait()
        sorted_rows = dot(perm, src[...].reshape(rows * pairs, entries))
        for h in range(2):
            parts = [sorted_rows[(h * half + j) * rows : (h * half + j + 1) * rows] for j in range(half)]
            halves[h] = jnp.concatenate(parts, axis=1)
        own[...] = halves[core].astype(BF)
        far[...] = halves[1 - core].astype(BF)
    both_far[0] = g_far[...]
    both_far[1] = b_far[...]


def table_kernel(
    near_ref, deriv_ref, phonon_ref, hi_ref, lo_ref, t_ref, perm_ref, join_ref, turn_ref, sort_ref,
    factors, bases, *, half, local_k, local_e,
):
    core = my_core()
    _, momenta, _, pairs, window = phonon_ref.shape
    size = NO * NO
    chip_k = 2 * local_k
    dims = perm_ref.shape
    e, k = split(index(dims, 0), momenta)
    perm_ref[...] = ones_at(index(dims, 1) == k * local_e + e)
    dims = join_ref.shape
    row, p = split(index(dims, 0), pairs)
    join_ref[...] = ones_at(index(dims, 1) == p * (local_k * local_e) + row)
    dims = sort_ref.shape
    k, i = split(index(dims, 0), 2 * local_e)
    at = jnp.where(i < local_e, (chip_k + k) * local_e + local_e - 1 - i, k * local_e + 2 * local_e - 1 - i)
    sort_ref[...] = ones_at((index(dims, 1) == at) & (k < chip_k))
    dims = turn_ref.shape[1:]
    u, i = split(index(dims, 0), NO)
    turn = ((index(dims, 1) == i * NO + u) & (u < NO)).astype(F32)
    for j in range(2 * half):
        shift = size * j % LANES
        moved = pltpu.roll(pltpu.roll(turn, shift, 0), shift, 1) if shift else turn
        turn_ref[j] = (moved * (1.0 - 2.0 * (j % 2))).astype(BF)
    x = (size, 2 * LANES)
    outer, inner = split(index(x, 0), NO)
    lane_outer, lane_inner = split(index(x, 1), NO)
    pick_l = ones_at(outer == lane_outer)
    pick_r = ones_at((outer == lane_inner) & (lane_outer < NO))
    picks = jnp.concatenate([pick_l, pick_r], axis=1)
    x = (size, 32)
    outer, inner = split(index(x, 0), NO)
    slot = split(index(x, 1), 16)[1]
    rows_l = ones_at(outer == slot)
    rows_r = ones_at(inner == slot)
    x = (16, size)
    mask = (split(index(x, 1), NO)[1] == index(x, 0)).astype(F32)
    atoms = deriv_ref.shape[1]
    spread = []
    for m in range(3):
        for atom in range(atoms):
            spread.append(deriv_ref[m, atom : atom + 1, :] * mask)
    spread = jnp.concatenate(spread, axis=0)
    spread_hi = spread.astype(BF)
    spread_lo = (spread - spread_hi.astype(F32)).astype(BF)
    for i, part in enumerate((spread_hi, spread_lo)):
        rows = dot(part, picks)
        for n in range(3 * atoms):
            factors[n, 16 * i : 16 * i + 16] = rows[16 * n : 16 * n + 16]
    for p in range(half):
        pair = core * half + p
        atom = pair // NB
        other = near_ref[atom, pair % NB]
        for m in range(3):
            u = factors[m * atoms + atom][:, : 2 * LANES]
            v = factors[m * atoms + other][:, 2 * LANES :]
            for c in range(2):
                j = 2 * p + c
                shift = size * j % LANES
                uj = pltpu.roll(u, shift, 1) if shift else u
                vj = pltpu.roll(v, shift, 1) if shift else v
                kron = dot(rows_l, uj.astype(BF)) * dot(rows_r, vj.astype(BF))
                k_hi = kron.astype(BF)
                hi_ref[j * 3 + m] = k_hi
                lo_ref[j * 3 + m] = (kron - k_hi.astype(F32)).astype(BF)
    tiles = 3 * local_e // 8
    step = 8 * momenta
    first = momenta * (3 * local_e - 8)
    length = bases.shape[3]
    middle = 2 * local_e - 8
    dims = (window, length)
    lane = index(dims, 1)
    depth = index(dims, 0) + 1
    line = None
    for side in range(2):
        gap = lane - momenta * (middle + depth if side else middle - depth)
        for q in range(momenta):
            place = ones_at(gap == (-q) % momenta)
            weights = phonon_ref[side, q].astype(F32).reshape(3 * pairs, window).astype(BF)
            term = dot(weights, place)
            line = term if line is None else line + term
    lane = index((1, length), 1)
    k = split(lane, momenta)[1]
    for a in range(chip_k):
        moved = line
        if a:
            moved = jnp.where(k >= a, pltpu.roll(line, a, 1), pltpu.roll(line, length - momenta + a, 1))
        bases[a] = moved.reshape(3, pairs, length)
    for p in range(half):
        for m in range(3):
            grid = {}
            for a in range(chip_k):
                row = bases[a, m, pl.ds(core * half + p, 1), :]
                block = pltpu.roll(jnp.broadcast_to(row, (8, length)), 0, 1, stride=momenta, stride_axis=0)
                moved = {0: block}
                for t in range(tiles):
                    offset = first - step * t
                    part = offset % LANES
                    if part not in moved:
                        moved[part] = pltpu.roll(block, length - part, 1)
                    start = offset - part
                    grid[(t, a)] = moved[part][:, start : start + 2 * LANES]
            order = []
            per = local_e // 8
            for blk in (0, 2, 1):
                for a in range(chip_k):
                    order += [grid[(blk * per + i, a)] for i in range(per)]
            table = jnp.where(index((1, 2 * LANES), 1) < momenta * local_e, jnp.concatenate(order, axis=0), 0.0)
            t_ref[p, :, m * 2 * LANES : (m + 1) * 2 * LANES] = table.astype(BF)


def product_kernel(*refs, half, entries, chips):
    core = my_core()
    blocks = refs[: 2 * chips]
    perm_ref, hi_ref, lo_ref, t_ref = refs[2 * chips : 2 * chips + 4]
    high_ref, own_ref, low_ref, up_ref, gathered, terms_ref, result = refs[2 * chips + 4 :]
    for s in range(chips):
        n = 2 * ((s - 1) % chips)
        gathered[2 * s + core] = blocks[n][...]
        gathered[2 * s + 1 - core] = blocks[n + 1][...] if s else blocks[n + 1][0]
    count, rows, width = gathered.shape
    depth = count * rows
    tiles = width // LANES
    g = dot(perm_ref[...], gathered[...].reshape(depth, width)).astype(BF)
    block_rows = hi_ref.shape[1]
    sums = [[None] * tiles for _ in range(3)]
    for j in range(2 * half):
        start = (entries // 2) * j // LANES * LANES
        shift = (entries // 2) * j - start
        lhs = g[:, start : start + 2 * LANES]
        lhs = jnp.concatenate([lhs, lhs], axis=1)
        above = [jnp.zeros((shift, 2 * LANES), BF)] if shift else []
        rest = 2 * LANES - shift - block_rows
        under = [jnp.zeros((rest, 2 * LANES), BF)] if rest else []
        for m in range(3):
            parts = above + [hi_ref[j * 3 + m]] + under + above + [lo_ref[j * 3 + m]] + under
            r = dot(lhs, jnp.concatenate(parts, axis=0))
            for i in range(2):
                tile = start // LANES + i
                piece = r[:, i * LANES : (i + 1) * LANES]
                sums[m][tile] = piece if sums[m][tile] is None else sums[m][tile] + piece
    spare = 2 * LANES - depth
    for m in range(3):
        for n in range(2):
            at = (3 * n + m) * 2 * LANES
            if spare:
                terms_ref[at + depth : at + 2 * LANES, :] = jnp.zeros((spare, width), BF)
        for i in range(tiles):
            high = sums[m][i].astype(BF)
            high_ref[m, :, i * LANES : (i + 1) * LANES] = high
            for n, part in enumerate((high, (sums[m][i] - high.astype(F32)).astype(BF))):
                at = (3 * n + m) * 2 * LANES
                terms_ref[at : at + depth, i * LANES : (i + 1) * LANES] = part
    correlate(t_ref, terms_ref, result, entries)
    place = lax.axis_index("en")
    below = jnp.where(place == 0, 0.0, 1.0)
    above = jnp.where(place == lax.axis_size("en") - 1, 0.0, 1.0)
    for i, c in enumerate((core, 1 - core)):
        low_ref[i] = (result[c] * below).astype(BF)
        up_ref[i] = (result[2 + c] * above).astype(BF)
        own_ref[i] = result[4 + c]


def correlate(t_ref, terms_ref, result, entries):
    count, rows, width = result.shape
    lane = index((1, LANES), 1)
    carried = None
    for p in range(width // entries):
        begin = entries * p
        first = begin // LANES
        last = (begin + entries - 1) // LANES
        t = t_ref[p]
        total = dot(jnp.concatenate([t, t], axis=1), terms_ref[:, first * LANES : (last + 1) * LANES])
        for i in range(first, last + 1):
            tile = total[:, (i - first) * LANES : (i - first + 1) * LANES]
            if i == first and begin % LANES:
                tile = jnp.where(lane < begin % LANES, carried, tile)
            if i == last and (begin + entries) % LANES:
                carried = tile
            else:
                for r in range(count):
                    result[r, :, i * LANES : (i + 1) * LANES] = tile[r * rows : (r + 1) * rows]


def polar_kernel(b_own, both_core, prev_own, prev_far, turn_ref, sort_ref, high_ref, out_ref, gathered, *, half, entries, momenta, local_k, local_e, scale):
    core = my_core()
    present = jnp.where(lax.axis_index("en") == 0, 0.0, 1.0)
    gathered[core] = (prev_own[...].astype(F32) * present).astype(BF)
    gathered[1 - core] = (prev_far[...].astype(F32) * present).astype(BF)
    gathered[2 + core] = b_own[...]
    gathered[3 - core] = both_core[1]
    count, rows, width = gathered.shape
    tiles = width // LANES
    b = dot(sort_ref[...], gathered[...].reshape(count * rows, width)).astype(BF)
    sums = [None] * tiles
    for j in range(2 * half):
        start = (entries // 2) * j // LANES * LANES
        r = dot(b[:, start : start + 2 * LANES], turn_ref[j])
        for i in range(2):
            tile = start // LANES + i
            piece = r[:, i * LANES : (i + 1) * LANES]
            sums[tile] = piece if sums[tile] is None else sums[tile] + piece
    chip_k = 2 * local_k
    group = 2 * local_e
    columns = sort_ref.shape[0]
    window = local_e
    lane = index((1, LANES), 1)
    pieces = []
    for p in range(half):
        begin = entries * p
        first = begin // LANES
        last = (begin + entries - 1) // LANES
        parts = []
        for i in range(first, last + 1):
            tile = sums[i]
            if i == first and begin % LANES:
                tile = jnp.where(lane < begin % LANES, 0.0, tile)
            if i == last and (begin + entries) % LANES:
                tile = jnp.where(lane < (begin + entries) % LANES, tile, 0.0)
            parts.append(tile.astype(BF))
        rhs = jnp.concatenate(parts, axis=1)
        held = None
        sources = high_ref[:, :, first * LANES : (last + 1) * LANES]
        products = dot_t(sources.reshape(-1, sources.shape[2]), rhs)
        for m in range(3):
            s = products[m * momenta * local_e : (m + 1) * momenta * local_e]
            acc = None
            for e in range(local_e):
                row = pltpu.roll(s[e * momenta : (e + 1) * momenta], columns - (local_e - e), 1)
                acc = row if acc is None else acc + row
            total = None
            for a in range(chip_k):
                piece = acc if a == 0 else pltpu.roll(acc, columns - group * a, 1)
                piece = piece[:, :LANES]
                if a:
                    piece = pltpu.roll(piece, momenta - a, 0)
                total = piece if total is None else total + piece
            total = jnp.where(lane < window, total * scale, 0.0)
            if m:
                total = pltpu.roll(total, m * (LANES // 4), 1)
            held = total if held is None else held + total
        pieces.append(held)
    targets, en = out_ref.shape[:2]
    for t in range(targets):
        tile = jnp.concatenate(
            [pieces[p][t * local_k + i : t * local_k + i + 1] for i in range(local_k) for p in range(half)], axis=0
        )
        for e in range(en):
            out_ref[t, e] = tile


def total_kernel(in_ref, after_ref, out_ref, *, half):
    targets, en = in_ref.shape[:2]
    local_k, _, _, window = out_ref.shape
    sums = []
    for c in range(2):
        total = None
        for t in range(c, targets, 2):
            for e in range(en):
                total = in_ref[t, e] if total is None else total + in_ref[t, e]
        sums.append(total)
    for i in range(local_k):
        tile = jnp.concatenate([sums[c][i * half : (i + 1) * half] for c in range(2)], axis=0)
        for m in range(3):
            moved = pltpu.roll(tile, LANES - m * (LANES // 4), 1) if m else tile
            out_ref[i, m] = moved[:, :window]


def sum_kernel(own, below, above, mine, theirs):
    for n, out in enumerate((mine, theirs)):
        out[...] = (own[n] + below[n].astype(F32) + above[n].astype(F32)).astype(BF)


def join_kernel(mine, other, perm_ref, out_ref, mark_ref, halves):
    core = my_core()
    pairs = out_ref.shape[2]
    entries = out_ref.shape[3]
    half = pairs // 2
    halves[core] = mine[...].astype(F32)
    halves[1 - core] = other[...].astype(F32)
    parts = []
    for p in range(pairs):
        begin = entries * (p % half)
        parts.append(halves[p // half][:, begin : begin + entries])
    stacked = jnp.concatenate(parts, axis=0).astype(BF)
    mark_ref[...] = jnp.zeros(mark_ref.shape, F32)
    out_ref[...] = dot(perm_ref[...], stacked).astype(BF).reshape(out_ref.shape)


def body(green_less, green_greater, derivative, neighbours, phonon, *, mom, en):
    local_k, local_e, pairs, entries = green_less.shape
    momenta, window = phonon.shape[1], phonon.shape[2]
    atoms = derivative.shape[0]
    half = pairs // 2
    rows = local_k * local_e
    width = half * entries
    chips = mom // 2
    chip_k = 2 * local_k
    total_e = local_e * en
    size = NO * NO

    deriv = derivative.transpose(1, 0, 2)
    weights = phonon.transpose(0, 1, 3, 4, 2)
    g_own, g_far, b_own, b_far, both_far = call(
        pack_kernel,
        [shape((rows, width), BF)] * 4 + [shape((2, rows, width), BF)],
        [green_less, green_greater],
        1.5,
        [
            pltpu.VMEM(green_less.shape, BF),
            pltpu.VMEM(green_less.shape, BF),
            pltpu.VMEM((2, rows, width), F32),
            pltpu.SemaphoreType.DMA((2,)),
        ],
        [HBM] * 2,
        limit=53.12,
    )

    def move(value, dchip, dcore, to=lambda e: e):
        links = []
        for m in range(mom):
            target = ((m // 2 + dchip) % chips) * 2 + (m % 2 if dcore == 0 else 1 - m % 2)
            for e in range(en):
                links.append((m * en + e, target * en + to(e)))
        return lax.ppermute(value, ("mom", "en"), links)

    def onward(e):
        return (e + 1) % en

    def back(e):
        return (e - 1) % en

    blocks = []
    for s in range(1, chips):
        blocks += [move(g_far, -s, 1), move(g_own, -s, 0)][::-1]
    both_core = move(both_far, 0, 1)
    blocks += [g_own, both_core]
    prev_far = move(b_far, 0, 1, onward)
    prev_own = move(b_own, 0, 0, onward)

    near = neighbours.astype(jnp.int32)
    columns = -(-chip_k * 2 * local_e // LANES) * LANES
    k_hi, k_lo, toeplitz, to_energy, to_rows, turn, sort_e = call(
        functools.partial(table_kernel, half=half, local_k=local_k, local_e=local_e),
        [
            shape((6 * half, size, 2 * LANES), BF),
            shape((6 * half, size, 2 * LANES), BF),
            shape((half, 3 * chip_k * local_e, 6 * LANES), BF),
            shape((momenta * local_e,) * 2, BF),
            shape((rows * pairs,) * 2, BF),
            shape((2 * half, 2 * LANES, 2 * LANES), BF),
            shape((columns, 2 * chip_k * local_e), BF),
        ],
        [near, deriv, weights],
        3,
        [
            pltpu.VMEM((3 * atoms, 32, 4 * LANES), F32),
            pltpu.VMEM((chip_k, 3, pairs, 4 * local_e * momenta), F32),
        ],
        [pl.BlockSpec(memory_space=pltpu.SMEM), VMEM, VMEM],
    )

    high, own, low, up = call(
        functools.partial(product_kernel, half=half, entries=entries, chips=chips),
        [
            shape((3, momenta * local_e, width), BF),
            shape((2, rows, width), F32),
            shape((2, rows, width), BF),
            shape((2, rows, width), BF),
        ],
        blocks + [to_energy, k_hi, k_lo, toeplitz],
        4,
        [
            pltpu.VMEM((2 * chips, rows, width), BF),
            pltpu.VMEM((12 * LANES, width), BF),
            pltpu.VMEM((6, rows, width), F32),
        ],
    )
    from_below = move(up, 0, 0, onward)
    from_above = move(low, 0, 0, back)
    (partial,) = call(
        functools.partial(
            polar_kernel, half=half, entries=entries, momenta=momenta, local_k=local_k, local_e=local_e,
            scale=1.0 / (NO * float(np.sqrt(momenta * total_e))),
        ),
        [shape((mom, en, local_k * half, LANES), F32)],
        [b_own, both_core, prev_own, prev_far, turn, sort_e, high],
        3,
        [pltpu.VMEM((4, rows, width), BF)],
    )
    terms = lax.all_to_all(
        partial.reshape(mom * en, local_k * half, LANES), ("mom", "en"), split_axis=0, concat_axis=0, tiled=True
    )
    mine, theirs = call(
        sum_kernel, [shape((rows, width), BF)] * 2, [own, from_below, from_above], 0.1
    )
    other = move(theirs, 0, 1)
    self_energy, mark = call(
        join_kernel,
        [shape(green_less.shape, BF), shape((8, LANES), F32)],
        [mine, other, to_rows],
        1,
        [pltpu.VMEM((2, rows, width), F32)],
    )
    (polar,) = call(
        functools.partial(total_kernel, half=half),
        [shape((local_k, 3, pairs, window), F32)],
        [terms.reshape(mom, en, local_k * half, LANES), mark],
        0.5,
    )
    polar = polar.transpose(0, 3, 1, 2)
    return (self_energy, polar)


def solution(mesh):
    return jax.shard_map(
        functools.partial(body, mom=mesh.shape["mom"], en=mesh.shape["en"]),
        mesh=mesh,
        in_specs=(P("mom", "en", None, None), P("mom", "en", None, None), P(), P(), P()),
        out_specs=(P("mom", "en", None, None), P("mom", None, None, None)),
        check_vma=False,
    )
```

```python
import functools

import jax
import jax.numpy as jnp
import numpy as np
from jax import lax
from jax.experimental import pallas as pl
from jax.experimental.pallas import tpu as pltpu
from jax.sharding import PartitionSpec as P

NO = 12
NB = 4
LANES = 128
BF = jnp.bfloat16
F32 = jnp.float32
HIGHEST = lax.Precision.HIGHEST
VMEM = pl.BlockSpec(memory_space=pltpu.VMEM)
HBM = pl.BlockSpec(memory_space=pltpu.HBM)
MIB = 1024 * 1024


def dot(a, b):
    return jnp.dot(a, b, preferred_element_type=F32)


def dot_t(a, b):
    return lax.dot_general(a, b, (((1,), (1,)), ((), ())), preferred_element_type=F32)


def call(kernel, outs, ins, work, scratch=(), specs=None, limit=24):
    return pl.pallas_call(
        kernel,
        out_shape=outs,
        in_specs=specs or [VMEM] * len(ins),
        out_specs=[VMEM] * len(outs),
        scratch_shapes=list(scratch),
        compiler_params=pltpu.CompilerParams(vmem_limit_bytes=int(limit * MIB)),
        cost_estimate=pl.CostEstimate(flops=int(work * 1e9), bytes_accessed=0, transcendentals=0),
    )(*ins)


def my_core():
    return lax.rem(lax.axis_index("mom"), 2).astype(jnp.int32)


def index(dims, axis):
    return lax.broadcasted_iota(jnp.int32, dims, axis)


def column(dims):
    return index((dims[0], 1), 0)


def row(dims):
    return index((1, dims[1]), 1)


def split(value, count):
    whole = jnp.floor((value.astype(F32) + 0.5) * (1.0 / count)).astype(jnp.int32)
    return whole, value - count * whole


def ones_at(condition):
    return condition.astype(F32).astype(BF)


def shape(dims, dtype):
    return jax.ShapeDtypeStruct(dims, dtype)


def pack_kernel(g_hbm, b_hbm, g_own, g_far, b_own, b_far, both_far, g_ref, b_ref, halves, sems):
    core = my_core()
    copies = []
    for i, (src, dst) in enumerate(((g_hbm, g_ref), (b_hbm, b_ref))):
        copies.append(pltpu.make_async_copy(src, dst, sems.at[i]))
        copies[-1].start()
    rows = g_own.shape[0]
    pairs = g_ref.shape[2]
    entries = g_ref.shape[3]
    half = pairs // 2
    dims = (rows, rows * pairs)
    gap = index(dims, 1) - pairs * index(dims, 0)
    perm = jnp.concatenate([ones_at(gap == p) for p in range(pairs)], axis=0)
    for copy, src, own, far in ((copies[0], g_ref, g_own, g_far), (copies[1], b_ref, b_own, b_far)):
        copy.wait()
        sorted_rows = dot(perm, src[...].reshape(rows * pairs, entries))
        for h in range(2):
            parts = [sorted_rows[(h * half + j) * rows : (h * half + j + 1) * rows] for j in range(half)]
            halves[h] = jnp.concatenate(parts, axis=1)
        own[...] = halves[core].astype(BF)
        far[...] = halves[1 - core].astype(BF)
    both_far[0] = g_far[...]
    both_far[1] = b_far[...]


def table_kernel(
    near_ref, deriv_ref, phonon_ref, hi_ref, lo_ref, t_ref, perm_ref, join_ref, turn_ref, sort_ref,
    factors, bases, *, half, local_k, local_e,
):
    core = my_core()
    _, momenta, _, pairs, window = phonon_ref.shape
    size = NO * NO
    chip_k = 2 * local_k
    dims = perm_ref.shape
    e, k = split(column(dims), momenta)
    perm_ref[...] = ones_at(row(dims) == k * local_e + e)
    dims = join_ref.shape
    n, p = split(column(dims), pairs)
    join_ref[...] = ones_at(row(dims) == p * (local_k * local_e) + n)
    dims = sort_ref.shape
    k, i = split(column(dims), 2 * local_e)
    at = jnp.where(i < local_e, (chip_k + k) * local_e + local_e - 1 - i, k * local_e + 2 * local_e - 1 - i)
    sort_ref[...] = ones_at(row(dims) == jnp.where(k < chip_k, at, -1))
    dims = turn_ref.shape[1:]
    u, i = split(column(dims), NO)
    turn = (row(dims) == jnp.where(u < NO, i * NO + u, -1)).astype(F32)
    for j in range(2 * half):
        shift = size * j % LANES
        moved = pltpu.roll(pltpu.roll(turn, shift, 0), shift, 1) if shift else turn
        turn_ref[j] = (moved * (1.0 - 2.0 * (j % 2))).astype(BF)
    x = (size, 2 * LANES)
    outer, inner = split(column(x), NO)
    lane_outer, lane_inner = split(row(x), NO)
    pick_l = ones_at(outer == lane_outer)
    pick_r = ones_at(outer == jnp.where(lane_outer < NO, lane_inner, -1))
    picks = jnp.concatenate([pick_l, pick_r], axis=1)
    x = (size, 32)
    slot = split(row(x), 16)[1]
    rows_l = ones_at(outer == slot)
    rows_r = ones_at(inner == slot)
    x = (16, size)
    mask = (split(row(x), NO)[1] == column(x)).astype(F32)
    atoms = deriv_ref.shape[1]
    spread = []
    for m in range(3):
        for atom in range(atoms):
            spread.append(deriv_ref[m, atom : atom + 1, :] * mask)
    spread = jnp.concatenate(spread, axis=0)
    spread_hi = spread.astype(BF)
    spread_lo = (spread - spread_hi.astype(F32)).astype(BF)
    for i, part in enumerate((spread_hi, spread_lo)):
        rows = dot(part, picks)
        for n in range(3 * atoms):
            factors[n, 16 * i : 16 * i + 16] = rows[16 * n : 16 * n + 16]
    for p in range(half):
        pair = core * half + p
        atom = pair // NB
        other = near_ref[atom, pair % NB]
        for m in range(3):
            u = factors[m * atoms + atom][:, : 2 * LANES]
            v = factors[m * atoms + other][:, 2 * LANES :]
            for c in range(2):
                j = 2 * p + c
                shift = size * j % LANES
                uj = pltpu.roll(u, shift, 1) if shift else u
                vj = pltpu.roll(v, shift, 1) if shift else v
                kron = dot(rows_l, uj.astype(BF)) * dot(rows_r, vj.astype(BF))
                k_hi = kron.astype(BF)
                hi_ref[j * 3 + m] = k_hi
                lo_ref[j * 3 + m] = (kron - k_hi.astype(F32)).astype(BF)
    tiles = 3 * local_e // 8
    step = 8 * momenta
    first = momenta * (3 * local_e - 8)
    length = bases.shape[3]
    middle = 2 * local_e - 8
    dims = (window, length)
    lane = index(dims, 1)
    depth = index(dims, 0) + 1
    line = None
    for side in range(2):
        gap = lane - momenta * (middle + depth if side else middle - depth)
        for q in range(momenta):
            place = ones_at(gap == (-q) % momenta)
            weights = phonon_ref[side, q].astype(F32).reshape(3 * pairs, window).astype(BF)
            term = dot(weights, place)
            line = term if line is None else line + term
    lane = index((1, length), 1)
    k = split(lane, momenta)[1]
    for a in range(chip_k):
        moved = line
        if a:
            moved = jnp.where(k >= a, pltpu.roll(line, a, 1), pltpu.roll(line, length - momenta + a, 1))
        bases[a] = moved.reshape(3, pairs, length)
    for p in range(half):
        for m in range(3):
            grid = {}
            for a in range(chip_k):
                line = bases[a, m, pl.ds(core * half + p, 1), :]
                block = pltpu.roll(jnp.broadcast_to(line, (8, length)), 0, 1, stride=momenta, stride_axis=0)
                moved = {0: block}
                for t in range(tiles):
                    offset = first - step * t
                    part = offset % LANES
                    if part not in moved:
                        moved[part] = pltpu.roll(block, length - part, 1)
                    start = offset - part
                    grid[(t, a)] = moved[part][:, start : start + 2 * LANES]
            order = []
            per = local_e // 8
            for blk in (0, 2, 1):
                for a in range(chip_k):
                    order += [grid[(blk * per + i, a)] for i in range(per)]
            table = jnp.where(index((1, 2 * LANES), 1) < momenta * local_e, jnp.concatenate(order, axis=0), 0.0)
            t_ref[p, :, m * 2 * LANES : (m + 1) * 2 * LANES] = table.astype(BF)


def product_kernel(*refs, half, entries, chips):
    core = my_core()
    blocks = refs[: 2 * chips]
    perm_ref, hi_ref, lo_ref, t_ref = refs[2 * chips : 2 * chips + 4]
    high_ref, own_ref, low_ref, up_ref, gathered, terms_ref, result = refs[2 * chips + 4 :]
    for s in range(chips):
        n = 2 * ((s - 1) % chips)
        gathered[2 * s + core] = blocks[n][...]
        gathered[2 * s + 1 - core] = blocks[n + 1][...] if s else blocks[n + 1][0]
    count, rows, width = gathered.shape
    depth = count * rows
    tiles = width // LANES
    g = dot(perm_ref[...], gathered[...].reshape(depth, width)).astype(BF)
    block_rows = hi_ref.shape[1]
    sums = [[None] * tiles for _ in range(3)]
    for j in range(2 * half):
        start = (entries // 2) * j // LANES * LANES
        shift = (entries // 2) * j - start
        lhs = g[:, start : start + 2 * LANES]
        lhs = jnp.concatenate([lhs, lhs], axis=1)
        above = [jnp.zeros((shift, 2 * LANES), BF)] if shift else []
        rest = 2 * LANES - shift - block_rows
        under = [jnp.zeros((rest, 2 * LANES), BF)] if rest else []
        for m in range(3):
            parts = above + [hi_ref[j * 3 + m]] + under + above + [lo_ref[j * 3 + m]] + under
            r = dot(lhs, jnp.concatenate(parts, axis=0))
            for i in range(2):
                tile = start // LANES + i
                piece = r[:, i * LANES : (i + 1) * LANES]
                sums[m][tile] = piece if sums[m][tile] is None else sums[m][tile] + piece
    spare = 2 * LANES - depth
    for m in range(3):
        for n in range(2):
            at = (3 * n + m) * 2 * LANES
            if spare:
                terms_ref[at + depth : at + 2 * LANES, :] = jnp.zeros((spare, width), BF)
        for i in range(tiles):
            high = sums[m][i].astype(BF)
            high_ref[m, :, i * LANES : (i + 1) * LANES] = high
            for n, part in enumerate((high, (sums[m][i] - high.astype(F32)).astype(BF))):
                at = (3 * n + m) * 2 * LANES
                terms_ref[at : at + depth, i * LANES : (i + 1) * LANES] = part
    correlate(t_ref, terms_ref, result, entries)
    place = lax.axis_index("en")
    below = jnp.where(place == 0, 0.0, 1.0)
    above = jnp.where(place == lax.axis_size("en") - 1, 0.0, 1.0)
    for i, c in enumerate((core, 1 - core)):
        low_ref[i] = (result[c] * below).astype(BF)
        up_ref[i] = (result[2 + c] * above).astype(BF)
        own_ref[i] = result[4 + c]


def correlate(t_ref, terms_ref, result, entries):
    count, rows, width = result.shape
    lane = index((1, LANES), 1)
    carried = None
    for p in range(width // entries):
        begin = entries * p
        first = begin // LANES
        last = (begin + entries - 1) // LANES
        t = t_ref[p]
        total = dot(jnp.concatenate([t, t], axis=1), terms_ref[:, first * LANES : (last + 1) * LANES])
        for i in range(first, last + 1):
            tile = total[:, (i - first) * LANES : (i - first + 1) * LANES]
            if i == first and begin % LANES:
                tile = jnp.where(lane < begin % LANES, carried, tile)
            if i == last and (begin + entries) % LANES:
                carried = tile
            else:
                for r in range(count):
                    result[r, :, i * LANES : (i + 1) * LANES] = tile[r * rows : (r + 1) * rows]


def polar_kernel(b_own, both_core, prev_own, prev_far, turn_ref, sort_ref, high_ref, out_ref, gathered, *, half, entries, momenta, local_k, local_e, scale):
    core = my_core()
    present = jnp.where(lax.axis_index("en") == 0, 0.0, 1.0)
    gathered[core] = (prev_own[...].astype(F32) * present).astype(BF)
    gathered[1 - core] = (prev_far[...].astype(F32) * present).astype(BF)
    gathered[2 + core] = b_own[...]
    gathered[3 - core] = both_core[1]
    count, rows, width = gathered.shape
    tiles = width // LANES
    b = dot(sort_ref[...], gathered[...].reshape(count * rows, width)).astype(BF)
    sums = [None] * tiles
    for j in range(2 * half):
        start = (entries // 2) * j // LANES * LANES
        r = dot(b[:, start : start + 2 * LANES], turn_ref[j])
        for i in range(2):
            tile = start // LANES + i
            piece = r[:, i * LANES : (i + 1) * LANES]
            sums[tile] = piece if sums[tile] is None else sums[tile] + piece
    chip_k = 2 * local_k
    group = 2 * local_e
    columns = sort_ref.shape[0]
    window = local_e
    lane = index((1, LANES), 1)
    pieces = []
    for p in range(half):
        begin = entries * p
        first = begin // LANES
        last = (begin + entries - 1) // LANES
        parts = []
        for i in range(first, last + 1):
            tile = sums[i]
            if i == first and begin % LANES:
                tile = jnp.where(lane < begin % LANES, 0.0, tile)
            if i == last and (begin + entries) % LANES:
                tile = jnp.where(lane < (begin + entries) % LANES, tile, 0.0)
            parts.append(tile.astype(BF))
        rhs = jnp.concatenate(parts, axis=1)
        held = None
        sources = high_ref[:, :, first * LANES : (last + 1) * LANES]
        products = dot_t(sources.reshape(-1, sources.shape[2]), rhs)
        for m in range(3):
            s = products[m * momenta * local_e : (m + 1) * momenta * local_e]
            acc = None
            for e in range(local_e):
                row = pltpu.roll(s[e * momenta : (e + 1) * momenta], columns - (local_e - e), 1)
                acc = row if acc is None else acc + row
            total = None
            for a in range(chip_k):
                piece = acc if a == 0 else pltpu.roll(acc, columns - group * a, 1)
                piece = piece[:, :LANES]
                if a:
                    piece = pltpu.roll(piece, momenta - a, 0)
                total = piece if total is None else total + piece
            total = jnp.where(lane < window, total * scale, 0.0)
            if m:
                total = pltpu.roll(total, m * (LANES // 4), 1)
            held = total if held is None else held + total
        pieces.append(held)
    targets, en = out_ref.shape[:2]
    for t in range(targets):
        tile = jnp.concatenate(
            [pieces[p][t * local_k + i : t * local_k + i + 1] for i in range(local_k) for p in range(half)], axis=0
        )
        for e in range(en):
            out_ref[t, e] = tile


def total_kernel(in_ref, after_ref, out_ref, *, half):
    targets, en = in_ref.shape[:2]
    local_k, _, _, window = out_ref.shape
    sums = []
    for c in range(2):
        total = None
        for t in range(c, targets, 2):
            for e in range(en):
                total = in_ref[t, e] if total is None else total + in_ref[t, e]
        sums.append(total)
    for i in range(local_k):
        tile = jnp.concatenate([sums[c][i * half : (i + 1) * half] for c in range(2)], axis=0)
        for m in range(3):
            moved = pltpu.roll(tile, LANES - m * (LANES // 4), 1) if m else tile
            out_ref[i, m] = moved[:, :window]


def sum_kernel(own, below, above, mine, theirs):
    for n, out in enumerate((mine, theirs)):
        out[...] = (own[n] + below[n].astype(F32) + above[n].astype(F32)).astype(BF)


def join_kernel(mine, other, perm_ref, out_ref, mark_ref, halves):
    core = my_core()
    pairs = out_ref.shape[2]
    entries = out_ref.shape[3]
    half = pairs // 2
    halves[core] = mine[...].astype(F32)
    halves[1 - core] = other[...].astype(F32)
    parts = []
    for p in range(pairs):
        begin = entries * (p % half)
        parts.append(halves[p // half][:, begin : begin + entries])
    stacked = jnp.concatenate(parts, axis=0).astype(BF)
    mark_ref[...] = jnp.zeros(mark_ref.shape, F32)
    out_ref[...] = dot(perm_ref[...], stacked).astype(BF).reshape(out_ref.shape)


def body(green_less, green_greater, derivative, neighbours, phonon, *, mom, en):
    local_k, local_e, pairs, entries = green_less.shape
    momenta, window = phonon.shape[1], phonon.shape[2]
    atoms = derivative.shape[0]
    half = pairs // 2
    rows = local_k * local_e
    width = half * entries
    chips = mom // 2
    chip_k = 2 * local_k
    total_e = local_e * en
    size = NO * NO

    deriv = derivative.transpose(1, 0, 2)
    weights = phonon.transpose(0, 1, 3, 4, 2)
    g_own, g_far, b_own, b_far, both_far = call(
        pack_kernel,
        [shape((rows, width), BF)] * 4 + [shape((2, rows, width), BF)],
        [green_less, green_greater],
        1.5,
        [
            pltpu.VMEM(green_less.shape, BF),
            pltpu.VMEM(green_less.shape, BF),
            pltpu.VMEM((2, rows, width), F32),
            pltpu.SemaphoreType.DMA((2,)),
        ],
        [HBM] * 2,
        limit=53.12,
    )

    def move(value, dchip, dcore, to=lambda e: e):
        links = []
        for m in range(mom):
            target = ((m // 2 + dchip) % chips) * 2 + (m % 2 if dcore == 0 else 1 - m % 2)
            for e in range(en):
                links.append((m * en + e, target * en + to(e)))
        return lax.ppermute(value, ("mom", "en"), links)

    def onward(e):
        return (e + 1) % en

    def back(e):
        return (e - 1) % en

    blocks = []
    for s in range(1, chips):
        blocks += [move(g_far, -s, 1), move(g_own, -s, 0)][::-1]
    both_core = move(both_far, 0, 1)
    blocks += [g_own, both_core]
    prev_far = move(b_far, 0, 1, onward)
    prev_own = move(b_own, 0, 0, onward)

    near = neighbours.astype(jnp.int32)
    columns = -(-chip_k * 2 * local_e // LANES) * LANES
    k_hi, k_lo, toeplitz, to_energy, to_rows, turn, sort_e = call(
        functools.partial(table_kernel, half=half, local_k=local_k, local_e=local_e),
        [
            shape((6 * half, size, 2 * LANES), BF),
            shape((6 * half, size, 2 * LANES), BF),
            shape((half, 3 * chip_k * local_e, 6 * LANES), BF),
            shape((momenta * local_e,) * 2, BF),
            shape((rows * pairs,) * 2, BF),
            shape((2 * half, 2 * LANES, 2 * LANES), BF),
            shape((columns, 2 * chip_k * local_e), BF),
        ],
        [near, deriv, weights],
        3,
        [
            pltpu.VMEM((3 * atoms, 32, 4 * LANES), F32),
            pltpu.VMEM((chip_k, 3, pairs, 4 * local_e * momenta), F32),
        ],
        [pl.BlockSpec(memory_space=pltpu.SMEM), VMEM, VMEM],
    )

    high, own, low, up = call(
        functools.partial(product_kernel, half=half, entries=entries, chips=chips),
        [
            shape((3, momenta * local_e, width), BF),
            shape((2, rows, width), F32),
            shape((2, rows, width), BF),
            shape((2, rows, width), BF),
        ],
        blocks + [to_energy, k_hi, k_lo, toeplitz],
        4,
        [
            pltpu.VMEM((2 * chips, rows, width), BF),
            pltpu.VMEM((12 * LANES, width), BF),
            pltpu.VMEM((6, rows, width), F32),
        ],
    )
    from_below = move(up, 0, 0, onward)
    from_above = move(low, 0, 0, back)
    (partial,) = call(
        functools.partial(
            polar_kernel, half=half, entries=entries, momenta=momenta, local_k=local_k, local_e=local_e,
            scale=1.0 / (NO * float(np.sqrt(momenta * total_e))),
        ),
        [shape((mom, en, local_k * half, LANES), F32)],
        [b_own, both_core, prev_own, prev_far, turn, sort_e, high],
        3,
        [pltpu.VMEM((4, rows, width), BF)],
    )
    terms = lax.all_to_all(
        partial.reshape(mom * en, local_k * half, LANES), ("mom", "en"), split_axis=0, concat_axis=0, tiled=True
    )
    mine, theirs = call(
        sum_kernel, [shape((rows, width), BF)] * 2, [own, from_below, from_above], 0.1
    )
    other = move(theirs, 0, 1)
    self_energy, mark = call(
        join_kernel,
        [shape(green_less.shape, BF), shape((8, LANES), F32)],
        [mine, other, to_rows],
        1,
        [pltpu.VMEM((2, rows, width), F32)],
    )
    (polar,) = call(
        functools.partial(total_kernel, half=half),
        [shape((local_k, 3, pairs, window), F32)],
        [terms.reshape(mom, en, local_k * half, LANES), mark],
        0.5,
    )
    polar = polar.transpose(0, 3, 1, 2)
    return (self_energy, polar)


def solution(mesh):
    return jax.shard_map(
        functools.partial(body, mom=mesh.shape["mom"], en=mesh.shape["en"]),
        mesh=mesh,
        in_specs=(P("mom", "en", None, None), P("mom", "en", None, None), P(), P(), P()),
        out_specs=(P("mom", "en", None, None), P("mom", None, None, None)),
        check_vma=False,
    )
```

```python
import functools

import jax
import jax.numpy as jnp
import numpy as np
from jax import lax
from jax.experimental import pallas as pl
from jax.experimental.pallas import tpu as pltpu
from jax.sharding import PartitionSpec as P

NO = 12
NB = 4
LANES = 128
BF = jnp.bfloat16
F32 = jnp.float32
HIGHEST = lax.Precision.HIGHEST
VMEM = pl.BlockSpec(memory_space=pltpu.VMEM)
HBM = pl.BlockSpec(memory_space=pltpu.HBM)
MIB = 1024 * 1024


def dot(a, b):
    return jnp.dot(a, b, preferred_element_type=F32)


def dot_t(a, b):
    return lax.dot_general(a, b, (((1,), (1,)), ((), ())), preferred_element_type=F32)


def call(kernel, outs, ins, work, scratch=(), specs=None, limit=24):
    return pl.pallas_call(
        kernel,
        out_shape=outs,
        in_specs=specs or [VMEM] * len(ins),
        out_specs=[VMEM] * len(outs),
        scratch_shapes=list(scratch),
        compiler_params=pltpu.CompilerParams(vmem_limit_bytes=int(limit * MIB)),
        cost_estimate=pl.CostEstimate(flops=int(work * 1e9), bytes_accessed=0, transcendentals=0),
    )(*ins)


def my_core():
    return lax.rem(lax.axis_index("mom"), 2).astype(jnp.int32)


def index(dims, axis):
    return lax.broadcasted_iota(jnp.int32, dims, axis)


def split(value, count):
    whole = jnp.floor((value.astype(F32) + 0.5) * (1.0 / count)).astype(jnp.int32)
    return whole, value - count * whole


def ones_at(condition):
    return condition.astype(F32).astype(BF)


def shape(dims, dtype):
    return jax.ShapeDtypeStruct(dims, dtype)


def pack_kernel(g_hbm, b_hbm, g_own, g_far, b_own, b_far, both_far, g_ref, b_ref, halves, sems):
    core = my_core()
    copies = []
    for i, (src, dst) in enumerate(((g_hbm, g_ref), (b_hbm, b_ref))):
        copies.append(pltpu.make_async_copy(src, dst, sems.at[i]))
        copies[-1].start()
    rows = g_own.shape[0]
    pairs = g_ref.shape[2]
    entries = g_ref.shape[3]
    half = pairs // 2
    dims = (rows, rows * pairs)
    gap = index(dims, 1) - pairs * index(dims, 0)
    perm = jnp.concatenate([ones_at(gap == p) for p in range(pairs)], axis=0)
    for copy, src, own, far in ((copies[0], g_ref, g_own, g_far), (copies[1], b_ref, b_own, b_far)):
        copy.wait()
        sorted_rows = dot(perm, src[...].reshape(rows * pairs, entries))
        for h in range(2):
            parts = [sorted_rows[(h * half + j) * rows : (h * half + j + 1) * rows] for j in range(half)]
            halves[h] = jnp.concatenate(parts, axis=1)
        own[...] = halves[core].astype(BF)
        far[...] = halves[1 - core].astype(BF)
    both_far[0] = g_far[...]
    both_far[1] = b_far[...]


def table_kernel(
    near_ref, deriv_ref, phonon_ref, hi_ref, lo_ref, t_ref, perm_ref, join_ref, turn_ref, sort_ref,
    factors, bases, *, half, local_k, local_e,
):
    core = my_core()
    _, momenta, _, pairs, window = phonon_ref.shape
    size = NO * NO
    chip_k = 2 * local_k
    dims = perm_ref.shape
    e, k = split(index(dims, 0), momenta)
    perm_ref[...] = ones_at(index(dims, 1) == k * local_e + e)
    dims = join_ref.shape
    row, p = split(index(dims, 0), pairs)
    join_ref[...] = ones_at(index(dims, 1) == p * (local_k * local_e) + row)
    dims = sort_ref.shape
    k, i = split(index(dims, 0), 2 * local_e)
    at = jnp.where(i < local_e, (chip_k + k) * local_e + local_e - 1 - i, k * local_e + 2 * local_e - 1 - i)
    sort_ref[...] = ones_at((index(dims, 1) == at) & (k < chip_k))
    dims = turn_ref.shape[1:]
    u, i = split(index(dims, 0), NO)
    turn = ((index(dims, 1) == i * NO + u) & (u < NO)).astype(F32)
    for j in range(2 * half):
        shift = size * j % LANES
        moved = pltpu.roll(pltpu.roll(turn, shift, 0), shift, 1) if shift else turn
        turn_ref[j] = (moved * (1.0 - 2.0 * (j % 2))).astype(BF)
    x = (size, 2 * LANES)
    outer, inner = split(index(x, 0), NO)
    lane_outer, lane_inner = split(index(x, 1), NO)
    pick_l = ones_at(outer == lane_outer)
    pick_r = ones_at((outer == lane_inner) & (lane_outer < NO))
    picks = jnp.concatenate([pick_l, pick_r], axis=1)
    x = (size, 32)
    outer, inner = split(index(x, 0), NO)
    slot = split(index(x, 1), 16)[1]
    rows_l = ones_at(outer == slot)
    rows_r = ones_at(inner == slot)
    x = (16, size)
    mask = (split(index(x, 1), NO)[1] == index(x, 0)).astype(F32)
    atoms = deriv_ref.shape[1]
    spread = []
    for m in range(3):
        for atom in range(atoms):
            spread.append(deriv_ref[m, atom : atom + 1, :] * mask)
    spread = jnp.concatenate(spread, axis=0)
    spread_hi = spread.astype(BF)
    spread_lo = (spread - spread_hi.astype(F32)).astype(BF)
    for i, part in enumerate((spread_hi, spread_lo)):
        rows = dot(part, picks)
        for n in range(3 * atoms):
            factors[n, 16 * i : 16 * i + 16] = rows[16 * n : 16 * n + 16]
    for p in range(half):
        pair = core * half + p
        atom = pair // NB
        other = near_ref[atom, pair % NB]
        for m in range(3):
            u = factors[m * atoms + atom][:, : 2 * LANES]
            v = factors[m * atoms + other][:, 2 * LANES :]
            for c in range(2):
                j = 2 * p + c
                shift = size * j % LANES
                uj = pltpu.roll(u, shift, 1) if shift else u
                vj = pltpu.roll(v, shift, 1) if shift else v
                kron = dot(rows_l, uj.astype(BF)) * dot(rows_r, vj.astype(BF))
                k_hi = kron.astype(BF)
                hi_ref[j * 3 + m] = k_hi
                lo_ref[j * 3 + m] = (kron - k_hi.astype(F32)).astype(BF)
    tiles = 3 * local_e // 8
    step = 8 * momenta
    first = momenta * (3 * local_e - 8)
    length = bases.shape[3]
    middle = 2 * local_e - 8
    dims = (window, length)
    lane = index(dims, 1)
    depth = index(dims, 0) + 1
    line = None
    for side in range(2):
        gap = lane - momenta * (middle + depth if side else middle - depth)
        for q in range(momenta):
            place = ones_at(gap == (-q) % momenta)
            weights = phonon_ref[side, q].astype(F32).reshape(3 * pairs, window).astype(BF)
            term = dot(weights, place)
            line = term if line is None else line + term
    lane = index((1, length), 1)
    k = split(lane, momenta)[1]
    for a in range(chip_k):
        moved = line
        if a:
            moved = jnp.where(k >= a, pltpu.roll(line, a, 1), pltpu.roll(line, length - momenta + a, 1))
        bases[a] = moved.reshape(3, pairs, length)
    for p in range(half):
        for m in range(3):
            grid = {}
            for a in range(chip_k):
                row = bases[a, m, pl.ds(core * half + p, 1), :]
                block = pltpu.roll(jnp.broadcast_to(row, (8, length)), 0, 1, stride=momenta, stride_axis=0)
                moved = {0: block}
                for t in range(tiles):
                    offset = first - step * t
                    part = offset % LANES
                    if part not in moved:
                        moved[part] = pltpu.roll(block, length - part, 1)
                    start = offset - part
                    grid[(t, a)] = moved[part][:, start : start + 2 * LANES]
            order = []
            per = local_e // 8
            for blk in (0, 2, 1):
                for a in range(chip_k):
                    order += [grid[(blk * per + i, a)] for i in range(per)]
            table = jnp.where(index((1, 2 * LANES), 1) < momenta * local_e, jnp.concatenate(order, axis=0), 0.0)
            t_ref[p, :, m * 2 * LANES : (m + 1) * 2 * LANES] = table.astype(BF)


def product_kernel(*refs, half, entries, chips):
    core = my_core()
    blocks = refs[: 2 * chips]
    perm_ref, hi_ref, lo_ref, t_ref = refs[2 * chips : 2 * chips + 4]
    high_ref, own_ref, far_ref, pair_ref, gathered, terms_ref, result = refs[2 * chips + 4 :]
    for s in range(chips):
        n = 2 * ((s - 1) % chips)
        gathered[2 * s + core] = blocks[n][...]
        gathered[2 * s + 1 - core] = blocks[n + 1][...] if s else blocks[n + 1][0]
    count, rows, width = gathered.shape
    depth = count * rows
    tiles = width // LANES
    g = dot(perm_ref[...], gathered[...].reshape(depth, width)).astype(BF)
    block_rows = hi_ref.shape[1]
    sums = [[None] * tiles for _ in range(3)]
    for j in range(2 * half):
        start = (entries // 2) * j // LANES * LANES
        shift = (entries // 2) * j - start
        lhs = g[:, start : start + 2 * LANES]
        lhs = jnp.concatenate([lhs, lhs], axis=1)
        above = [jnp.zeros((shift, 2 * LANES), BF)] if shift else []
        rest = 2 * LANES - shift - block_rows
        under = [jnp.zeros((rest, 2 * LANES), BF)] if rest else []
        for m in range(3):
            parts = above + [hi_ref[j * 3 + m]] + under + above + [lo_ref[j * 3 + m]] + under
            r = dot(lhs, jnp.concatenate(parts, axis=0))
            for i in range(2):
                tile = start // LANES + i
                piece = r[:, i * LANES : (i + 1) * LANES]
                sums[m][tile] = piece if sums[m][tile] is None else sums[m][tile] + piece
    spare = 2 * LANES - depth
    for m in range(3):
        for n in range(2):
            at = (3 * n + m) * 2 * LANES
            if spare:
                terms_ref[at + depth : at + 2 * LANES, :] = jnp.zeros((spare, width), BF)
        for i in range(tiles):
            high = sums[m][i].astype(BF)
            high_ref[m, :, i * LANES : (i + 1) * LANES] = high
            for n, part in enumerate((high, (sums[m][i] - high.astype(F32)).astype(BF))):
                at = (3 * n + m) * 2 * LANES
                terms_ref[at : at + depth, i * LANES : (i + 1) * LANES] = part
    correlate(t_ref, terms_ref, result, entries)
    place = lax.axis_index("en")
    below = jnp.where(place == 0, 0.0, 1.0)
    above = jnp.where(place == lax.axis_size("en") - 1, 0.0, 1.0)
    odd = lax.rem(place, 2)
    keep_pair = jnp.where(odd == 1, below, above)
    keep_far = jnp.where(odd == 1, above, below)
    for i, c in enumerate((core, 1 - core)):
        pair_ref[i] = (result[2 - 2 * odd + c] * keep_pair).astype(BF)
        far_ref[i] = (result[2 * odd + c] * keep_far).astype(BF)
        own_ref[i] = result[4 + c]


def correlate(t_ref, terms_ref, result, entries):
    count, rows, width = result.shape
    lane = index((1, LANES), 1)
    carried = None
    for p in range(width // entries):
        begin = entries * p
        first = begin // LANES
        last = (begin + entries - 1) // LANES
        t = t_ref[p]
        total = dot(jnp.concatenate([t, t], axis=1), terms_ref[:, first * LANES : (last + 1) * LANES])
        for i in range(first, last + 1):
            tile = total[:, (i - first) * LANES : (i - first + 1) * LANES]
            if i == first and begin % LANES:
                tile = jnp.where(lane < begin % LANES, carried, tile)
            if i == last and (begin + entries) % LANES:
                carried = tile
            else:
                for r in range(count):
                    result[r, :, i * LANES : (i + 1) * LANES] = tile[r * rows : (r + 1) * rows]


def polar_kernel(b_own, both_core, prev_own, prev_far, turn_ref, sort_ref, high_ref, out_ref, gathered, *, half, entries, momenta, local_k, local_e, scale):
    core = my_core()
    present = jnp.where(lax.axis_index("en") == 0, 0.0, 1.0)
    gathered[core] = (prev_own[...].astype(F32) * present).astype(BF)
    gathered[1 - core] = (prev_far[...].astype(F32) * present).astype(BF)
    gathered[2 + core] = b_own[...]
    gathered[3 - core] = both_core[1]
    count, rows, width = gathered.shape
    tiles = width // LANES
    b = dot(sort_ref[...], gathered[...].reshape(count * rows, width)).astype(BF)
    sums = [None] * tiles
    for j in range(2 * half):
        start = (entries // 2) * j // LANES * LANES
        r = dot(b[:, start : start + 2 * LANES], turn_ref[j])
        for i in range(2):
            tile = start // LANES + i
            piece = r[:, i * LANES : (i + 1) * LANES]
            sums[tile] = piece if sums[tile] is None else sums[tile] + piece
    chip_k = 2 * local_k
    group = 2 * local_e
    columns = sort_ref.shape[0]
    window = local_e
    lane = index((1, LANES), 1)
    pieces = []
    for p in range(half):
        begin = entries * p
        first = begin // LANES
        last = (begin + entries - 1) // LANES
        parts = []
        for i in range(first, last + 1):
            tile = sums[i]
            if i == first and begin % LANES:
                tile = jnp.where(lane < begin % LANES, 0.0, tile)
            if i == last and (begin + entries) % LANES:
                tile = jnp.where(lane < (begin + entries) % LANES, tile, 0.0)
            parts.append(tile.astype(BF))
        rhs = jnp.concatenate(parts, axis=1)
        held = None
        sources = high_ref[:, :, first * LANES : (last + 1) * LANES]
        products = dot_t(sources.reshape(-1, sources.shape[2]), rhs)
        for m in range(3):
            s = products[m * momenta * local_e : (m + 1) * momenta * local_e]
            acc = None
            for e in range(local_e):
                row = pltpu.roll(s[e * momenta : (e + 1) * momenta], columns - (local_e - e), 1)
                acc = row if acc is None else acc + row
            total = None
            for a in range(chip_k):
                piece = acc if a == 0 else pltpu.roll(acc, columns - group * a, 1)
                piece = piece[:, :LANES]
                if a:
                    piece = pltpu.roll(piece, momenta - a, 0)
                total = piece if total is None else total + piece
            total = jnp.where(lane < window, total * scale, 0.0)
            if m:
                total = pltpu.roll(total, m * (LANES // 4), 1)
            held = total if held is None else held + total
        pieces.append(held)
    targets, en = out_ref.shape[:2]
    for t in range(targets):
        tile = jnp.concatenate(
            [pieces[p][t * local_k + i : t * local_k + i + 1] for i in range(local_k) for p in range(half)], axis=0
        )
        for e in range(en):
            out_ref[t, e] = tile


def total_kernel(in_ref, after_ref, out_ref, *, half):
    targets, en = in_ref.shape[:2]
    local_k, _, _, window = out_ref.shape
    sums = []
    for c in range(2):
        total = None
        for t in range(c, targets, 2):
            for e in range(en):
                total = in_ref[t, e] if total is None else total + in_ref[t, e]
        sums.append(total)
    for i in range(local_k):
        tile = jnp.concatenate([sums[c][i * half : (i + 1) * half] for c in range(2)], axis=0)
        for m in range(3):
            moved = pltpu.roll(tile, LANES - m * (LANES // 4), 1) if m else tile
            out_ref[i, m] = moved[:, :window]


def sum_kernel(own, far, pair, mine, theirs):
    for n, out in enumerate((mine, theirs)):
        out[...] = (own[n] + far[n].astype(F32) + pair[n].astype(F32)).astype(BF)


def join_kernel(mine, other, perm_ref, out_ref, mark_ref, halves):
    core = my_core()
    pairs = out_ref.shape[2]
    entries = out_ref.shape[3]
    half = pairs // 2
    halves[core] = mine[...].astype(F32)
    halves[1 - core] = other[...].astype(F32)
    parts = []
    for p in range(pairs):
        begin = entries * (p % half)
        parts.append(halves[p // half][:, begin : begin + entries])
    stacked = jnp.concatenate(parts, axis=0).astype(BF)
    mark_ref[...] = jnp.zeros(mark_ref.shape, F32)
    out_ref[...] = dot(perm_ref[...], stacked).astype(BF).reshape(out_ref.shape)


def body(green_less, green_greater, derivative, neighbours, phonon, *, mom, en):
    local_k, local_e, pairs, entries = green_less.shape
    momenta, window = phonon.shape[1], phonon.shape[2]
    atoms = derivative.shape[0]
    half = pairs // 2
    rows = local_k * local_e
    width = half * entries
    chips = mom // 2
    chip_k = 2 * local_k
    total_e = local_e * en
    size = NO * NO

    deriv = derivative.transpose(1, 0, 2)
    weights = phonon.transpose(0, 1, 3, 4, 2)
    g_own, g_far, b_own, b_far, both_far = call(
        pack_kernel,
        [shape((rows, width), BF)] * 4 + [shape((2, rows, width), BF)],
        [green_less, green_greater],
        1.5,
        [
            pltpu.VMEM(green_less.shape, BF),
            pltpu.VMEM(green_less.shape, BF),
            pltpu.VMEM((2, rows, width), F32),
            pltpu.SemaphoreType.DMA((2,)),
        ],
        [HBM] * 2,
        limit=53.12,
    )

    def move(value, dchip, dcore, to=lambda e: e, cross=False):
        links = []
        for m in range(mom):
            for e in range(en):
                other = (m + dcore + (cross and e == 0)) % 2
                target = ((m // 2 + dchip) % chips) * 2 + other
                links.append((m * en + e, target * en + to(e)))
        return lax.ppermute(value, ("mom", "en"), links)

    def onward(e):
        return (e + 1) % en

    def to_pair(e):
        return e ^ 1 if e ^ 1 < en else e

    def to_far(e):
        other = e + 1 if e % 2 else e - 1
        return other % en if en % 2 == 0 else max(other, 0)

    blocks = []
    for s in range(1, chips):
        blocks += [move(g_far, -s, 1), move(g_own, -s, 0)][::-1]
    both_core = move(both_far, 0, 1)
    blocks += [g_own, both_core]
    prev_far = move(b_far, 0, 1, onward)
    prev_own = move(b_own, 0, 0, onward)

    near = neighbours.astype(jnp.int32)
    columns = -(-chip_k * 2 * local_e // LANES) * LANES
    k_hi, k_lo, toeplitz, to_energy, to_rows, turn, sort_e = call(
        functools.partial(table_kernel, half=half, local_k=local_k, local_e=local_e),
        [
            shape((6 * half, size, 2 * LANES), BF),
            shape((6 * half, size, 2 * LANES), BF),
            shape((half, 3 * chip_k * local_e, 6 * LANES), BF),
            shape((momenta * local_e,) * 2, BF),
            shape((rows * pairs,) * 2, BF),
            shape((2 * half, 2 * LANES, 2 * LANES), BF),
            shape((columns, 2 * chip_k * local_e), BF),
        ],
        [near, deriv, weights],
        3,
        [
            pltpu.VMEM((3 * atoms, 32, 4 * LANES), F32),
            pltpu.VMEM((chip_k, 3, pairs, 4 * local_e * momenta), F32),
        ],
        [pl.BlockSpec(memory_space=pltpu.SMEM), VMEM, VMEM],
    )

    high, own, far, pair = call(
        functools.partial(product_kernel, half=half, entries=entries, chips=chips),
        [
            shape((3, momenta * local_e, width), BF),
            shape((2, rows, width), F32),
            shape((2, rows, width), BF),
            shape((2, rows, width), BF),
        ],
        blocks + [to_energy, k_hi, k_lo, toeplitz],
        4,
        [
            pltpu.VMEM((2 * chips, rows, width), BF),
            pltpu.VMEM((12 * LANES, width), BF),
            pltpu.VMEM((6, rows, width), F32),
        ],
    )
    from_far = move(far, 0, 0, to_far, True)
    from_pair = move(pair, 0, 0, to_pair)
    (partial,) = call(
        functools.partial(
            polar_kernel, half=half, entries=entries, momenta=momenta, local_k=local_k, local_e=local_e,
            scale=1.0 / (NO * float(np.sqrt(momenta * total_e))),
        ),
        [shape((mom, en, local_k * half, LANES), F32)],
        [b_own, both_core, prev_own, prev_far, turn, sort_e, high],
        3,
        [pltpu.VMEM((4, rows, width), BF)],
    )
    terms = lax.all_to_all(
        partial.reshape(mom * en, local_k * half, LANES), ("mom", "en"), split_axis=0, concat_axis=0, tiled=True
    )
    mine, theirs = call(
        sum_kernel, [shape((rows, width), BF)] * 2, [own, from_far, from_pair], 0.1
    )
    other = move(theirs, 0, 1)
    self_energy, mark = call(
        join_kernel,
        [shape(green_less.shape, BF), shape((8, LANES), F32)],
        [mine, other, to_rows],
        1,
        [pltpu.VMEM((2, rows, width), F32)],
    )
    (polar,) = call(
        functools.partial(total_kernel, half=half),
        [shape((local_k, 3, pairs, window), F32)],
        [terms.reshape(mom, en, local_k * half, LANES), mark],
        0.5,
    )
    polar = polar.transpose(0, 3, 1, 2)
    return (self_energy, polar)


def solution(mesh):
    return jax.shard_map(
        functools.partial(body, mom=mesh.shape["mom"], en=mesh.shape["en"]),
        mesh=mesh,
        in_specs=(P("mom", "en", None, None), P("mom", "en", None, None), P(), P(), P()),
        out_specs=(P("mom", "en", None, None), P("mom", None, None, None)),
        check_vma=False,
    )
```
